32 devices in a mesh: dp: 8 (over y, x, core), fsdp: 4 (over z).
Axes of the slice: x: 2, y: 2, z: 4, core: 2. Of those that a mesh axis runs over, the one named last changes fastest.
Arguments:
- tokens: bfloat16 [32768, 768], P(('dp', 'fsdp')), may hold values from -6 to 6
- segment_ids: int32 [32, 1024], P(('dp', 'fsdp')), may hold values from 0 to 5, never falling along the last dimension, each value on 1 to 512 neighbouring positions
- cotangent: bfloat16 [32768, 768], P(('dp', 'fsdp')), may hold values from -6 to 6
- projector: bfloat16 [768, 2304], P(('dp', 'fsdp')), may hold values from -0.21875 to 0.21875
- combiner: bfloat16 [768, 768], P(('dp', 'fsdp')), may hold values from -0.875 to 0.875
- attend_bias: bfloat16 [768], P(('dp', 'fsdp')), may hold values from -1.796875 to 1.796875
- expander: bfloat16 [768, 3072], P(('dp', 'fsdp')), may hold values from -0.21875 to 0.21875
- expand_bias: bfloat16 [3072], P(('dp', 'fsdp')), may hold values from -1.796875 to 1.796875
- reducer: bfloat16 [3072, 768], P(('dp', 'fsdp')), may hold values from -0.109375 to 0.109375
- reduce_bias: bfloat16 [768], P(('dp', 'fsdp')), may hold values from -1.796875 to 1.796875
- first_gain: bfloat16 [768], P(('dp', 'fsdp')), may hold values from 0.5 to 1.5
- first_shift: bfloat16 [768], P(('dp', 'fsdp')), may hold values from -1.796875 to 1.796875
- second_gain: bfloat16 [768], P(('dp', 'fsdp')), may hold values from 0.5 to 1.5
- second_shift: bfloat16 [768], P(('dp', 'fsdp')), may hold values from -1.796875 to 1.796875
Outputs:
- layer_output: bfloat16 [32768, 768], P(('dp', 'fsdp'))
- grad_tokens: float32 [32768, 768], P(('dp', 'fsdp'))
- grad_projector: float32 [768, 2304], P(('dp', 'fsdp'))
- grad_combiner: float32 [768, 768], P(('dp', 'fsdp'))
- grad_attend_bias: float32 [768], P(('dp', 'fsdp'))
- grad_expander: float32 [768, 3072], P(('dp', 'fsdp'))
- grad_expand_bias: float32 [3072], P(('dp', 'fsdp'))
- grad_reducer: float32 [3072, 768], P(('dp', 'fsdp'))
- grad_reduce_bias: float32 [768], P(('dp', 'fsdp'))
- grad_first_gain: float32 [768], P(('dp', 'fsdp'))
- grad_first_shift: float32 [768], P(('dp', 'fsdp'))
- grad_second_gain: float32 [768], P(('dp', 'fsdp'))
- grad_second_shift: float32 [768], P(('dp', 'fsdp'))
The draws below stay inside these ranges and needn't reach their ends.
Inputs may be any that keep to these rules, and one draw needn't show every extreme that they name: `segment_ids`: within each window the ids never fall; an id covers 1 to 512 consecutive positions, and some id exactly that many.
All inputs are finite; a program needn't handle non-finite values.
Results may differ from the reference program's by a relative error of at most 0.0092.
Values may be sent and summed in bfloat16 or wider, within the bound.
No kernel may reach another device: no remote copies, remote signals or barrier semaphores. Data moves between devices by JAX's collectives and lax.ppermute only.
A program may use at most 192 MiB of HBM per device.

```python
import math
import jax
import jax.numpy as jnp
import numpy as np
from jax import lax

D = 768
HEADS = 24
HD = 32
FF = 3072
WIN = 1024
WINDOWS = 32
TOKENS = 32768


def block_levels(own_key, dims, pieces, low, top_value):
    loudness = 1.0
    for axis_at, shards_of in pieces:
        steps = jax.random.uniform(jax.random.fold_in(jax.random.fold_in(own_key, 6), axis_at), (shards_of,), jnp.float32, low / len(pieces), top_value / len(pieces))
        loudness = loudness * jnp.repeat(jnp.exp(steps), dims[axis_at] // shards_of).reshape((-1,) + (1,) * (len(dims) - 1 - axis_at))
    return loudness


def length_profile(amount, total, most, skew):
    weights = [(1 << 20) // math.isqrt(grade ** skew) + 1 for grade in range(2, amount + 1)]
    surplus, given = total - most - (amount - 1), [1] * (amount - 1)
    while surplus > 0:
        free = [i for i in range(amount - 1) if given[i] < most]
        mass, left = sum([weights[i] for i in free]), surplus
        for i in free:
            extra = min(most - given[i], max(1, left * weights[i] // mass), surplus)
            given[i] = given[i] + extra
            surplus = surplus - extra
    return np.array([most] + given)


def ragged_sizes(rng, amount, total, most, skew):
    if amount == 2:
        one = jax.random.randint(rng, (), max(1, total - most), min(most, total - 1) + 1)
        return jnp.stack([one, total - one])
    lengths = jnp.asarray(length_profile(amount, total, most, skew), jnp.int32)
    couples = (amount - 1) // 2
    giver, sink = lengths[1:1 + 2 * couples:2], lengths[2:2 + 2 * couples:2]
    room = jnp.minimum(giver - 1, most - sink)
    shifted = jax.random.randint(jax.random.fold_in(rng, 1), (couples,), 0, 1 << 20) % (room + 1)
    lengths = lengths.at[1:1 + 2 * couples:2].set(giver - shifted).at[2:2 + 2 * couples:2].set(sink + shifted)
    return lengths[jax.random.permutation(jax.random.fold_in(rng, 2), amount)]


def normal_values(key, shape, scale, most, cuts=(), kind=jnp.bfloat16):
    factor_of = block_levels(key, shape, cuts, -0.22, 0.18) if cuts else 1.0
    values = jax.random.normal(key, shape, jnp.float32) * scale * factor_of
    return jnp.minimum(jnp.maximum(values, -most), most).astype(kind)


def setup_inputs(seed: int = 0) -> dict:
    keys = jax.random.split(jax.random.key(seed), 15)
    tokens = normal_values(keys[0], (TOKENS, D), 1.0, 6.0, ((0, 32),))
    segment_ids = jax.vmap(lambda own: jnp.searchsorted(jnp.cumsum(ragged_sizes(own, 6, WIN, WIN // 2, 2)), jnp.arange(WIN), side="right"))(jax.random.split(keys[1], WINDOWS)).reshape((WINDOWS, WIN)).astype(jnp.int32)
    cotangent = normal_values(keys[2], (TOKENS, D), 1.0, 6.0, ((0, 32),))
    projector = normal_values(keys[3], (D, 3 * D), D ** -0.5, 0.21875, ((0, 32),))
    combiner = normal_values(keys[4], (D, D), (D // 16) ** -0.5, 0.875, ((0, 32),))
    attend_bias = normal_values(keys[5], (D,), 0.3, 1.796875, ((0, 32),))
    expander = normal_values(keys[6], (D, FF), D ** -0.5, 0.21875, ((0, 32),))
    expand_bias = normal_values(keys[7], (FF,), 0.3, 1.796875, ((0, 32),))
    reducer = normal_values(keys[8], (FF, D), FF ** -0.5, 0.109375, ((0, 32),))
    reduce_bias = normal_values(keys[9], (D,), 0.3, 1.796875, ((0, 32),))
    first_gain = jnp.clip(1.0 + 0.1 * jax.random.normal(keys[10], (D,), jnp.float32), 0.5, 1.5).astype(jnp.bfloat16)
    first_shift = normal_values(keys[11], (D,), 0.3, 1.796875, ((0, 32),))
    second_gain = jnp.clip(1.0 + 0.1 * jax.random.normal(keys[12], (D,), jnp.float32), 0.5, 1.5).astype(jnp.bfloat16)
    second_shift = normal_values(keys[13], (D,), 0.3, 1.796875, ((0, 32),))
    return dict(tokens=tokens, segment_ids=segment_ids, cotangent=cotangent, projector=projector, combiner=combiner, attend_bias=attend_bias, expander=expander, expand_bias=expand_bias, reducer=reducer, reduce_bias=reduce_bias, first_gain=first_gain, first_shift=first_shift, second_gain=second_gain, second_shift=second_shift)


epsilon = 1e-05
highest = lax.Precision.HIGHEST

@jax.custom_vjp
def low(v):
    return lax.optimization_barrier(v.astype(jnp.bfloat16)).astype(jnp.float32)

@jax.custom_vjp
def low_back(v):
    return v

def low_keep(v):
    return (low(v), None)

def low_pass(kept, grad):
    return (grad,)

def back_keep(v):
    return (v, None)

def back_low(kept, grad):
    return (low(grad),)
low.defvjp(low_keep, low_pass)
low_back.defvjp(back_keep, back_low)

def layer_norm(values, gain_vec, shift_vec):
    average = lax.optimization_barrier(jnp.mean(values, axis=-1, keepdims=True))
    centred = values - average
    variance = lax.optimization_barrier(jnp.mean(centred * centred, axis=-1, keepdims=True))
    return centred * lax.rsqrt(variance + epsilon) * gain_vec + shift_vec

def window_layer(inputs, episode, params):
    projector, combiner, attend_bias, expander, expand_bias, reducer, reduce_bias, first_gain, first_shift, second_gain, second_shift = params
    groups = inputs.shape[0]
    normed_one = low(layer_norm(inputs, first_gain, first_shift))
    project = low_back(low(jnp.einsum('gtd,de->gte', normed_one, projector, precision=highest)))
    queries = project[:, :, :D].reshape(groups, WIN, HEADS, HD)
    key_rows = project[:, :, D:2 * D].reshape(groups, WIN, HEADS, HD)
    value_rows = project[:, :, 2 * D:].reshape(groups, WIN, HEADS, HD)
    scores = jnp.einsum('gqhe,gkhe->ghqk', queries, key_rows, precision=highest) * HD ** (-0.5)
    positions = jnp.arange(WIN)
    allowed = (episode[:, :, None] == episode[:, None, :]) & (positions[:, None] >= positions[None, :])
    scores = low_back(jnp.where(allowed[:, None], scores, -1000000000.0))
    maximum = lax.optimization_barrier(jnp.max(scores, axis=-1, keepdims=True))
    exponent = jnp.exp(scores - maximum)
    probability = exponent / lax.optimization_barrier(jnp.sum(exponent, axis=-1, keepdims=True))
    attended = jnp.einsum('ghqk,gkhe->gqhe', low(probability), value_rows, precision=highest)
    attended = low_back(low(attended.reshape(groups, WIN, D)))
    branch = low_back(jnp.einsum('gte,ed->gtd', attended, combiner, precision=highest) + attend_bias)
    middle = inputs + branch
    normed_two = low(layer_norm(middle, second_gain, second_shift))
    upper = low_back(jnp.einsum('gtd,df->gtf', normed_two, expander, precision=highest) + expand_bias)
    active = low(jax.nn.gelu(upper))
    lowered = low_back(jnp.einsum('gtf,fd->gtd', active, reducer, precision=highest) + reduce_bias)
    return middle + lowered

def whole_layer(values, params, episode_ids):
    group = 4 if WINDOWS % 4 == 0 else 1
    token_groups = values.reshape(WINDOWS // group, group, WIN, D)
    id_groups = episode_ids.reshape(WINDOWS // group, group, WIN)
    step_layer = jax.checkpoint(window_layer)

    def advance(running, member):
        return (running, step_layer(member[0], member[1], params))
    unused, outputs = lax.scan(advance, jnp.zeros((), jnp.float32), (token_groups, id_groups))
    return outputs.reshape(TOKENS, D)

def reference(tokens, segment_ids, cotangent, projector, combiner, attend_bias, expander, expand_bias, reducer, reduce_bias, first_gain, first_shift, second_gain, second_shift):
    params = tuple((weight.astype(jnp.float32) for weight in (projector, combiner, attend_bias, expander, expand_bias, reducer, reduce_bias, first_gain, first_shift, second_gain, second_shift)))
    start = tokens.astype(jnp.float32)

    def forward(values, weights):
        return whole_layer(values, weights, segment_ids)
    output, pullback = jax.vjp(forward, start, params)
    grad_input, grads = pullback(cotangent.astype(jnp.float32))
    return (output.astype(jnp.bfloat16), grad_input, grads[0], grads[1], grads[2], grads[3], grads[4], grads[5], grads[6], grads[7], grads[8], grads[9], grads[10])
```

```python
import functools
import math

import jax
import jax.numpy as jnp
from jax import lax
from jax.experimental import pallas as pl
from jax.experimental.pallas import tpu as pltpu
from jax.sharding import PartitionSpec as P

D = 768
HD = 32
HEADS = 24
WIN = 1024
BLOCK = 256
EPS = 1e-05
LOG2E = math.log2(math.e)
BIG = float(2**30)
VEC = 128
f32 = jnp.float32
bf16 = jnp.bfloat16
VMEM_LIMIT = 58 << 20
NN = (((1,), (0,)), ((), ()))
NT = (((1,), (1,)), ((), ()))
ANY = pl.BlockSpec(memory_space=pl.ANY)
SMEM = pl.BlockSpec(memory_space=pltpu.SMEM)
PARAMS = pltpu.CompilerParams(vmem_limit_bytes=VMEM_LIMIT)


def dot(a, b, dims=NN):
    return lax.dot_general(a, b, dims, preferred_element_type=f32)


def whole(shape):
    return pl.BlockSpec(shape, lambda *_: (0,) * len(shape))


def flip(value, bit, count):
    return lax.ppermute(value, "dp", [(i, i ^ bit) for i in range(count)])


def shift(value, step, count):
    return lax.ppermute(value, "fsdp", [(i, (i + step) % count) for i in range(count)])


def gather_z(shard, nf):
    parts = [shard] + [shift(shard, k, nf) for k in range(1, nf)]
    me = lax.axis_index("fsdp")
    slots = [lax.select_n(lax.rem(me - j + nf, nf), *parts) for j in range(nf)]
    return jnp.concatenate(slots, axis=0)


def gather_dp(block, order, nd):
    blocks = {0: block}
    for bit in order:
        for m in list(blocks):
            blocks[m ^ bit] = flip(blocks[m], bit, nd)
    return [blocks[m] for m in range(nd)]


def orders(nd):
    upper = [1 << i for i in range(1, nd.bit_length() - 1)]
    return upper, upper[::-1]


def add(a, b):
    return (a.astype(f32) + b.astype(f32)).astype(bf16)


def scatter_dp(send, keep, order, nd):
    got = flip(send, 1, nd)
    masks = list(range(nd // 2))
    total = add(keep, got)
    for bit in order:
        half = bit >> 1
        low = [i for i, m in enumerate(masks) if not m & half]
        high = [i for i, m in enumerate(masks) if m & half]
        out = jnp.stack([total[i] for i in high])
        stay = jnp.stack([total[i] for i in low])
        total = add(stay, flip(out, bit, nd))
        masks = [masks[i] for i in low]
    return total[0]


def scatter_z(block, rows, nf):
    me = lax.axis_index("fsdp")

    def piece(z):
        got, at = [], 0
        for r in rows:
            got.append(lax.dynamic_slice_in_dim(block, at + z * r, r, 0))
            at += nf * r
        return got[0] if len(got) == 1 else jnp.concatenate(got, axis=0)

    total = piece(me).astype(f32)
    for k in range(1, nf):
        total = total + shift(piece(lax.rem(me + k, nf)), k, nf).astype(f32)
    return total


def load_blocks(me, refs, target, sems, base):
    rows = refs[0].shape[0]
    copies = []
    for m, ref in enumerate(refs):
        at = pl.multiple_of((me ^ m) * rows, 16)
        copy = pltpu.make_async_copy(ref, target.at[pl.ds(at, rows), :], sems.at[base + m])
        copy.start()
        copies.append(copy)
    return copies


def norm_parts(v):
    c = v - jnp.mean(v, axis=-1, keepdims=True)
    rstd = lax.rsqrt(jnp.mean(c * c, axis=-1, keepdims=True) + EPS)
    return c * rstd, rstd


def norm_back(grad, gain, h, rstd):
    e = grad * gain
    return (e - jnp.mean(e, -1, keepdims=True) - h * jnp.mean(e * h, -1, keepdims=True)) * rstd


def project_kernel(nd, me_ref, x_ref, *rest):
    w1, w2 = rest[:nd], rest[nd : 2 * nd]
    pt_ref, nt_ref, vec_ref, s1, s2, sems = rest[2 * nd :]
    me = me_ref[0]
    first = load_blocks(me, w1, s1, sems, 0)
    second = load_blocks(me, w2, s2, sems, nd)
    x = x_ref[...].astype(f32)
    h, _ = norm_parts(x)
    for copy in first:
        copy.wait()
    vec = s1[:, 2 * D : 2 * D + VEC].astype(f32).T
    vec_ref[...] = vec[:16]
    normed = (h * vec[0:1] + vec[1:2]).astype(bf16)
    nt_ref[...] = normed.T
    for c in range(0, 2 * D, BLOCK):
        pt_ref[c : c + BLOCK, :] = dot(s1[:, c : c + BLOCK].T, nt_ref[...]).astype(bf16)
    for copy in second:
        copy.wait()
    for c in range(0, D, BLOCK):
        pt_ref[2 * D + c : 2 * D + c + BLOCK, :] = dot(
            s2[:, c : c + BLOCK].T, nt_ref[...]
        ).astype(bf16)


def project(me, tokens, w1, w2):
    nd = len(w1)
    return pl.pallas_call(
        functools.partial(project_kernel, nd),
        in_specs=[SMEM, whole((WIN, D))] + [ANY] * (2 * nd),
        out_specs=[whole((3 * D, WIN)), whole((D, WIN)), whole((16, D))],
        out_shape=[
            jax.ShapeDtypeStruct((3 * D, WIN), bf16),
            jax.ShapeDtypeStruct((D, WIN), bf16),
            jax.ShapeDtypeStruct((16, D), f32),
        ],
        scratch_shapes=[
            pltpu.VMEM((D, w1[0].shape[1]), bf16),
            pltpu.VMEM((D, w2[0].shape[1]), bf16),
            pltpu.SemaphoreType.DMA((2 * nd,)),
        ],
        grid=(1,),
        compiler_params=PARAMS,
        cost_estimate=pl.CostEstimate(flops=2 * WIN * D * 3 * D, bytes_accessed=12 << 20, transcendentals=0),
        name="project",
    )(me, tokens, *w1, *w2)


GH = 8
SH = 8
GR = GH * HD


def causal_penalty():
    ik = lax.broadcasted_iota(jnp.int32, (BLOCK, BLOCK), 0)
    iq = lax.broadcasted_iota(jnp.int32, (BLOCK, BLOCK), 1)
    return jnp.where(iq >= ik, 0.0, -BIG)


def split_scaled(q):
    scaled = q.astype(f32) * (HD**-0.5 * LOG2E)
    high = scaled.astype(bf16)
    return high, (scaled - high.astype(f32)).astype(bf16)


def episode_rows(seg):
    hot = lax.broadcasted_iota(jnp.int32, (8, WIN), 0) == seg
    return hot.astype(f32), jnp.where(hot, 0.0, -BIG)


def attend_kernel(q_ref, k_ref, v_ref, seg_ref, out_ref, lse_ref, qa, ka, va, cm):
    @pl.when(pl.program_id(0) == 0)
    def _():
        cm[...] = causal_penalty()

    hot, pen = episode_rows(seg_ref[...])
    pad = jnp.zeros((56, WIN), f32)
    tail_q = jnp.concatenate([hot, pad], axis=0).astype(bf16)
    tail_k = jnp.concatenate([pen, pad], axis=0).astype(bf16)
    ones = jnp.ones((16, WIN), bf16)
    for h in range(GH):
        rows = slice(h * HD, (h + 1) * HD)
        high, low = split_scaled(q_ref[rows, :])
        k = k_ref[rows, :]
        qa[h] = jnp.concatenate([high, low, tail_q], axis=0)
        ka[h] = jnp.concatenate([k, k, tail_k], axis=0).T
        va[h] = jnp.concatenate([v_ref[rows, :], ones], axis=0)
    c = cm[...]
    for qb in range(WIN // BLOCK):
        k0, k1 = max(0, qb - 2) * BLOCK, (qb + 1) * BLOCK
        qs = slice(qb * BLOCK, k1)
        for hb in range(0, GH, SH):
            heads = range(hb, hb + SH)
            s = [dot(ka[h, k0:k1, :], qa[h, :, qs]) for h in heads]
            w = k1 - k0 - BLOCK
            s = [jnp.concatenate([x[:w], x[w:] + c], axis=0) if w else x + c for x in s]
            top = [jnp.max(x, axis=0, keepdims=True) for x in s]
            p = [jnp.exp2(x - y) for x, y in zip(s, top)]
            o = [dot(va[h, :, k0:k1], y.astype(bf16)) for h, y in zip(heads, p)]
            for i, h in enumerate(heads):
                total = o[i][HD : HD + 1]
                out_ref[h * HD : (h + 1) * HD, qs] = (o[i][:HD] * (1.0 / total)).astype(bf16)
                lse_ref[h, :, qs] = top[i] + jnp.log2(total)


def head_rows(offset):
    return pl.BlockSpec((GR, WIN), lambda g: (g + offset, 0))


def attend(project_t, seg):
    groups = HEADS // GH
    return pl.pallas_call(
        attend_kernel,
        grid=(groups,),
        in_specs=[head_rows(0), head_rows(groups), head_rows(2 * groups), whole((1, WIN))],
        out_specs=[head_rows(0), pl.BlockSpec((GH, 1, WIN), lambda g: (g, 0, 0))],
        out_shape=[
            jax.ShapeDtypeStruct((D, WIN), bf16),
            jax.ShapeDtypeStruct((HEADS, 1, WIN), f32),
        ],
        scratch_shapes=[
            pltpu.VMEM((GH, 128, WIN), bf16),
            pltpu.VMEM((GH, WIN, 128), bf16),
            pltpu.VMEM((GH, HD + 16, WIN), bf16),
            pltpu.VMEM((BLOCK, BLOCK), f32),
        ],
        compiler_params=PARAMS,
        cost_estimate=pl.CostEstimate(flops=20_000_000_000, bytes_accessed=8 << 20, transcendentals=0),
        name="attend",
    )(project_t, project_t, project_t, seg)


def attend_back_kernel(
    q_ref, k_ref, v_ref, o_ref, do_ref, lse_ref, seg_ref, dq_ref, dk_ref, dv_ref, qa, ka, va, da, aq, cm
):
    @pl.when(pl.program_id(0) == 0)
    def _():
        cm[...] = causal_penalty()

    hot, pen = episode_rows(seg_ref[...])
    ids = lax.broadcasted_iota(jnp.int32, (8, WIN), 0)
    ones3 = jnp.where(ids < 3, 1.0, 0.0)
    z48 = jnp.zeros((48, WIN), f32)
    z88 = jnp.zeros((88, WIN), f32)

    def rows3(v):
        a = v.astype(bf16).astype(f32)
        b = (v - a).astype(bf16).astype(f32)
        return jnp.where(ids == 0, a, jnp.where(ids == 1, b, jnp.where(ids == 2, v - a - b, 0.0)))

    tail_k = jnp.concatenate([pen, ones3, z48], axis=0).astype(bf16)
    tail_v = jnp.concatenate([ones3, z88], axis=0).astype(bf16)
    for h in range(GH):
        rows = slice(h * HD, (h + 1) * HD)
        high, low = split_scaled(q_ref[rows, :])
        k, v, g = k_ref[rows, :], v_ref[rows, :], do_ref[rows, :]
        delta = jnp.sum(g.astype(f32) * o_ref[rows, :].astype(f32), axis=0, keepdims=True)
        tail_q = jnp.concatenate([hot, rows3(-lse_ref[h]), z48], axis=0).astype(bf16)
        tail_g = jnp.concatenate([rows3(-delta), z88], axis=0).astype(bf16)
        qa[h] = jnp.concatenate([high, low, tail_q], axis=0)
        ka[h] = jnp.concatenate([k, k, tail_k], axis=0).T
        va[h] = jnp.concatenate([v, tail_v], axis=0).T
        da[h] = jnp.concatenate([g, tail_g], axis=0)
    c = cm[...]
    scale = HD**-0.5
    step = 4
    nb = WIN // BLOCK
    for kb in range(nb):
        q0, q1 = kb * BLOCK, min(nb, kb + 3) * BLOCK
        ks = slice(q0, q0 + BLOCK)
        for hb in range(0, GH, step):
            heads = range(hb, hb + step)
            rows = [slice(h * HD, (h + 1) * HD) for h in heads]
            s = [dot(ka[h, ks, :], qa[h, :, q0:q1]) for h in heads]
            dp = [dot(va[h, ks, :], da[h, :, q0:q1]) for h in heads]
            s = [
                jnp.concatenate([x[:, :BLOCK] + c, x[:, BLOCK:]], axis=1) if q1 - q0 > BLOCK else x + c
                for x in s
            ]
            p = [jnp.exp2(x) for x in s]
            ds = [(x * y).astype(bf16) for x, y in zip(p, dp)]
            pb = [x.astype(bf16) for x in p]
            dv = [dot(do_ref[x, q0:q1], y, NT) for x, y in zip(rows, pb)]
            dk = [dot(q_ref[x, q0:q1], y, NT) for x, y in zip(rows, ds)]
            dq = [dot(k_ref[x, ks], y) for x, y in zip(rows, ds)]
            for i in range(step):
                dv_ref[rows[i], ks] = dv[i].astype(bf16)
                dk_ref[rows[i], ks] = (dk[i] * scale).astype(bf16)
                done = min(nb, kb + 2) * BLOCK if kb else 0
                if done > q0:
                    aq[rows[i], q0:done] += dq[i][:, : done - q0]
                if q1 > max(done, q0):
                    at = max(done, q0)
                    aq[rows[i], at:q1] = dq[i][:, at - q0 :]
    dq_ref[...] = (aq[...] * scale).astype(bf16)


def attend_back(project_t, attended_t, grad_t, lse, seg):
    groups = HEADS // GH
    return pl.pallas_call(
        attend_back_kernel,
        grid=(groups,),
        in_specs=[
            head_rows(0),
            head_rows(groups),
            head_rows(2 * groups),
            head_rows(0),
            head_rows(0),
            pl.BlockSpec((GH, 1, WIN), lambda g: (g, 0, 0)),
            whole((1, WIN)),
        ],
        out_specs=[head_rows(0)] * 3,
        out_shape=[jax.ShapeDtypeStruct((D, WIN), bf16)] * 3,
        scratch_shapes=[
            pltpu.VMEM((GH, 128, WIN), bf16),
            pltpu.VMEM((GH, WIN, 128), bf16),
            pltpu.VMEM((GH, WIN, 128), bf16),
            pltpu.VMEM((GH, 128, WIN), bf16),
            pltpu.VMEM((GR, WIN), f32),
            pltpu.VMEM((BLOCK, BLOCK), f32),
        ],
        compiler_params=PARAMS,
        cost_estimate=pl.CostEstimate(flops=40_000_000_000, bytes_accessed=14 << 20, transcendentals=0),
        name="attend_back",
    )(project_t, project_t, project_t, attended_t, grad_t, lse, seg)


def gelu_both(u):
    a, b = math.sqrt(2 / math.pi), 0.044715
    sq = u * u
    t = jnp.tanh(u * (a + (a * b) * sq))
    half = 0.5 + 0.5 * t
    slope = half + (0.5 * u) * (1.0 - t * t) * (a + (3 * a * b) * sq)
    return u * half, slope


def ffn_kernel(nd, me_ref, x_ref, at_ref, cot_ref, vec_ref, be_ref, *rest):
    w2, we, wr = rest[:nd], rest[nd : 2 * nd], rest[2 * nd : 3 * nd]
    (
        out_ref, gm_ref, dt_ref, es_ref, ek_ref, rs_ref, rk_ref, gbe_ref, gv_ref,
        comb, exp, red, mid, n2, n2t, cott, oacc, nacc, ascr, gscr, ext, rdt, tmp, sems,
    ) = rest[3 * nd :]
    i = pl.program_id(0)
    steps = nd // 2
    me = me_ref[0]
    core = me & 1
    chunk = exp.shape[1] // steps
    rb = D // nd
    rr = chunk // 2
    tb = 256

    @pl.when(i == 0)
    def _():
        got = load_blocks(me, [r.at[:, D : 2 * D] for r in w2], comb, sems, 0)
        late = load_blocks(me, we, exp, sems, nd) + load_blocks(me, wr, red, sems, 2 * nd)
        cott[...] = cot_ref[...].T
        for copy in got:
            copy.wait()
        for t in range(0, WIN, tb):
            rows = slice(t, t + tb)
            m = (
                x_ref[rows, :].astype(f32)
                + dot(at_ref[:, rows].T, comb[...])
                + vec_ref[2:3, :]
            )
            mid[rows, :] = m
            h, _ = norm_parts(m)
            n = (h * vec_ref[3:4, :] + vec_ref[4:5, :]).astype(bf16)
            n2[rows, :] = n
            n2t[:, rows] = n.T
        oacc[...] = jnp.zeros_like(oacc)
        nacc[...] = jnp.zeros_like(nacc)
        for copy in late:
            copy.wait()

    j = (me >> 1) ^ i
    cols = pl.ds(pl.multiple_of(j * chunk, 128), chunk)
    ext[...] = exp[:, cols].T
    rdt[...] = red[cols, :].T
    bias = be_ref[...]
    gb = jnp.zeros((1, chunk), f32)
    for t in range(0, WIN, tb):
        rows = slice(t, t + tb)
        u = dot(n2[rows, :], exp[:, cols]) + bias
        ga = dot(cot_ref[rows, :], rdt[...])
        act, slope = gelu_both(u)
        act = act.astype(bf16)
        gu = (ga * slope).astype(bf16)
        ascr[rows, :] = act
        gscr[rows, :] = gu
        gb = gb + jnp.sum(gu.astype(f32), axis=0, keepdims=True)
        oacc[rows, :] += dot(act, red[cols, :])
        nacc[rows, :] += dot(gu, ext[...])
    gbe_ref[...] = gb
    ge = dot(n2t[...], gscr[...]).astype(bf16)
    tmp[...] = ge
    for s in range(steps):
        far = pl.multiple_of((me ^ (2 * s + 1)) * rb, 16)
        near = pl.multiple_of((me ^ (2 * s)) * rb, 16)
        es_ref[s] = tmp[pl.ds(far, rb), :]
        ek_ref[s] = tmp[pl.ds(near, rb), :]
    gr = dot(cott[...], ascr[...]).astype(bf16)
    ext[...] = gr.T
    rs_ref[i, :rr, :] = ext[pl.ds(pl.multiple_of((1 - core) * rr, 16), rr), :]
    rk_ref[i, :rr, :] = ext[pl.ds(pl.multiple_of(core * rr, 16), rr), :]

    @pl.when(i == steps - 1)
    def _():
        zero = jnp.zeros((1, D), f32)
        ggain, gshift, gattend, greduce = zero, zero, zero, zero
        for t in range(0, WIN, tb):
            rows = slice(t, t + tb)
            m = mid[rows, :]
            out_ref[rows, :] = (m + oacc[rows, :] + vec_ref[5:6, :]).astype(bf16)
            h, rstd = norm_parts(m)
            g = nacc[rows, :]
            cot = cot_ref[rows, :].astype(f32)
            gm = cot + norm_back(g, vec_ref[3:4, :], h, rstd)
            gm_ref[rows, :] = gm
            low = gm.astype(bf16)
            n2[rows, :] = low
            n2t[:, rows] = low.T
            ggain += jnp.sum(g * h, axis=0, keepdims=True)
            gshift += jnp.sum(g, axis=0, keepdims=True)
            gattend += jnp.sum(low.astype(f32), axis=0, keepdims=True)
            greduce += jnp.sum(cot, axis=0, keepdims=True)
        gv_ref[...] = jnp.concatenate(
            [zero, zero, gattend, ggain, gshift, greduce, zero, zero], axis=0
        )
        dt_ref[...] = dot(comb[...], n2t[...]).astype(bf16)
        mid[:D, :] = dot(at_ref[...], n2[...])
        for s in range(steps):
            far = pl.multiple_of((me ^ (2 * s + 1)) * rb, 16)
            near = pl.multiple_of((me ^ (2 * s)) * rb, 16)
            rs_ref[s, rr : rr + rb, :] = mid[pl.ds(far, rb), :].astype(bf16)
            rk_ref[s, rr : rr + rb, :] = mid[pl.ds(near, rb), :].astype(bf16)


def feed_forward(me, tokens, attended_t, cotangent, vec, bias, w2, we, wr):
    nd = len(we)
    ff = we[0].shape[1]
    steps = nd // 2
    chunk = ff // steps
    rb, rr = D // nd, chunk // 2
    half_e = pl.BlockSpec((steps, rb, chunk), lambda i, s: (0, 0, (s[0] >> 1) ^ i))
    by_chunk = pl.BlockSpec((1, chunk), lambda i, s: (0, (s[0] >> 1) ^ i))
    shape = jax.ShapeDtypeStruct
    return pl.pallas_call(
        functools.partial(ffn_kernel, nd),
        grid_spec=pltpu.PrefetchScalarGridSpec(
            num_scalar_prefetch=1,
            grid=(steps,),
            in_specs=[whole((WIN, D)), whole((D, WIN)), whole((WIN, D)), whole((16, D)), by_chunk]
            + [ANY] * (3 * nd),
            out_specs=[
                whole((WIN, D)),
                whole((WIN, D)),
                whole((D, WIN)),
                half_e,
                half_e,
                whole((steps, rr + rb, D)),
                whole((steps, rr + rb, D)),
                by_chunk,
                whole((8, D)),
            ],
            scratch_shapes=[
                pltpu.VMEM((D, D), bf16),
                pltpu.VMEM((D, ff), bf16),
                pltpu.VMEM((ff, D), bf16),
                pltpu.VMEM((WIN, D), f32),
                pltpu.VMEM((WIN, D), bf16),
                pltpu.VMEM((D, WIN), bf16),
                pltpu.VMEM((D, WIN), bf16),
                pltpu.VMEM((WIN, D), f32),
                pltpu.VMEM((WIN, D), f32),
                pltpu.VMEM((WIN, chunk), bf16),
                pltpu.VMEM((WIN, chunk), bf16),
                pltpu.VMEM((chunk, D), bf16),
                pltpu.VMEM((D, chunk), bf16),
                pltpu.VMEM((D, chunk), bf16),
                pltpu.SemaphoreType.DMA((3 * nd,)),
            ],
        ),
        out_shape=[
            shape((WIN, D), bf16),
            shape((WIN, D), f32),
            shape((D, WIN), bf16),
            shape((steps, rb, ff), bf16),
            shape((steps, rb, ff), bf16),
            shape((steps, rr + rb, D), bf16),
            shape((steps, rr + rb, D), bf16),
            shape((1, ff), f32),
            shape((8, D), f32),
        ],
        compiler_params=PARAMS,
        cost_estimate=pl.CostEstimate(flops=12 * WIN * D * ff, bytes_accessed=40 << 20, transcendentals=0),
        name="feed_forward",
    )(me, tokens, attended_t, cotangent, vec, bias, *w2, *we, *wr)


def project_back_kernel(nd, me_ref, x_ref, gm_ref, nt_ref, dq_ref, dk_ref, dv_ref, vec_ref, gv_ref, *rest):
    w1, w2 = rest[:nd], rest[nd : 2 * nd]
    gt_ref, as_ref, ak_ref, bs_ref, bk_ref, s1, s2, tmp, gx, gvt, sems = rest[2 * nd :]
    me = me_ref[0]
    steps = nd // 2
    rb = D // nd
    first = load_blocks(me, w1, s1, sems, 0)
    second = load_blocks(me, w2, s2, sems, nd)

    def emit(source, send, keep, at, width):
        for s in range(steps):
            far = pl.multiple_of((me ^ (2 * s + 1)) * rb, 16)
            near = pl.multiple_of((me ^ (2 * s)) * rb, 16)
            send[s, :, at : at + width] = source[pl.ds(far, rb), :]
            keep[s, :, at : at + width] = source[pl.ds(near, rb), :]

    for c, (ref, send, keep, at) in enumerate(
        ((dq_ref, as_ref, ak_ref, 0), (dk_ref, as_ref, ak_ref, D), (dv_ref, bs_ref, bk_ref, 0))
    ):
        for b in range(0, D, BLOCK):
            tmp[:, b : b + BLOCK] = dot(nt_ref[...], ref[b : b + BLOCK, :].T).astype(bf16)
        emit(tmp, send, keep, at, D)
    for copy in first:
        copy.wait()
    for copy in second:
        copy.wait()
    for t in range(0, WIN, BLOCK):
        cols = slice(t, t + BLOCK)
        gx[:, cols] = (
            dot(s1[:, :D], dq_ref[:, cols])
            + dot(s1[:, D : 2 * D], dk_ref[:, cols])
            + dot(s2[:, :D], dv_ref[:, cols])
        )
    ggain = jnp.zeros((1, D), f32)
    gshift = jnp.zeros((1, D), f32)
    for t in range(0, WIN, BLOCK):
        rows = slice(t, t + BLOCK)
        g = gx[:, rows].T
        h, rstd = norm_parts(x_ref[rows, :].astype(f32))
        gt_ref[rows, :] = gm_ref[rows, :] + norm_back(g, vec_ref[0:1, :], h, rstd)
        ggain += jnp.sum(g * h, axis=0, keepdims=True)
        gshift += jnp.sum(g, axis=0, keepdims=True)
    rows = jnp.concatenate(
        [ggain, gshift, gv_ref[2:, :], jnp.zeros((VEC - gv_ref.shape[0], D), f32)], axis=0
    )
    gvt[...] = rows.T.astype(bf16)
    emit(gvt, bs_ref, bk_ref, D, VEC)


def project_back(me, tokens, grad_middle, normed_t, dq, dk, dv, vec, gvec, w1, w2):
    nd = len(w1)
    steps, rb = nd // 2, D // nd
    shape = jax.ShapeDtypeStruct
    return pl.pallas_call(
        functools.partial(project_back_kernel, nd),
        grid=(1,),
        in_specs=[SMEM, whole((WIN, D)), whole((WIN, D))]
        + [whole((D, WIN))] * 4
        + [whole((16, D)), whole((16, D))]
        + [ANY] * (2 * nd),
        out_specs=[whole((WIN, D))]
        + [whole((steps, rb, 2 * D))] * 2
        + [whole((steps, rb, D + VEC))] * 2,
        out_shape=[shape((WIN, D), f32)]
        + [shape((steps, rb, 2 * D), bf16)] * 2
        + [shape((steps, rb, D + VEC), bf16)] * 2,
        scratch_shapes=[
            pltpu.VMEM((D, w1[0].shape[1]), bf16),
            pltpu.VMEM((D, w2[0].shape[1]), bf16),
            pltpu.VMEM((D, D), bf16),
            pltpu.VMEM((D, WIN), f32),
            pltpu.VMEM((D, VEC), bf16),
            pltpu.SemaphoreType.DMA((2 * nd,)),
        ],
        compiler_params=PARAMS,
        cost_estimate=pl.CostEstimate(flops=4 * WIN * D * 3 * D, bytes_accessed=30 << 20, transcendentals=0),
        name="project_back",
    )(me, tokens, grad_middle, normed_t, dq, dk, dv, vec, gvec, *w1, *w2)


def body(nd, nf, tokens, segment_ids, cotangent, projector, combiner, attend_bias, expander,
         expand_bias, reducer, reduce_bias, first_gain, first_shift, second_gain, second_shift):
    r = projector.shape[0]
    up, down = orders(nd)
    me = lax.axis_index("dp").astype(jnp.int32).reshape(1)
    vec = jnp.stack(
        [first_gain, first_shift, attend_bias, second_gain, second_shift, reduce_bias], axis=1
    )
    vec = jnp.concatenate([vec, expand_bias.reshape(r, 4), jnp.zeros((r, VEC - 10), bf16)], axis=1)
    shard1 = jnp.concatenate([projector[:, : 2 * D], vec], axis=1)
    shard2 = jnp.concatenate([projector[:, 2 * D :], combiner], axis=1)
    z1, z2 = gather_z(shard1, nf), gather_z(shard2, nf)
    w1, w2 = gather_dp(z1, up + [1], nd), gather_dp(z2, down + [1], nd)
    ze, zr = gather_z(expander, nf), gather_z(reducer, nf)
    we, wr = gather_dp(ze, up + [1], nd), gather_dp(zr, down + [1], nd)

    project_t, normed_t, vecs = project(me, tokens, w1, w2)
    attended_t, lse = attend(project_t, segment_ids)
    bias = vecs[6:10].T.reshape(1, -1)
    out, grad_middle, grad_t, es, ek, rs, rk, gbe, gvec = feed_forward(
        me, tokens, attended_t, cotangent, vecs, bias, w2, we, wr
    )
    ve = scatter_dp(es, ek, up, nd)
    vr = scatter_dp(rs, rk, down, nd)
    grad_expander = scatter_z(ve, [r], nf)
    grad_rc = scatter_z(vr, [reducer.shape[0], r], nf)
    dq, dk, dv = attend_back(project_t, attended_t, grad_t, lse, segment_ids)
    gvec = jnp.concatenate(
        [gvec[:6], gbe.reshape(-1, 4).T, jnp.zeros((6, D), f32)], axis=0
    )
    grad_tokens, s1, k1, s2, k2 = project_back(
        me, tokens, grad_middle, normed_t, dq, dk, dv, vecs, gvec, w1, w2
    )
    g1 = scatter_z(scatter_dp(s1, k1, up, nd), [r], nf)
    g2 = scatter_z(scatter_dp(s2, k2, down, nd), [r], nf)
    small = g2[:, D : D + 10]
    return (
        out,
        grad_tokens,
        jnp.concatenate([g1, g2[:, :D]], axis=1),
        grad_rc[reducer.shape[0] :],
        small[:, 2],
        grad_expander,
        small[:, 6:10].reshape(-1),
        grad_rc[: reducer.shape[0]],
        small[:, 5],
        small[:, 0],
        small[:, 1],
        small[:, 3],
        small[:, 4],
    )


def solution(mesh):
    rows, flat = P(("dp", "fsdp"), None), P(("dp", "fsdp"))
    return jax.shard_map(
        functools.partial(body, mesh.shape["dp"], mesh.shape["fsdp"]),
        mesh=mesh,
        in_specs=(rows, rows, rows, rows, rows, flat, rows, flat, rows, flat, flat, flat, flat, flat),
        out_specs=(rows, rows, rows, rows, flat, rows, flat, rows, flat, flat, flat, flat, flat),
        check_vma=False,
    )
```

```python
import functools
import math

import jax
import jax.numpy as jnp
import numpy as np
from jax import lax
from jax.experimental import pallas as pl
from jax.experimental.pallas import tpu as pltpu
from jax.sharding import PartitionSpec as P

D = 768
HD = 32
HEADS = 24
WIN = 1024
BLOCK = 256
EPS = 1e-05
LOG2E = math.log2(math.e)
BIG = float(2**30)
VEC = 128
f32 = jnp.float32
bf16 = jnp.bfloat16
NN = (((1,), (0,)), ((), ()))
NT = (((1,), (1,)), ((), ()))
ANY = pl.BlockSpec(memory_space=pl.ANY)
SMEM = pl.BlockSpec(memory_space=pltpu.SMEM)


def room(mib):
    return pltpu.CompilerParams(vmem_limit_bytes=mib << 20)


def dot(a, b, dims=NN):
    return lax.dot_general(a, b, dims, preferred_element_type=f32)


def whole(shape):
    return pl.BlockSpec(shape, lambda *_: (0,) * len(shape), pipeline_mode=pl.Buffered(1))


def flip(value, bit, count):
    return lax.ppermute(value, "dp", [(i, i ^ bit) for i in range(count)])


def shift(value, step, count):
    return lax.ppermute(value, "fsdp", [(i, (i + step) % count) for i in range(count)])


def after(value, *others):
    return lax.optimization_barrier((value, others))[0]


def shifts(shard, nf):
    return [shard] + [shift(shard, k, nf) for k in range(1, nf)]


def line_up_kernel(nf, moves, me_ref, *refs):
    me = me_ref[0]
    parts, outs = refs[:nf], refs[nf:]
    for k in range(nf):
        for j in range(nf):
            @pl.when(lax.rem(me - k + nf, nf) == j)
            def _():
                for source, rows, out, row, col in moves:
                    value = parts[k][source : source + rows, :]
                    at = row + j * rows
                    outs[out][at : at + rows, col : col + value.shape[1]] = value


def line_up(nf, moves, shapes, parts):
    return pl.pallas_call(
        functools.partial(line_up_kernel, nf, moves),
        in_specs=[SMEM] + [whole(p.shape) for p in parts],
        out_specs=[whole(x) for x in shapes],
        out_shape=[jax.ShapeDtypeStruct(x, bf16) for x in shapes],
        grid=(1,),
        compiler_params=room(10),
        cost_estimate=pl.CostEstimate(flops=0, bytes_accessed=4 << 20, transcendentals=0),
        name="line_up",
    )(lax.axis_index("fsdp").astype(jnp.int32).reshape(1), *parts)


def add(a, b):
    return (a.astype(f32) + b.astype(f32)).astype(bf16)


def spread_plane(block, nd):
    return {m: flip(block, m, nd) if m else block for m in range(0, nd, 2)}


def spread_cores(blocks, nd):
    both = {**blocks, **{m ^ 1: flip(v, 1, nd) for m, v in blocks.items()}}
    return [both[m] for m in range(nd)]


def sum_cores(send, keep, nd):
    got = flip(send, 1, nd)
    return [add(keep[m], got[m]) for m in range(nd // 2)]


def meet_plane(totals, nd):
    return [flip(v, 2 * m, nd) if m else v for m, v in enumerate(totals)]


def scatter_z(block, rows, nf):
    me = lax.axis_index("fsdp")

    def piece(z):
        got, at = [], 0
        for r in rows:
            got.append(lax.dynamic_slice_in_dim(block, at + z * r, r, 0))
            at += nf * r
        return got[0] if len(got) == 1 else jnp.concatenate(got, axis=0)

    total = piece(me).astype(f32)
    for k in range(1, nf):
        total = total + shift(piece(lax.rem(me + k, nf)), k, nf).astype(f32)
    return total


def half_columns(q):
    o = np.arange(D // 2)
    source = (o // q) * (2 * q) + o % q
    picks = np.arange(D)[None, :, None] == (source[None, None, :] + q * np.arange(2)[:, None, None])
    return jnp.asarray(picks, bf16)


def pack_kernel(proj_ref, exp_ref, red_ref, comb_ref, pick_ref, *refs):
    vec_refs, (w_ref, f1_ref, f2_ref) = refs[:-3], refs[-3:]
    r, q = proj_ref.shape[0], red_ref.shape[0] // 2
    w_ref[:, : 3 * D] = proj_ref[...]
    row = [ref[...].astype(f32).reshape(1, -1) for ref in vec_refs]
    rows = row[:6] + [row[6][:, j * r : (j + 1) * r] for j in range(4)]
    rows.append(jnp.zeros((VEC - 10, r), f32))
    w_ref[:, 3 * D :] = jnp.concatenate(rows, axis=0).T.astype(bf16)
    for h, ref in enumerate((f1_ref, f2_ref)):
        for c in range(4):
            at, col = (c // 2) * r, (c % 2) * (D // 2)
            ref[at : at + r, col : col + D // 2] = dot(
                exp_ref[:, c * D : (c + 1) * D], pick_ref[h]
            ).astype(bf16)
        ref[2 * r : 2 * r + q, :] = red_ref[h * q : (h + 1) * q, :]
    f1_ref[2 * r + q :, :] = comb_ref[...]


def pack(projector, expander, reducer, combiner, picks, vectors):
    r, q = projector.shape[0], reducer.shape[0] // 2
    shapes = [(r, 3 * D + VEC), (3 * r + q, D), (2 * r + q, D)]
    arrays = (projector, expander, reducer, combiner, picks, *vectors)
    return pl.pallas_call(
        pack_kernel,
        grid=(1,),
        in_specs=[whole(a.shape) for a in arrays],
        out_specs=[whole(x) for x in shapes],
        out_shape=[jax.ShapeDtypeStruct(x, bf16) for x in shapes],
        compiler_params=room(58),
        cost_estimate=pl.CostEstimate(flops=0, bytes_accessed=3 << 20, transcendentals=0),
        name="pack",
    )(*arrays)


def pieces_kernel(nf, moves, me_ref, *refs):
    terms, outs = refs[:-nf], refs[-nf:]
    me = me_ref[0]
    for row, rows, at in moves:
        for j in range(nf):
            here = slice(row + j * rows, row + (j + 1) * rows)
            value = sum(t[here, :].astype(f32) for t in terms).astype(bf16)
            for k in range(nf):
                @pl.when(lax.rem(me + k, nf) == j)
                def _():
                    outs[k][at : at + rows, :] = value


def pieces(nf, moves, terms):
    rows = sum(m[1] for m in moves)
    return pl.pallas_call(
        functools.partial(pieces_kernel, nf, moves),
        in_specs=[SMEM] + [whole(x.shape) for x in terms],
        out_specs=[whole((rows, D))] * nf,
        out_shape=[jax.ShapeDtypeStruct((rows, D), bf16)] * nf,
        grid=(1,),
        compiler_params=room(12),
        cost_estimate=pl.CostEstimate(flops=0, bytes_accessed=6 << 20, transcendentals=0),
        name="pieces",
    )(lax.axis_index("fsdp").astype(jnp.int32).reshape(1), *terms)


def finish_kernel(r, q, nf, pick_ref, *refs):
    halves, (ge_ref, gr_ref, gc_ref) = (refs[:nf], refs[nf : 2 * nf]), refs[2 * nf :]
    for c in range(4):
        total = jnp.zeros((r, D), f32)
        for h in range(2):
            at, col = (c // 2) * r, (c % 2) * (D // 2)
            for p in halves[h]:
                total += dot(p[at : at + r, col : col + D // 2], pick_ref[h], NT)
        ge_ref[:, c * D : (c + 1) * D] = total
    for h in range(2):
        gr_ref[h * q : (h + 1) * q, :] = sum(p[2 * r : 2 * r + q, :].astype(f32) for p in halves[h])
    gc_ref[...] = sum(p[2 * r + q :, :].astype(f32) for p in halves[1])


def finish(r, q, picks, first, second):
    shapes = [(r, 4 * D), (2 * q, D), (r, D)]
    arrays = (picks, *first, *second)
    return pl.pallas_call(
        functools.partial(finish_kernel, r, q, len(first)),
        grid=(1,),
        in_specs=[whole(x.shape) for x in arrays],
        out_specs=[whole(x) for x in shapes],
        out_shape=[jax.ShapeDtypeStruct(x, f32) for x in shapes],
        compiler_params=room(12),
        cost_estimate=pl.CostEstimate(flops=0, bytes_accessed=3 << 20, transcendentals=0),
        name="finish",
    )(*arrays)


def load_blocks(me, refs, target, sems, base, row=0, rows=None, col=0):
    rows = rows or refs[0].shape[0]
    width = refs[0].shape[1]
    copies = []
    for m, ref in enumerate(refs):
        at = pl.multiple_of((me ^ m) * rows, 16)
        copy = pltpu.make_async_copy(
            ref.at[pl.ds(row, rows), :], target.at[pl.ds(at, rows), pl.ds(col, width)], sems.at[base + m]
        )
        copy.start()
        copies.append(copy)
    return copies


def norm_parts(v):
    c = v - jnp.mean(v, axis=-1, keepdims=True)
    rstd = lax.rsqrt(jnp.mean(c * c, axis=-1, keepdims=True) + EPS)
    return c * rstd, rstd


def norm_back(grad, gain, h, rstd):
    e = grad * gain
    return (e - jnp.mean(e, -1, keepdims=True) - h * jnp.mean(e * h, -1, keepdims=True)) * rstd


def prepare_kernel(x_ref, cot_ref, ht_ref, ct_ref):
    @pl.loop(0, WIN // BLOCK)
    def _(t):
        rows = pl.ds(pl.multiple_of(t * BLOCK, BLOCK), BLOCK)
        h, _ = norm_parts(x_ref[rows, :].astype(f32))
        ht_ref[:, rows] = h.T
        ct_ref[:, rows] = cot_ref[rows, :].T


def prepare(tokens, cotangent):
    return pl.pallas_call(
        prepare_kernel,
        grid=(1,),
        in_specs=[whole((WIN, D))] * 2,
        out_specs=[whole((D, WIN))] * 2,
        out_shape=[jax.ShapeDtypeStruct((D, WIN), f32), jax.ShapeDtypeStruct((D, WIN), bf16)],
        compiler_params=room(20),
        cost_estimate=pl.CostEstimate(flops=5_000_000_000, bytes_accessed=8 << 20, transcendentals=0),
        name="prepare",
    )(tokens, cotangent)


def project_kernel(nd, me_ref, ht_ref, turn_ref, *rest):
    w = rest[:nd]
    pt_ref, nt_ref, vec_ref, bias_ref, full, sems = rest[nd:]
    for copy in load_blocks(me_ref[0], w, full, sems, 0):
        copy.wait()
    columns = full[:, 3 * D :].astype(f32)
    vec = columns.T
    vec_ref[...] = vec[:16]
    low = vec[:16].astype(bf16)
    for i in range(4):
        c, row = i % 2, 6 + 2 * (i // 2)
        parts = [dot(low[:, c * (D // 2) : (c + 1) * (D // 2)], turn_ref[k], NT) for k in range(2)]
        bias_ref[:, i * D : (i + 1) * D] = parts[0][row : row + 1] + parts[1][row + 1 : row + 2]
    nt_ref[...] = (ht_ref[...] * columns[:, 0:1] + columns[:, 1:2]).astype(bf16)

    for c in range(0, 3 * D, BLOCK):
        cols = slice(c, c + BLOCK)
        pt_ref[cols, :] = dot(full[:, cols].T, nt_ref[...]).astype(bf16)


def project(me, normed_t, turns, w):
    nd = len(w)
    return pl.pallas_call(
        functools.partial(project_kernel, nd),
        in_specs=[SMEM, whole((D, WIN)), whole(turns.shape)] + [ANY] * nd,
        out_specs=[whole((3 * D, WIN)), whole((D, WIN)), whole((16, D)), whole((1, 4 * D))],
        out_shape=[
            jax.ShapeDtypeStruct((3 * D, WIN), bf16),
            jax.ShapeDtypeStruct((D, WIN), bf16),
            jax.ShapeDtypeStruct((16, D), f32),
            jax.ShapeDtypeStruct((1, 4 * D), f32),
        ],
        scratch_shapes=[pltpu.VMEM((D, w[0].shape[1]), bf16), pltpu.SemaphoreType.DMA((nd,))],
        grid=(1,),
        compiler_params=room(26),
        cost_estimate=pl.CostEstimate(flops=2 * WIN * D * 3 * D, bytes_accessed=12 << 20, transcendentals=0),
        name="project",
    )(me, normed_t, turns, *w)


GH = 8
SH = 8
GR = GH * HD


def causal_penalty():
    ik = lax.broadcasted_iota(jnp.int32, (BLOCK, BLOCK), 0)
    iq = lax.broadcasted_iota(jnp.int32, (BLOCK, BLOCK), 1)
    return jnp.where(iq >= ik, 0.0, -BIG)


def split_scaled(q):
    scaled = q.astype(f32) * (HD**-0.5 * LOG2E)
    high = scaled.astype(bf16)
    return high, (scaled - high.astype(f32)).astype(bf16)


def episode_rows(seg):
    hot = lax.broadcasted_iota(jnp.int32, (8, WIN), 0) == seg
    return hot.astype(f32), jnp.where(hot, 0.0, -BIG)


def attend_kernel(q_ref, k_ref, v_ref, seg_ref, out_ref, lse_ref, qa, ka, va, cm):
    @pl.when(pl.program_id(0) == 0)
    def _():
        cm[...] = causal_penalty()

    hot, pen = episode_rows(seg_ref[...])
    pad = jnp.zeros((56, WIN), f32)
    tail_q = jnp.concatenate([hot, pad], axis=0).astype(bf16)
    tail_k = jnp.concatenate([pen, pad], axis=0).astype(bf16)
    ones = jnp.ones((16, WIN), bf16)
    for h in range(GH):
        rows = slice(h * HD, (h + 1) * HD)
        high, low = split_scaled(q_ref[rows, :])
        k = k_ref[rows, :]
        qa[h] = jnp.concatenate([high, low, tail_q], axis=0)
        ka[h] = jnp.concatenate([k, k, tail_k], axis=0).T
        va[h] = jnp.concatenate([v_ref[rows, :], ones], axis=0)
    c = cm[...]
    for qb in range(WIN // BLOCK):
        k0, k1 = max(0, qb - 2) * BLOCK, (qb + 1) * BLOCK
        qs = slice(qb * BLOCK, k1)
        for hb in range(0, GH, SH):
            heads = range(hb, hb + SH)
            s = [dot(ka[h, k0:k1, :], qa[h, :, qs]) for h in heads]
            w = k1 - k0 - BLOCK
            s = [jnp.concatenate([x[:w], x[w:] + c], axis=0) if w else x + c for x in s]
            top = [jnp.max(x, axis=0, keepdims=True) for x in s]
            p = [jnp.exp2(x - y) for x, y in zip(s, top)]
            o = [dot(va[h, :, k0:k1], y.astype(bf16)) for h, y in zip(heads, p)]
            for i, h in enumerate(heads):
                total = o[i][HD : HD + 1]
                out_ref[h * HD : (h + 1) * HD, qs] = (o[i][:HD] * (1.0 / total)).astype(bf16)
                lse_ref[h, :, qs] = top[i] + jnp.log2(total)


GROUPS = HEADS // GH


def head_rows(index):
    return pl.BlockSpec((GR, WIN), lambda i: (index, 0))


def head_sums(index):
    return pl.BlockSpec((GH, 1, WIN), lambda i: (index, 0, 0))


def attend(group, project_t, seg):
    return pl.pallas_call(
        attend_kernel,
        grid=(1,),
        in_specs=[head_rows(group + j * GROUPS) for j in range(3)] + [whole((1, WIN))],
        out_specs=[head_rows(0), head_sums(0)],
        out_shape=[
            jax.ShapeDtypeStruct((GR, WIN), bf16),
            jax.ShapeDtypeStruct((GH, 1, WIN), f32),
        ],
        scratch_shapes=[
            pltpu.VMEM((GH, 128, WIN), bf16),
            pltpu.VMEM((GH, WIN, 128), bf16),
            pltpu.VMEM((GH, HD + 16, WIN), bf16),
            pltpu.VMEM((BLOCK, BLOCK), f32),
        ],
        compiler_params=room(24),
        cost_estimate=pl.CostEstimate(flops=7_000_000_000, bytes_accessed=3 << 20, transcendentals=0),
        name="attend",
    )(project_t, project_t, project_t, seg)


def attend_back_kernel(
    q_ref, k_ref, v_ref, o_ref, do_ref, lse_ref, seg_ref, dq_ref, dk_ref, dv_ref, qa, ka, va, da, aq, cm
):
    hot, pen = episode_rows(seg_ref[...])
    ids = lax.broadcasted_iota(jnp.int32, (8, WIN), 0)
    ones3 = jnp.where(ids < 3, 1.0, 0.0)
    z48 = jnp.zeros((48, WIN), f32)
    z88 = jnp.zeros((88, WIN), f32)

    def rows3(v):
        a = v.astype(bf16).astype(f32)
        b = (v - a).astype(bf16).astype(f32)
        return jnp.where(ids == 0, a, jnp.where(ids == 1, b, jnp.where(ids == 2, v - a - b, 0.0)))

    tail_k = jnp.concatenate([pen, ones3, z48], axis=0).astype(bf16)
    tail_v = jnp.concatenate([ones3, z88], axis=0).astype(bf16)
    for h in range(GH):
        rows = slice(h * HD, (h + 1) * HD)
        high, low = split_scaled(q_ref[rows, :])
        k, v, g = k_ref[rows, :], v_ref[rows, :], do_ref[rows, :]
        delta = jnp.sum(g.astype(f32) * o_ref[rows, :].astype(f32), axis=0, keepdims=True)
        tail_q = jnp.concatenate([hot, rows3(-lse_ref[h]), z48], axis=0).astype(bf16)
        tail_g = jnp.concatenate([rows3(-delta), z88], axis=0).astype(bf16)
        qa[h] = jnp.concatenate([high, low, tail_q], axis=0).T
        ka[h] = jnp.concatenate([k, k, tail_k], axis=0)
        va[h] = jnp.concatenate([v, tail_v], axis=0)
        da[h] = jnp.concatenate([g, tail_g], axis=0).T
    ik = lax.broadcasted_iota(jnp.int32, (BLOCK, BLOCK), 1)
    iq = lax.broadcasted_iota(jnp.int32, (BLOCK, BLOCK), 0)
    cm[...] = jnp.where(iq >= ik, 0.0, -BIG)
    c = cm[...]
    scale = HD**-0.5
    step = 4
    nb = WIN // BLOCK
    for kb in range(nb):
        q0, q1 = kb * BLOCK, min(nb, kb + 3) * BLOCK
        ks = slice(q0, q0 + BLOCK)
        for hb in range(0, GH, step):
            heads = range(hb, hb + step)
            rows = [slice(h * HD, (h + 1) * HD) for h in heads]
            s = [dot(qa[h, q0:q1, :], ka[h, :, ks]) for h in heads]
            dp = [dot(da[h, q0:q1, :], va[h, :, ks]) for h in heads]
            s = [
                jnp.concatenate([x[:BLOCK] + c, x[BLOCK:]], axis=0) if q1 - q0 > BLOCK else x + c
                for x in s
            ]
            p = [jnp.exp2(x) for x in s]
            ds = [(x * y).astype(bf16) for x, y in zip(p, dp)]
            pb = [x.astype(bf16) for x in p]
            dv = [dot(do_ref[x, q0:q1], y) for x, y in zip(rows, pb)]
            dk = [dot(q_ref[x, q0:q1], y) for x, y in zip(rows, ds)]
            dq = [dot(k_ref[x, ks], y, NT) for x, y in zip(rows, ds)]
            for i in range(step):
                dv_ref[rows[i], ks] = dv[i].astype(bf16)
                dk_ref[rows[i], ks] = (dk[i] * scale).astype(bf16)
                done = min(nb, kb + 2) * BLOCK if kb else 0
                if done > q0:
                    aq[rows[i], q0:done] += dq[i][:, : done - q0]
                if q1 > max(done, q0):
                    at = max(done, q0)
                    aq[rows[i], at:q1] = dq[i][:, at - q0 :]
    dq_ref[...] = (aq[...] * scale).astype(bf16)


def attend_back(group, project_t, attended_t, grad_t, lse, seg):
    return pl.pallas_call(
        attend_back_kernel,
        grid=(1,),
        in_specs=[head_rows(group + j * GROUPS) for j in range(3)]
        + [head_rows(0), head_rows(group), head_sums(0), whole((1, WIN))],
        out_specs=[head_rows(0)] * 3,
        out_shape=[jax.ShapeDtypeStruct((GR, WIN), bf16)] * 3,
        scratch_shapes=[
            pltpu.VMEM((GH, WIN, 128), bf16),
            pltpu.VMEM((GH, 128, WIN), bf16),
            pltpu.VMEM((GH, 128, WIN), bf16),
            pltpu.VMEM((GH, WIN, 128), bf16),
            pltpu.VMEM((GR, WIN), f32),
            pltpu.VMEM((BLOCK, BLOCK), f32),
        ],
        compiler_params=room(32),
        cost_estimate=pl.CostEstimate(flops=14_000_000_000, bytes_accessed=5 << 20, transcendentals=0),
        name="attend_back",
    )(project_t, project_t, project_t, attended_t, grad_t, lse, seg)


def gelu_both(u):
    a, b = math.sqrt(2 / math.pi), 0.044715
    sq = u * u
    t = jnp.tanh(u * (a + (a * b) * sq))
    half = 0.5 + 0.5 * t
    slope = half + (0.5 * u) * (1.0 - t * t) * (a + (3 * a * b) * sq)
    return u * half, slope


TB = 1024


def token_loop(step):
    @pl.loop(0, WIN // TB)
    def _(t):
        step(pl.ds(pl.multiple_of(t * TB, TB), TB))


def load_weights(me, nd, blocks, exp, red, sems):
    rb, rr = D // nd, red.shape[0] // nd
    copies = load_blocks(me, blocks, exp, sems, nd, 0, rb, 0)
    copies += load_blocks(me, blocks, exp, sems, 2 * nd, rb, rb, D)
    return copies + load_blocks(me, blocks, red, sems, 3 * nd, 2 * rb, rr, 0)


def ffn_chunk(i, me, nd, cot_ref, be_ref, exp, red, n2, n2t, cott, oacc, nacc, ascr, gscr, tmp, gbe_ref, send, keep):
    rb, rr, chunk = D // nd, red.shape[0] // nd, tmp.shape[1]
    cols = pl.ds(pl.multiple_of(i * chunk, 128), chunk)
    gbe_ref[...] = jnp.zeros((1, chunk), f32)

    def step(rows):
        u = dot(n2[rows, :], exp[:, cols]) + be_ref[...]
        ga = dot(cot_ref[rows, :], red[cols, :], NT)
        act, slope = gelu_both(u)
        act = act.astype(bf16)
        gu = (ga * slope).astype(bf16)
        ascr[rows, :] = act
        gscr[rows, :] = gu
        gbe_ref[...] += jnp.sum(gu.astype(f32), axis=0, keepdims=True)
        oacc[rows, :] += dot(act, red[cols, :])
        nacc[rows, :] += dot(gu, exp[:, cols], NT)

    token_loop(step)
    tmp[...] = dot(n2t[...], gscr[...]).astype(bf16)
    emit(me, tmp, send, keep, pl.ds(pl.multiple_of(i * rb, 16), rb))
    tmp[...] = dot(cott[...], ascr[...]).astype(bf16).T
    per = chunk // rr
    for b in range(per):
        mask = me ^ (i * per + b)
        for odd, ref in ((1, send), (0, keep)):
            @pl.when((mask & 1) == odd)
            def _():
                ref[mask >> 1, 2 * rb : 2 * rb + rr, :] = tmp[b * rr : (b + 1) * rr, :]


def ffn_first_kernel(nd, me_ref, x_ref, cot_ref, cott, vec_ref, be_ref, *rest):
    att, blocks, rest = rest[:GROUPS], rest[GROUPS : GROUPS + nd], rest[GROUPS + nd :]
    mid_ref, n2_ref, part_ref, nacc_ref, send, keep, gbe_ref = rest[:7]
    comb, exp, red, mid, n2, n2t, oacc, nacc, ascr, gscr, tmp, sems = rest[7:]
    i = pl.program_id(0)
    me = me_ref[0]
    rb, rr = D // nd, red.shape[0] // nd
    outs = [
        pltpu.make_async_copy(a, b, sems.at[4 * nd + j])
        for j, (a, b) in enumerate(((mid, mid_ref), (n2, n2_ref), (oacc, part_ref), (nacc, nacc_ref)))
    ]

    @pl.when(i == 0)
    def _():
        got = load_blocks(me, blocks, comb, sems, 0, 2 * rb + rr, rb, 0)
        late = load_weights(me, nd, blocks, exp, red, sems)
        for copy in got:
            copy.wait()

        def step(rows):
            m = x_ref[rows, :].astype(f32) + vec_ref[2:3, :]
            for g in range(GROUPS):
                m += dot(att[g][:, rows].T, comb[g * GR : (g + 1) * GR, :])
            mid[rows, :] = m
            oacc[rows, :] = m + vec_ref[5:6, :]
            h, _ = norm_parts(m)
            n = (h * vec_ref[3:4, :] + vec_ref[4:5, :]).astype(bf16)
            n2[rows, :] = n
            n2t[:, rows] = n.T

        token_loop(step)
        nacc[...] = jnp.zeros_like(nacc)
        outs[0].start()
        outs[1].start()
        for copy in late:
            copy.wait()

    ffn_chunk(i, me, nd, cot_ref, be_ref, exp, red, n2, n2t, cott, oacc, nacc, ascr, gscr, tmp, gbe_ref, send, keep)

    @pl.when(i == pl.num_programs(0) - 1)
    def _():
        outs[2].start()
        outs[3].start()
        for copy in outs:
            copy.wait()


def ffn_last_kernel(nd, me_ref, cot_ref, cott, vec_ref, be_ref, *rest):
    att, blocks, rest = rest[:GROUPS], rest[GROUPS : GROUPS + nd], rest[GROUPS + nd :]
    others, rest = rest[:nd], rest[nd:]
    mid_ref, n2_ref, part_ref, naccin_ref = rest[:4]
    out_ref, gm_ref, dt_ref, send, keep, gbe_ref, gv_ref = rest[4:11]
    comb, exp, red, mid, part, nin, n2, n2t, oacc, nacc, ascr, gscr, tmp, sems = rest[11:]
    i = pl.program_id(0)
    me = me_ref[0]
    rb, rr = D // nd, red.shape[0] // nd
    ins = [
        pltpu.make_async_copy(a, b, sems.at[4 * nd + j])
        for j, (a, b) in enumerate(((n2_ref, n2), (mid_ref, mid), (part_ref, part), (naccin_ref, nin)))
    ]

    @pl.when(i == 0)
    def _():
        ins[0].start()
        got = load_weights(me, nd, blocks, exp, red, sems)
        got += load_blocks(me, others, comb, sems, 0, 2 * rb + rr, rb, 0)
        for copy in ins[1:]:
            copy.start()
        oacc[...] = jnp.zeros_like(oacc)
        nacc[...] = jnp.zeros_like(nacc)
        ins[0].wait()
        n2t[...] = n2[...].T
        for copy in got:
            copy.wait()

    ffn_chunk(i, me, nd, cot_ref, be_ref, exp, red, n2, n2t, cott, oacc, nacc, ascr, gscr, tmp, gbe_ref, send, keep)

    @pl.when(i == pl.num_programs(0) - 1)
    def _():
        for copy in ins[1:]:
            copy.wait()
        gv_ref[...] = jnp.zeros((8, D), f32)

        def step(rows):
            out_ref[rows, :] = (part[rows, :] + oacc[rows, :]).astype(bf16)
            h, rstd = norm_parts(mid[rows, :])
            g = nacc[rows, :] + nin[rows, :]
            cot = cot_ref[rows, :].astype(f32)
            gm = cot + norm_back(g, vec_ref[3:4, :], h, rstd)
            gm_ref[rows, :] = gm
            low = gm.astype(bf16)
            n2[rows, :] = low
            n2t[:, rows] = low.T
            sums = (low.astype(f32), g * h, g, cot)
            gv_ref[2:6, :] += jnp.concatenate([jnp.sum(v, axis=0, keepdims=True) for v in sums], axis=0)

        token_loop(step)
        dt_ref[...] = dot(comb[...], n2t[...]).astype(bf16)
        for g in range(GROUPS):
            tmp[g * GR : (g + 1) * GR, :] = dot(att[g][...], n2[...]).astype(bf16)
        emit(me, tmp, send, keep, slice(2 * rb + rr, 3 * rb + rr))


def ffn_call(kernel, specs, arrays, nd, rows, out_shapes, last):
    ff = 2 * D
    shape = jax.ShapeDtypeStruct
    half = (nd // 2, rows, D)
    wide = pltpu.VMEM((WIN, D), f32)
    low, turned = pltpu.VMEM((WIN, D), bf16), pltpu.VMEM((D, WIN), bf16)
    return pl.pallas_call(
        functools.partial(kernel, nd),
        grid=(ff // D,),
        in_specs=specs,
        out_specs=[whole(x.shape) if last else ANY for x in out_shapes]
        + [whole(half), whole(half), pl.BlockSpec((1, D), lambda i: (0, i))]
        + ([whole((8, D))] if last else []),
        out_shape=list(out_shapes)
        + [shape(half, bf16), shape(half, bf16), shape((1, ff), f32)]
        + ([shape((8, D), f32)] if last else []),
        scratch_shapes=[pltpu.VMEM((D, D), bf16), pltpu.VMEM((D, ff), bf16), pltpu.VMEM((ff, D), bf16)]
        + [wide] * (3 if last else 1)
        + [low, turned, wide, wide, low, low, pltpu.VMEM((D, D), bf16)]
        + [pltpu.SemaphoreType.DMA((4 * nd + 4,))],
        compiler_params=room(56 if last else 44),
        cost_estimate=pl.CostEstimate(flops=12 * WIN * D * ff, bytes_accessed=20 << 20, transcendentals=0),
        name="ffn_last" if last else "ffn_first",
    )(*arrays)


def ffn_first(me, tokens, attended, cotangent, cotangent_t, vec, bias, blocks, nd):
    shape = jax.ShapeDtypeStruct
    outs = [shape((WIN, D), f32), shape((WIN, D), bf16), shape((WIN, D), f32), shape((WIN, D), f32)]
    specs = [SMEM, whole((WIN, D)), whole((WIN, D)), whole((D, WIN)), whole((16, D))]
    specs += [pl.BlockSpec((1, D), lambda i: (0, i))]
    specs += [whole((GR, WIN))] * GROUPS + [ANY] * nd
    arrays = (me, tokens, cotangent, cotangent_t, vec, bias, *attended, *blocks)
    return ffn_call(ffn_first_kernel, specs, arrays, nd, (4 * D) // nd, outs, False)


def ffn_last(me, attended, cotangent, cotangent_t, vec, bias, blocks, others, state, nd):
    shape = jax.ShapeDtypeStruct
    outs = [shape((WIN, D), bf16), shape((WIN, D), f32), shape((D, WIN), bf16)]
    specs = [SMEM, whole((WIN, D)), whole((D, WIN)), whole((16, D)), pl.BlockSpec((1, D), lambda i: (0, i + 2))]
    specs += [whole((GR, WIN))] * GROUPS + [ANY] * (2 * nd + 4)
    arrays = (me, cotangent, cotangent_t, vec, bias, *attended, *blocks, *others, *state)
    return ffn_call(ffn_last_kernel, specs, arrays, nd, (5 * D) // nd, outs, True)


def emit(me, source, send, keep, rows=slice(None), cols=slice(None)):
    steps = send.shape[0]
    rb = source.shape[0] // (2 * steps)
    for s in range(steps):
        far = pl.multiple_of((me ^ (2 * s + 1)) * rb, 16)
        near = pl.multiple_of((me ^ (2 * s)) * rb, 16)
        send[s, rows, cols] = source[pl.ds(far, rb), :]
        keep[s, rows, cols] = source[pl.ds(near, rb), :]


def weight_grad_kernel(nd, me_ref, nt_ref, vec_ref, gv_ref, b1_ref, b2_ref, turn_ref, *rest):
    grads, rest = rest[: 3 * GROUPS], rest[3 * GROUPS :]
    send, keep, full, tmp, gvt, acc, sems = rest[nd:]
    me = me_ref[0]
    copies = load_blocks(me, rest[:nd], full, sems, 0)
    acc[...] = jnp.zeros_like(acc)
    for i, ref in enumerate(grads):
        g = ref[...].T
        gw = dot(nt_ref[...], g)
        tmp[...] = gw.astype(bf16)
        emit(me, tmp, send, keep, cols=slice(i * GR, (i + 1) * GR))
        if i == 0:
            for copy in copies:
                copy.wait()
        w = full[:, i * GR : (i + 1) * GR].astype(f32)
        total = jnp.sum(g.astype(f32), axis=0, keepdims=True)
        for j, value in enumerate((w * gw, w * total)):
            acc[j] += value[:, :128] + value[:, 128:]
    rows = [gv_ref[:6, :]]
    for ref in (b1_ref, b2_ref):
        low = ref[...].astype(bf16)
        for k in range(2):
            rows.append(
                jnp.concatenate([dot(low[:, c * D : (c + 1) * D], turn_ref[k]) for c in range(2)], axis=1)
            )
    rows += [jnp.zeros((6, D), f32), vec_ref[:2, :], jnp.zeros((VEC - 18, D), f32)]
    base = jnp.concatenate(rows, axis=0).T
    gshift = jnp.sum(acc[1], axis=1, keepdims=True)
    ggain = (jnp.sum(acc[0], axis=1, keepdims=True) - base[:, 17:18] * gshift) / base[:, 16:17]
    lane = lax.broadcasted_iota(jnp.int32, (D, VEC), 1)
    gvt[...] = jnp.where(lane == 0, ggain, jnp.where(lane == 1, gshift, base)).astype(bf16)
    emit(me, gvt, send, keep, cols=slice(3 * D, 3 * D + VEC))


def weight_grad(me, nd, normed_t, vec, gvec, sums, turns, grads, w):
    half = (nd // 2, D // nd, 3 * D + VEC)
    return pl.pallas_call(
        functools.partial(weight_grad_kernel, nd),
        grid=(1,),
        in_specs=[SMEM, whole((D, WIN)), whole((16, D)), whole((8, D))]
        + [whole((1, 2 * D))] * 2
        + [whole(turns.shape)]
        + [whole((GR, WIN))] * (3 * GROUPS)
        + [ANY] * nd,
        out_specs=[whole(half)] * 2,
        out_shape=[jax.ShapeDtypeStruct(half, bf16)] * 2,
        scratch_shapes=[
            pltpu.VMEM((D, 3 * D + VEC), bf16),
            pltpu.VMEM((D, GR), bf16),
            pltpu.VMEM((D, VEC), bf16),
            pltpu.VMEM((2, D, 128), f32),
            pltpu.SemaphoreType.DMA((nd,)),
        ],
        compiler_params=room(30),
        cost_estimate=pl.CostEstimate(flops=2 * WIN * D * 3 * D, bytes_accessed=10 << 20, transcendentals=0),
        name="weight_grad",
    )(me, normed_t, vec, gvec, *sums, turns, *grads, *w)


def project_back_kernel(nd, me_ref, x_ref, gm_ref, vec_ref, *rest):
    grads, rest = rest[: 3 * GROUPS], rest[3 * GROUPS :]
    gt_ref, full, sems = rest[nd:]
    for copy in load_blocks(me_ref[0], rest[:nd], full, sems, 0):
        copy.wait()

    @pl.loop(0, WIN // BLOCK)
    def _(t):
        rows = pl.ds(pl.multiple_of(t * BLOCK, BLOCK), BLOCK)
        total = dot(full[:, :GR], grads[0][:, rows])
        for i in range(1, 3 * GROUPS):
            total += dot(full[:, i * GR : (i + 1) * GR], grads[i][:, rows])
        h, rstd = norm_parts(x_ref[rows, :].astype(f32))
        gt_ref[rows, :] = gm_ref[rows, :] + norm_back(total.T, vec_ref[0:1, :], h, rstd)


def project_back(me, tokens, grad_middle, vec, grads, w):
    nd = len(w)
    return pl.pallas_call(
        functools.partial(project_back_kernel, nd),
        grid=(1,),
        in_specs=[SMEM, whole((WIN, D)), whole((WIN, D)), whole((16, D))]
        + [whole((GR, WIN))] * (3 * GROUPS)
        + [ANY] * nd,
        out_specs=whole((WIN, D)),
        out_shape=jax.ShapeDtypeStruct((WIN, D), f32),
        scratch_shapes=[pltpu.VMEM((D, w[0].shape[1]), bf16), pltpu.SemaphoreType.DMA((nd,))],
        compiler_params=room(58),
        cost_estimate=pl.CostEstimate(flops=2 * WIN * D * 3 * D, bytes_accessed=20 << 20, transcendentals=0),
        name="project_back",
    )(me, tokens, grad_middle, vec, *grads, *w)


def body(nd, nf, tokens, segment_ids, cotangent, projector, combiner, attend_bias, expander,
         expand_bias, reducer, reduce_bias, first_gain, first_shift, second_gain, second_shift):
    r, q = projector.shape[0], reducer.shape[0] // 2
    count = nd * nf
    me = lax.axis_index("dp").astype(jnp.int32).reshape(1)
    picks = half_columns(q)
    turns = half_columns(r)
    vectors = (first_gain, first_shift, attend_bias, second_gain, second_shift, reduce_bias, expand_bias)
    tie = lax.optimization_barrier

    shard_w, shard_1, shard_2 = pack(projector, expander, reducer, combiner, picks, vectors)
    parts_w, parts_1 = shifts(shard_w, nf), shifts(shard_1, nf)
    scaled_t, cotangent_t = prepare(after(tokens, shard_w), cotangent)
    parts_w, scaled_t, cotangent_t = tie((parts_w, scaled_t, cotangent_t))
    (zw,) = line_up(nf, [(0, r, 0, 0, 0)], [(nf * r, 3 * D + VEC)], parts_w)
    w = spread_plane(zw, nd)
    moves = [(0, r, 0, 0, 0), (r, r, 0, nf * r, 0), (2 * r, q, 0, 2 * nf * r, 0)]
    extra = [(2 * r + q, r, 0, nf * (2 * r + q), 0)]
    (z1,) = line_up(nf, moves + extra, [(nf * (3 * r + q), D)], after(parts_1, zw))
    w, z1 = tie((w, z1))
    w = spread_cores(w, nd)
    scaled_t, z1 = tie((scaled_t, z1))
    f1 = spread_plane(z1, nd)
    project_t, normed_t, vecs, bias = project(me, scaled_t, turns, w)
    parts_2 = shifts(after(shard_2, project_t), nf)
    attended, sums = [], []
    for g in range(GROUPS):
        if g == GROUPS - 1:
            f1, parts_2, project_t, _ = tie((f1, parts_2, project_t, attended))
            (z2,) = line_up(nf, moves, [(nf * (2 * r + q), D)], parts_2)
            z2, project_t = tie((z2, project_t))
            f2 = spread_plane(z2, nd)
            f1 = spread_cores(f1, nd)
        a, l = attend(g, project_t, segment_ids)
        attended.append(a)
        sums.append(l)
    *state, s1, k1, gbe1 = ffn_first(me, tokens, attended, cotangent, cotangent_t, vecs, bias, f1, nd)
    s1, k1, f2 = tie((s1, k1, f2))
    got, f2 = tie((flip(s1, 1, nd), f2))
    f2 = spread_cores(f2, nd)
    t1 = [add(k1[m], got[m]) for m in range(nd // 2)]
    t1, cotangent = tie((t1, cotangent))
    m1 = meet_plane(t1, nd)
    out, grad_middle, grad_t, s2, k2, gbe2, gvec = ffn_last(
        me, attended, cotangent, cotangent_t, vecs, bias, f2, f1, state, nd
    )

    cuts = [(0, r, 0), (nf * r, r, r), (2 * nf * r, q, 2 * r)]
    more = [(nf * (2 * r + q), r, 2 * r + q)]
    m1, s2, k2, grad_t = tie((m1, s2, k2, grad_t))
    p1 = pieces(nf, cuts, m1)
    p1, grad_t = tie((p1, grad_t))
    got = flip(s2, 1, nd)
    p1 = [shift(p, k, nf) if k else p for k, p in enumerate(p1)]
    grads = [attend_back(0, project_t, attended[0], grad_t, sums[0], segment_ids)]
    got, k2, grads, grad_t = tie((got, k2, grads, grad_t))
    t2 = [add(k2[m], got[m]) for m in range(nd // 2)]
    t2, grad_t = tie((t2, grad_t))
    m2 = meet_plane(t2, nd)
    for g in range(1, GROUPS):
        grads.append(attend_back(g, project_t, attended[g], grad_t, sums[g], segment_ids))
    m2, p1, grads = tie((m2, p1, grads))
    p2 = pieces(nf, cuts + more, m2)
    p2, grads = tie((p2, grads))
    p2 = [shift(p, k, nf) if k else p for k, p in enumerate(p2)]
    grads = [grads[g][j] for j in range(3) for g in range(GROUPS)]
    send, keep = weight_grad(me, nd, normed_t, vecs, gvec, (gbe1, gbe2), turns, grads, w)
    totals = sum_cores(send, keep, nd)
    grads, totals = tie((grads, totals))
    met = meet_plane(totals, nd)
    grad_tokens = project_back(me, tokens, grad_middle, vecs, grads, w)
    grad_tokens, met, p2 = tie((grad_tokens, met, p2))
    gw = sum(v.astype(f32) for v in met).astype(bf16)
    grad_expander, grad_reducer, grad_combiner = finish(r, q, picks, p1, p2)
    last = scatter_z(gw, [r], nf)
    grad_projector, small = last[:, : 3 * D], last[:, 3 * D :]
    return (
        out,
        grad_tokens,
        grad_projector,
        grad_combiner,
        small[:, 2],
        grad_expander,
        small[:, 6:10].T.reshape(-1),
        grad_reducer,
        small[:, 5],
        small[:, 0],
        small[:, 1],
        small[:, 3],
        small[:, 4],
    )


def solution(mesh):
    rows, flat = P(("dp", "fsdp"), None), P(("dp", "fsdp"))
    return jax.shard_map(
        functools.partial(body, mesh.shape["dp"], mesh.shape["fsdp"]),
        mesh=mesh,
        in_specs=(rows, rows, rows, rows, rows, flat, rows, flat, rows, flat, flat, flat, flat, flat),
        out_specs=(rows, rows, rows, rows, flat, rows, flat, rows, flat, flat, flat, flat, flat),
        check_vma=False,
    )
```

```python
import functools
import math

import jax
import jax.numpy as jnp
import numpy as np
from jax import lax
from jax.experimental import pallas as pl
from jax.experimental.pallas import tpu as pltpu
from jax.sharding import PartitionSpec as P

D = 768
HD = 32
HEADS = 24
WIN = 1024
BLOCK = 256
EPS = 1e-05
LOG2E = math.log2(math.e)
BIG = float(2**30)
VEC = 128
f32 = jnp.float32
bf16 = jnp.bfloat16
NN = (((1,), (0,)), ((), ()))
NT = (((1,), (1,)), ((), ()))
ANY = pl.BlockSpec(memory_space=pl.ANY)
SMEM = pl.BlockSpec(memory_space=pltpu.SMEM)


def room(mib):
    return pltpu.CompilerParams(vmem_limit_bytes=mib << 20)


def dot(a, b, dims=NN):
    return lax.dot_general(a, b, dims, preferred_element_type=f32)


def whole(shape):
    return pl.BlockSpec(shape, lambda *_: (0,) * len(shape), pipeline_mode=pl.Buffered(1))


def flip(value, bit, count):
    return lax.ppermute(value, "dp", [(i, i ^ bit) for i in range(count)])


def shift(value, step, count):
    return lax.ppermute(value, "fsdp", [(i, (i + step) % count) for i in range(count)])


def after(value, *others):
    return lax.optimization_barrier((value, others))[0]


def shifts(shard, nf):
    return [shard] + [shift(shard, k, nf) for k in range(1, nf)]


def line_up_kernel(nf, moves, me_ref, *refs):
    me = me_ref[0]
    parts, outs = refs[:nf], refs[nf:]
    for k in range(nf):
        for j in range(nf):
            @pl.when(lax.rem(me - k + nf, nf) == j)
            def _():
                for source, rows, out, row, col in moves:
                    value = parts[k][source : source + rows, :]
                    at = row + j * rows
                    outs[out][at : at + rows, col : col + value.shape[1]] = value


def line_up(nf, moves, shapes, parts):
    return pl.pallas_call(
        functools.partial(line_up_kernel, nf, moves),
        in_specs=[SMEM] + [whole(p.shape) for p in parts],
        out_specs=[whole(x) for x in shapes],
        out_shape=[jax.ShapeDtypeStruct(x, bf16) for x in shapes],
        grid=(1,),
        compiler_params=room(10),
        cost_estimate=pl.CostEstimate(flops=0, bytes_accessed=4 << 20, transcendentals=0),
        name="line_up",
    )(lax.axis_index("fsdp").astype(jnp.int32).reshape(1), *parts)


def add(a, b):
    return (a.astype(f32) + b.astype(f32)).astype(bf16)


def spread_plane(block, nd):
    return {m: flip(block, m, nd) if m else block for m in range(0, nd, 2)}


def spread_cores(blocks, nd):
    both = {**blocks, **{m ^ 1: flip(v, 1, nd) for m, v in blocks.items()}}
    return [both[m] for m in range(nd)]


def sum_cores(send, keep, nd):
    got = flip(send, 1, nd)
    return [add(keep[m], got[m]) for m in range(nd // 2)]


def meet_plane(totals, nd):
    return [flip(v, 2 * m, nd) if m else v for m, v in enumerate(totals)]


def scatter_z(block, rows, nf):
    me = lax.axis_index("fsdp")

    def piece(z):
        got, at = [], 0
        for r in rows:
            got.append(lax.dynamic_slice_in_dim(block, at + z * r, r, 0))
            at += nf * r
        return got[0] if len(got) == 1 else jnp.concatenate(got, axis=0)

    total = piece(me).astype(f32)
    for k in range(1, nf):
        total = total + shift(piece(lax.rem(me + k, nf)), k, nf).astype(f32)
    return total


def half_columns(q):
    o = np.arange(D // 2)
    source = (o // q) * (2 * q) + o % q
    picks = np.arange(D)[None, :, None] == (source[None, None, :] + q * np.arange(2)[:, None, None])
    return jnp.asarray(picks, bf16)


def pack_kernel(proj_ref, exp_ref, red_ref, comb_ref, pick_ref, *refs):
    vec_refs, (w_ref, f1_ref, f2_ref) = refs[:-3], refs[-3:]
    r, q = proj_ref.shape[0], red_ref.shape[0] // 2
    w_ref[:, : 3 * D] = proj_ref[...]
    row = [ref[...].astype(f32).reshape(1, -1) for ref in vec_refs]
    rows = row[:6] + [row[6][:, j * r : (j + 1) * r] for j in range(4)]
    rows.append(jnp.zeros((VEC - 10, r), f32))
    w_ref[:, 3 * D :] = jnp.concatenate(rows, axis=0).T.astype(bf16)
    for h, ref in enumerate((f1_ref, f2_ref)):
        for c in range(4):
            at, col = (c // 2) * r, (c % 2) * (D // 2)
            ref[at : at + r, col : col + D // 2] = dot(
                exp_ref[:, c * D : (c + 1) * D], pick_ref[h]
            ).astype(bf16)
        ref[2 * r : 2 * r + q, :] = red_ref[h * q : (h + 1) * q, :]
    f1_ref[2 * r + q :, :] = comb_ref[...]


def pack(projector, expander, reducer, combiner, picks, vectors):
    r, q = projector.shape[0], reducer.shape[0] // 2
    shapes = [(r, 3 * D + VEC), (3 * r + q, D), (2 * r + q, D)]
    arrays = (projector, expander, reducer, combiner, picks, *vectors)
    return pl.pallas_call(
        pack_kernel,
        grid=(1,),
        in_specs=[whole(a.shape) for a in arrays],
        out_specs=[whole(x) for x in shapes],
        out_shape=[jax.ShapeDtypeStruct(x, bf16) for x in shapes],
        compiler_params=room(58),
        cost_estimate=pl.CostEstimate(flops=0, bytes_accessed=3 << 20, transcendentals=0),
        name="pack",
    )(*arrays)


def pieces_kernel(nf, moves, me_ref, *refs):
    terms, outs = refs[:-nf], refs[-nf:]
    me = me_ref[0]
    for row, rows, at in moves:
        for j in range(nf):
            here = slice(row + j * rows, row + (j + 1) * rows)
            value = sum(t[here, :].astype(f32) for t in terms).astype(bf16)
            for k in range(nf):
                @pl.when(lax.rem(me + k, nf) == j)
                def _():
                    outs[k][at : at + rows, :] = value


def pieces(nf, moves, terms):
    rows = sum(m[1] for m in moves)
    return pl.pallas_call(
        functools.partial(pieces_kernel, nf, moves),
        in_specs=[SMEM] + [whole(x.shape) for x in terms],
        out_specs=[whole((rows, D))] * nf,
        out_shape=[jax.ShapeDtypeStruct((rows, D), bf16)] * nf,
        grid=(1,),
        compiler_params=room(12),
        cost_estimate=pl.CostEstimate(flops=0, bytes_accessed=6 << 20, transcendentals=0),
        name="pieces",
    )(lax.axis_index("fsdp").astype(jnp.int32).reshape(1), *terms)


def finish_kernel(r, q, nf, pick_ref, *refs):
    halves, (ge_ref, gr_ref, gc_ref) = (refs[:nf], refs[nf : 2 * nf]), refs[2 * nf :]
    for c in range(4):
        total = jnp.zeros((r, D), f32)
        for h in range(2):
            at, col = (c // 2) * r, (c % 2) * (D // 2)
            for p in halves[h]:
                total += dot(p[at : at + r, col : col + D // 2], pick_ref[h], NT)
        ge_ref[:, c * D : (c + 1) * D] = total
    for h in range(2):
        gr_ref[h * q : (h + 1) * q, :] = sum(p[2 * r : 2 * r + q, :].astype(f32) for p in halves[h])
    gc_ref[...] = sum(p[2 * r + q :, :].astype(f32) for p in halves[1])


def finish(r, q, picks, first, second):
    shapes = [(r, 4 * D), (2 * q, D), (r, D)]
    arrays = (picks, *first, *second)
    return pl.pallas_call(
        functools.partial(finish_kernel, r, q, len(first)),
        grid=(1,),
        in_specs=[whole(x.shape) for x in arrays],
        out_specs=[whole(x) for x in shapes],
        out_shape=[jax.ShapeDtypeStruct(x, f32) for x in shapes],
        compiler_params=room(12),
        cost_estimate=pl.CostEstimate(flops=0, bytes_accessed=3 << 20, transcendentals=0),
        name="finish",
    )(*arrays)


def load_blocks(me, refs, target, sems, base, row=0, rows=None, col=0):
    rows = rows or refs[0].shape[0]
    width = refs[0].shape[1]
    copies = []
    for m, ref in enumerate(refs):
        at = pl.multiple_of((me ^ m) * rows, 16)
        copy = pltpu.make_async_copy(
            ref.at[pl.ds(row, rows), :], target.at[pl.ds(at, rows), pl.ds(col, width)], sems.at[base + m]
        )
        copy.start()
        copies.append(copy)
    return copies


def norm_parts(v):
    c = v - jnp.mean(v, axis=-1, keepdims=True)
    rstd = lax.rsqrt(jnp.mean(c * c, axis=-1, keepdims=True) + EPS)
    return c * rstd, rstd


def norm_back(grad, gain, h, rstd):
    e = grad * gain
    return (e - jnp.mean(e, -1, keepdims=True) - h * jnp.mean(e * h, -1, keepdims=True)) * rstd


def prepare_kernel(x_ref, cot_ref, ht_ref, ct_ref):
    @pl.loop(0, WIN // BLOCK)
    def _(t):
        rows = pl.ds(pl.multiple_of(t * BLOCK, BLOCK), BLOCK)
        h, _ = norm_parts(x_ref[rows, :].astype(f32))
        ht_ref[:, rows] = h.T
        ct_ref[:, rows] = cot_ref[rows, :].T


def prepare(tokens, cotangent):
    return pl.pallas_call(
        prepare_kernel,
        grid=(1,),
        in_specs=[whole((WIN, D))] * 2,
        out_specs=[whole((D, WIN))] * 2,
        out_shape=[jax.ShapeDtypeStruct((D, WIN), f32), jax.ShapeDtypeStruct((D, WIN), bf16)],
        compiler_params=room(20),
        cost_estimate=pl.CostEstimate(flops=5_000_000_000, bytes_accessed=8 << 20, transcendentals=0),
        name="prepare",
    )(tokens, cotangent)


def project_kernel(nd, me_ref, ht_ref, turn_ref, *rest):
    w = rest[:nd]
    pt_ref, nt_ref, vec_ref, bias_ref, full, sems = rest[nd:]
    for copy in load_blocks(me_ref[0], w, full, sems, 0):
        copy.wait()
    columns = full[:, 3 * D :].astype(f32)
    vec = columns.T
    vec_ref[...] = vec[:16]
    low = vec[:16].astype(bf16)
    for i in range(4):
        c, row = i % 2, 6 + 2 * (i // 2)
        parts = [dot(low[:, c * (D // 2) : (c + 1) * (D // 2)], turn_ref[k], NT) for k in range(2)]
        bias_ref[:, i * D : (i + 1) * D] = parts[0][row : row + 1] + parts[1][row + 1 : row + 2]
    nt_ref[...] = (ht_ref[...] * columns[:, 0:1] + columns[:, 1:2]).astype(bf16)

    for c in range(0, 3 * D, BLOCK):
        cols = slice(c, c + BLOCK)
        pt_ref[cols, :] = dot(full[:, cols].T, nt_ref[...]).astype(bf16)


def project(me, normed_t, turns, w):
    nd = len(w)
    return pl.pallas_call(
        functools.partial(project_kernel, nd),
        in_specs=[SMEM, whole((D, WIN)), whole(turns.shape)] + [ANY] * nd,
        out_specs=[whole((3 * D, WIN)), whole((D, WIN)), whole((16, D)), whole((1, 4 * D))],
        out_shape=[
            jax.ShapeDtypeStruct((3 * D, WIN), bf16),
            jax.ShapeDtypeStruct((D, WIN), bf16),
            jax.ShapeDtypeStruct((16, D), f32),
            jax.ShapeDtypeStruct((1, 4 * D), f32),
        ],
        scratch_shapes=[pltpu.VMEM((D, w[0].shape[1]), bf16), pltpu.SemaphoreType.DMA((nd,))],
        grid=(1,),
        compiler_params=room(26),
        cost_estimate=pl.CostEstimate(flops=2 * WIN * D * 3 * D, bytes_accessed=12 << 20, transcendentals=0),
        name="project",
    )(me, normed_t, turns, *w)


GH = 8
SH = 8
GR = GH * HD


def causal_penalty():
    ik = lax.broadcasted_iota(jnp.int32, (BLOCK, BLOCK), 0)
    iq = lax.broadcasted_iota(jnp.int32, (BLOCK, BLOCK), 1)
    return jnp.where(iq >= ik, 0.0, -BIG)


def split_scaled(q):
    scaled = q.astype(f32) * (HD**-0.5 * LOG2E)
    high = scaled.astype(bf16)
    return high, (scaled - high.astype(f32)).astype(bf16)


def episode_rows(seg):
    hot = lax.broadcasted_iota(jnp.int32, (8, WIN), 0) == seg
    return hot.astype(f32), jnp.where(hot, 0.0, -BIG)


def attend_kernel(q_ref, k_ref, v_ref, seg_ref, out_ref, lse_ref, qa, ka, va, cm):
    @pl.when(pl.program_id(0) == 0)
    def _():
        cm[...] = causal_penalty()

    hot, pen = episode_rows(seg_ref[...])
    pad = jnp.zeros((56, WIN), f32)
    tail_q = jnp.concatenate([hot, pad], axis=0).astype(bf16)
    tail_k = jnp.concatenate([pen, pad], axis=0).astype(bf16)
    ones = jnp.ones((16, WIN), bf16)
    for h in range(GH):
        rows = slice(h * HD, (h + 1) * HD)
        high, low = split_scaled(q_ref[rows, :])
        k = k_ref[rows, :]
        qa[h] = jnp.concatenate([high, low, tail_q], axis=0)
        ka[h] = jnp.concatenate([k, k, tail_k], axis=0).T
        va[h] = jnp.concatenate([v_ref[rows, :], ones], axis=0)
    c = cm[...]
    for qb in range(WIN // BLOCK):
        k0, k1 = max(0, qb - 2) * BLOCK, (qb + 1) * BLOCK
        qs = slice(qb * BLOCK, k1)
        for hb in range(0, GH, SH):
            heads = range(hb, hb + SH)
            s = [dot(ka[h, k0:k1, :], qa[h, :, qs]) for h in heads]
            w = k1 - k0 - BLOCK
            s = [jnp.concatenate([x[:w], x[w:] + c], axis=0) if w else x + c for x in s]
            top = [jnp.max(x, axis=0, keepdims=True) for x in s]
            p = [jnp.exp2(x - y) for x, y in zip(s, top)]
            o = [dot(va[h, :, k0:k1], y.astype(bf16)) for h, y in zip(heads, p)]
            for i, h in enumerate(heads):
                total = o[i][HD : HD + 1]
                out_ref[h * HD : (h + 1) * HD, qs] = (o[i][:HD] * (1.0 / total)).astype(bf16)
                lse_ref[h, :, qs] = top[i] + jnp.log2(total)


GROUPS = HEADS // GH


def head_rows(index):
    return pl.BlockSpec((GR, WIN), lambda i: (index, 0))


def head_sums(index):
    return pl.BlockSpec((GH, 1, WIN), lambda i: (index, 0, 0))


def attend(group, project_t, seg):
    return pl.pallas_call(
        attend_kernel,
        grid=(1,),
        in_specs=[head_rows(group + j * GROUPS) for j in range(3)] + [whole((1, WIN))],
        out_specs=[head_rows(0), head_sums(0)],
        out_shape=[
            jax.ShapeDtypeStruct((GR, WIN), bf16),
            jax.ShapeDtypeStruct((GH, 1, WIN), f32),
        ],
        scratch_shapes=[
            pltpu.VMEM((GH, 128, WIN), bf16),
            pltpu.VMEM((GH, WIN, 128), bf16),
            pltpu.VMEM((GH, HD + 16, WIN), bf16),
            pltpu.VMEM((BLOCK, BLOCK), f32),
        ],
        compiler_params=room(24),
        cost_estimate=pl.CostEstimate(flops=7_000_000_000, bytes_accessed=3 << 20, transcendentals=0),
        name="attend",
    )(project_t, project_t, project_t, seg)


def attend_back_kernel(
    q_ref, k_ref, v_ref, o_ref, do_ref, lse_ref, seg_ref, dq_ref, dk_ref, dv_ref, qa, ka, va, da, aq, cm
):
    hot, pen = episode_rows(seg_ref[...])
    ids = lax.broadcasted_iota(jnp.int32, (8, WIN), 0)
    ones3 = jnp.where(ids < 3, 1.0, 0.0)
    z48 = jnp.zeros((48, WIN), f32)
    z88 = jnp.zeros((88, WIN), f32)

    def rows3(v):
        a = v.astype(bf16).astype(f32)
        b = (v - a).astype(bf16).astype(f32)
        return jnp.where(ids == 0, a, jnp.where(ids == 1, b, jnp.where(ids == 2, v - a - b, 0.0)))

    tail_k = jnp.concatenate([pen, ones3, z48], axis=0).astype(bf16)
    tail_v = jnp.concatenate([ones3, z88], axis=0).astype(bf16)
    for h in range(GH):
        rows = slice(h * HD, (h + 1) * HD)
        high, low = split_scaled(q_ref[rows, :])
        k, v, g = k_ref[rows, :], v_ref[rows, :], do_ref[rows, :]
        delta = jnp.sum(g.astype(f32) * o_ref[rows, :].astype(f32), axis=0, keepdims=True)
        tail_q = jnp.concatenate([hot, rows3(-lse_ref[h]), z48], axis=0).astype(bf16)
        tail_g = jnp.concatenate([rows3(-delta), z88], axis=0).astype(bf16)
        qa[h] = jnp.concatenate([high, low, tail_q], axis=0).T
        ka[h] = jnp.concatenate([k, k, tail_k], axis=0)
        va[h] = jnp.concatenate([v, tail_v], axis=0)
        da[h] = jnp.concatenate([g, tail_g], axis=0).T
    ik = lax.broadcasted_iota(jnp.int32, (BLOCK, BLOCK), 1)
    iq = lax.broadcasted_iota(jnp.int32, (BLOCK, BLOCK), 0)
    cm[...] = jnp.where(iq >= ik, 0.0, -BIG)
    c = cm[...]
    scale = HD**-0.5
    step = 4
    nb = WIN // BLOCK
    for kb in range(nb):
        q0, q1 = kb * BLOCK, min(nb, kb + 3) * BLOCK
        ks = slice(q0, q0 + BLOCK)
        for hb in range(0, GH, step):
            heads = range(hb, hb + step)
            rows = [slice(h * HD, (h + 1) * HD) for h in heads]
            s = [dot(qa[h, q0:q1, :], ka[h, :, ks]) for h in heads]
            dp = [dot(da[h, q0:q1, :], va[h, :, ks]) for h in heads]
            s = [
                jnp.concatenate([x[:BLOCK] + c, x[BLOCK:]], axis=0) if q1 - q0 > BLOCK else x + c
                for x in s
            ]
            p = [jnp.exp2(x) for x in s]
            ds = [(x * y).astype(bf16) for x, y in zip(p, dp)]
            pb = [x.astype(bf16) for x in p]
            dv = [dot(do_ref[x, q0:q1], y) for x, y in zip(rows, pb)]
            dk = [dot(q_ref[x, q0:q1], y) for x, y in zip(rows, ds)]
            dq = [dot(k_ref[x, ks], y, NT) for x, y in zip(rows, ds)]
            for i in range(step):
                dv_ref[rows[i], ks] = dv[i].astype(bf16)
                dk_ref[rows[i], ks] = (dk[i] * scale).astype(bf16)
                done = min(nb, kb + 2) * BLOCK if kb else 0
                if done > q0:
                    aq[rows[i], q0:done] += dq[i][:, : done - q0]
                if q1 > max(done, q0):
                    at = max(done, q0)
                    aq[rows[i], at:q1] = dq[i][:, at - q0 :]
    dq_ref[...] = (aq[...] * scale).astype(bf16)


def attend_back(group, project_t, attended_t, grad_t, lse, seg):
    return pl.pallas_call(
        attend_back_kernel,
        grid=(1,),
        in_specs=[head_rows(group + j * GROUPS) for j in range(3)]
        + [head_rows(0), head_rows(group), head_sums(0), whole((1, WIN))],
        out_specs=[head_rows(0)] * 3,
        out_shape=[jax.ShapeDtypeStruct((GR, WIN), bf16)] * 3,
        scratch_shapes=[
            pltpu.VMEM((GH, WIN, 128), bf16),
            pltpu.VMEM((GH, 128, WIN), bf16),
            pltpu.VMEM((GH, 128, WIN), bf16),
            pltpu.VMEM((GH, WIN, 128), bf16),
            pltpu.VMEM((GR, WIN), f32),
            pltpu.VMEM((BLOCK, BLOCK), f32),
        ],
        compiler_params=room(32),
        cost_estimate=pl.CostEstimate(flops=14_000_000_000, bytes_accessed=5 << 20, transcendentals=0),
        name="attend_back",
    )(project_t, project_t, project_t, attended_t, grad_t, lse, seg)


def gelu_both(u):
    a, b = math.sqrt(2 / math.pi), 0.044715
    sq = u * u
    t = jnp.tanh(u * (a + (a * b) * sq))
    half = 0.5 + 0.5 * t
    slope = half + (0.5 * u) * (1.0 - t * t) * (a + (3 * a * b) * sq)
    return u * half, slope


TB = 512


def token_loop(step):
    @pl.loop(0, WIN // TB)
    def _(t):
        step(pl.ds(pl.multiple_of(t * TB, TB), TB))


def load_weights(me, nd, blocks, exp, red, sems):
    rb, rr = D // nd, red.shape[0] // nd
    copies = load_blocks(me, blocks, exp, sems, nd, 0, rb, 0)
    copies += load_blocks(me, blocks, exp, sems, 2 * nd, rb, rb, D)
    return copies + load_blocks(me, blocks, red, sems, 3 * nd, 2 * rb, rr, 0)


def ffn_chunk(i, me, nd, cot_ref, be_ref, exp, red, n2, n2t, cott, oacc, nacc, ascr, gscr, tmp, gbe_ref, send, keep):
    rb, rr, chunk = D // nd, red.shape[0] // nd, tmp.shape[1]
    cols = pl.ds(pl.multiple_of(i * chunk, 128), chunk)
    gbe_ref[...] = jnp.zeros((1, chunk), f32)

    def step(rows):
        u = dot(n2[rows, :], exp[:, cols]) + be_ref[...]
        ga = dot(cot_ref[rows, :], red[cols, :], NT)
        act, slope = gelu_both(u)
        act = act.astype(bf16)
        gu = (ga * slope).astype(bf16)
        ascr[rows, :] = act
        gscr[rows, :] = gu
        gbe_ref[...] += jnp.sum(gu.astype(f32), axis=0, keepdims=True)
        oacc[rows, :] += dot(act, red[cols, :])
        nacc[rows, :] += dot(gu, exp[:, cols], NT)

    token_loop(step)
    tmp[...] = dot(n2t[...], gscr[...]).astype(bf16)
    emit(me, tmp, send, keep, pl.ds(pl.multiple_of(i * rb, 16), rb))
    tmp[...] = dot(cott[...], ascr[...]).astype(bf16).T
    per = chunk // rr
    for b in range(per):
        mask = me ^ (i * per + b)
        for odd, ref in ((1, send), (0, keep)):
            @pl.when((mask & 1) == odd)
            def _():
                ref[mask >> 1, 2 * rb : 2 * rb + rr, :] = tmp[b * rr : (b + 1) * rr, :]


def ffn_first_kernel(nd, me_ref, x_ref, cot_ref, cott, vec_ref, be_ref, *rest):
    att, blocks, rest = rest[:GROUPS], rest[GROUPS : GROUPS + nd], rest[GROUPS + nd :]
    mid_ref, n2_ref, part_ref, nacc_ref, send, keep, gbe_ref = rest[:7]
    comb, exp, red, mid, n2, n2t, oacc, nacc, ascr, gscr, tmp, sems = rest[7:]
    i = pl.program_id(0)
    me = me_ref[0]
    rb, rr = D // nd, red.shape[0] // nd
    outs = [
        pltpu.make_async_copy(a, b, sems.at[4 * nd + j])
        for j, (a, b) in enumerate(((mid, mid_ref), (n2, n2_ref), (oacc, part_ref), (nacc, nacc_ref)))
    ]

    @pl.when(i == 0)
    def _():
        got = load_blocks(me, blocks, comb, sems, 0, 2 * rb + rr, rb, 0)
        late = load_weights(me, nd, blocks, exp, red, sems)
        for copy in got:
            copy.wait()

        def step(rows):
            m = x_ref[rows, :].astype(f32) + vec_ref[2:3, :]
            for g in range(GROUPS):
                m += dot(att[g][:, rows].T, comb[g * GR : (g + 1) * GR, :])
            mid[rows, :] = m
            oacc[rows, :] = m + vec_ref[5:6, :]
            h, _ = norm_parts(m)
            n = (h * vec_ref[3:4, :] + vec_ref[4:5, :]).astype(bf16)
            n2[rows, :] = n
            n2t[:, rows] = n.T

        token_loop(step)
        nacc[...] = jnp.zeros_like(nacc)
        outs[0].start()
        outs[1].start()
        for copy in late:
            copy.wait()

    ffn_chunk(i, me, nd, cot_ref, be_ref, exp, red, n2, n2t, cott, oacc, nacc, ascr, gscr, tmp, gbe_ref, send, keep)

    @pl.when(i == pl.num_programs(0) - 1)
    def _():
        outs[2].start()
        outs[3].start()
        for copy in outs:
            copy.wait()


def ffn_last_kernel(nd, me_ref, cot_ref, cott, vec_ref, be_ref, *rest):
    att, blocks, rest = rest[:GROUPS], rest[GROUPS : GROUPS + nd], rest[GROUPS + nd :]
    others, rest = rest[:nd], rest[nd:]
    mid_ref, n2_ref, part_ref, naccin_ref = rest[:4]
    out_ref, gm_ref, dt_ref, send, keep, gbe_ref, gv_ref = rest[4:11]
    comb, exp, red, mid, part, nin, n2, n2t, oacc, nacc, ascr, gscr, tmp, sems = rest[11:]
    i = pl.program_id(0)
    me = me_ref[0]
    rb, rr = D // nd, red.shape[0] // nd
    ins = [
        pltpu.make_async_copy(a, b, sems.at[4 * nd + j])
        for j, (a, b) in enumerate(((n2_ref, n2), (mid_ref, mid), (part_ref, part), (naccin_ref, nin)))
    ]

    @pl.when(i == 0)
    def _():
        ins[0].start()
        got = load_weights(me, nd, blocks, exp, red, sems)
        got += load_blocks(me, others, comb, sems, 0, 2 * rb + rr, rb, 0)
        for copy in ins[1:]:
            copy.start()
        oacc[...] = jnp.zeros_like(oacc)
        nacc[...] = jnp.zeros_like(nacc)
        ins[0].wait()
        n2t[...] = n2[...].T
        for copy in got:
            copy.wait()

    ffn_chunk(i, me, nd, cot_ref, be_ref, exp, red, n2, n2t, cott, oacc, nacc, ascr, gscr, tmp, gbe_ref, send, keep)

    @pl.when(i == pl.num_programs(0) - 1)
    def _():
        for copy in ins[1:]:
            copy.wait()
        gv_ref[...] = jnp.zeros((8, D), f32)

        def step(rows):
            out_ref[rows, :] = (part[rows, :] + oacc[rows, :]).astype(bf16)
            h, rstd = norm_parts(mid[rows, :])
            g = nacc[rows, :] + nin[rows, :]
            cot = cot_ref[rows, :].astype(f32)
            gm = cot + norm_back(g, vec_ref[3:4, :], h, rstd)
            gm_ref[rows, :] = gm
            low = gm.astype(bf16)
            n2[rows, :] = low
            n2t[:, rows] = low.T
            sums = (low.astype(f32), g * h, g, cot)
            gv_ref[2:6, :] += jnp.concatenate([jnp.sum(v, axis=0, keepdims=True) for v in sums], axis=0)

        token_loop(step)
        dt_ref[...] = dot(comb[...], n2t[...]).astype(bf16)
        for g in range(GROUPS):
            tmp[g * GR : (g + 1) * GR, :] = dot(att[g][...], n2[...]).astype(bf16)
        emit(me, tmp, send, keep, slice(2 * rb + rr, 3 * rb + rr))


def ffn_call(kernel, specs, arrays, nd, rows, out_shapes, last):
    ff = 2 * D
    shape = jax.ShapeDtypeStruct
    half = (nd // 2, rows, D)
    wide = pltpu.VMEM((WIN, D), f32)
    low, turned = pltpu.VMEM((WIN, D), bf16), pltpu.VMEM((D, WIN), bf16)
    return pl.pallas_call(
        functools.partial(kernel, nd),
        grid=(ff // D,),
        in_specs=specs,
        out_specs=[whole(x.shape) if last else ANY for x in out_shapes]
        + [whole(half), whole(half), pl.BlockSpec((1, D), lambda i: (0, i))]
        + ([whole((8, D))] if last else []),
        out_shape=list(out_shapes)
        + [shape(half, bf16), shape(half, bf16), shape((1, ff), f32)]
        + ([shape((8, D), f32)] if last else []),
        scratch_shapes=[pltpu.VMEM((D, D), bf16), pltpu.VMEM((D, ff), bf16), pltpu.VMEM((ff, D), bf16)]
        + [wide] * (3 if last else 1)
        + [low, turned, wide, wide, low, low, pltpu.VMEM((D, D), bf16)]
        + [pltpu.SemaphoreType.DMA((4 * nd + 4,))],
        compiler_params=room(52 if last else 36),
        cost_estimate=pl.CostEstimate(flops=12 * WIN * D * ff, bytes_accessed=20 << 20, transcendentals=0),
        name="ffn_last" if last else "ffn_first",
    )(*arrays)


def ffn_first(me, tokens, attended, cotangent, cotangent_t, vec, bias, blocks, nd):
    shape = jax.ShapeDtypeStruct
    outs = [shape((WIN, D), f32), shape((WIN, D), bf16), shape((WIN, D), f32), shape((WIN, D), f32)]
    specs = [SMEM, whole((WIN, D)), whole((WIN, D)), whole((D, WIN)), whole((16, D))]
    specs += [pl.BlockSpec((1, D), lambda i: (0, i))]
    specs += [whole((GR, WIN))] * GROUPS + [ANY] * nd
    arrays = (me, tokens, cotangent, cotangent_t, vec, bias, *attended, *blocks)
    return ffn_call(ffn_first_kernel, specs, arrays, nd, (4 * D) // nd, outs, False)


def ffn_last(me, attended, cotangent, cotangent_t, vec, bias, blocks, others, state, nd):
    shape = jax.ShapeDtypeStruct
    outs = [shape((WIN, D), bf16), shape((WIN, D), f32), shape((D, WIN), bf16)]
    specs = [SMEM, whole((WIN, D)), whole((D, WIN)), whole((16, D)), pl.BlockSpec((1, D), lambda i: (0, i + 2))]
    specs += [whole((GR, WIN))] * GROUPS + [ANY] * (2 * nd + 4)
    arrays = (me, cotangent, cotangent_t, vec, bias, *attended, *blocks, *others, *state)
    return ffn_call(ffn_last_kernel, specs, arrays, nd, (5 * D) // nd, outs, True)


def emit(me, source, send, keep, rows=slice(None), cols=slice(None)):
    steps = send.shape[0]
    rb = source.shape[0] // (2 * steps)
    for s in range(steps):
        far = pl.multiple_of((me ^ (2 * s + 1)) * rb, 16)
        near = pl.multiple_of((me ^ (2 * s)) * rb, 16)
        send[s, rows, cols] = source[pl.ds(far, rb), :]
        keep[s, rows, cols] = source[pl.ds(near, rb), :]


def weight_grad_kernel(nd, me_ref, nt_ref, vec_ref, gv_ref, b1_ref, b2_ref, turn_ref, *rest):
    grads, rest = rest[: 3 * GROUPS], rest[3 * GROUPS :]
    send, keep, full, tmp, gvt, acc, sems = rest[nd:]
    me = me_ref[0]
    copies = load_blocks(me, rest[:nd], full, sems, 0)
    acc[...] = jnp.zeros_like(acc)
    for i, ref in enumerate(grads):
        g = ref[...].T
        gw = dot(nt_ref[...], g)
        tmp[...] = gw.astype(bf16)
        emit(me, tmp, send, keep, cols=slice(i * GR, (i + 1) * GR))
        if i == 0:
            for copy in copies:
                copy.wait()
        w = full[:, i * GR : (i + 1) * GR].astype(f32)
        total = jnp.sum(g.astype(f32), axis=0, keepdims=True)
        for j, value in enumerate((w * gw, w * total)):
            acc[j] += value[:, :128] + value[:, 128:]
    rows = [gv_ref[:6, :]]
    for ref in (b1_ref, b2_ref):
        low = ref[...].astype(bf16)
        for k in range(2):
            rows.append(
                jnp.concatenate([dot(low[:, c * D : (c + 1) * D], turn_ref[k]) for c in range(2)], axis=1)
            )
    rows += [jnp.zeros((6, D), f32), vec_ref[:2, :], jnp.zeros((VEC - 18, D), f32)]
    base = jnp.concatenate(rows, axis=0).T
    gshift = jnp.sum(acc[1], axis=1, keepdims=True)
    ggain = (jnp.sum(acc[0], axis=1, keepdims=True) - base[:, 17:18] * gshift) / base[:, 16:17]
    lane = lax.broadcasted_iota(jnp.int32, (D, VEC), 1)
    gvt[...] = jnp.where(lane == 0, ggain, jnp.where(lane == 1, gshift, base)).astype(bf16)
    emit(me, gvt, send, keep, cols=slice(3 * D, 3 * D + VEC))


def weight_grad(me, nd, normed_t, vec, gvec, sums, turns, grads, w):
    half = (nd // 2, D // nd, 3 * D + VEC)
    return pl.pallas_call(
        functools.partial(weight_grad_kernel, nd),
        grid=(1,),
        in_specs=[SMEM, whole((D, WIN)), whole((16, D)), whole((8, D))]
        + [whole((1, 2 * D))] * 2
        + [whole(turns.shape)]
        + [whole((GR, WIN))] * (3 * GROUPS)
        + [ANY] * nd,
        out_specs=[whole(half)] * 2,
        out_shape=[jax.ShapeDtypeStruct(half, bf16)] * 2,
        scratch_shapes=[
            pltpu.VMEM((D, 3 * D + VEC), bf16),
            pltpu.VMEM((D, GR), bf16),
            pltpu.VMEM((D, VEC), bf16),
            pltpu.VMEM((2, D, 128), f32),
            pltpu.SemaphoreType.DMA((nd,)),
        ],
        compiler_params=room(30),
        cost_estimate=pl.CostEstimate(flops=2 * WIN * D * 3 * D, bytes_accessed=10 << 20, transcendentals=0),
        name="weight_grad",
    )(me, normed_t, vec, gvec, *sums, turns, *grads, *w)


def project_back_kernel(nd, me_ref, x_ref, gm_ref, vec_ref, *rest):
    grads, rest = rest[: 3 * GROUPS], rest[3 * GROUPS :]
    gt_ref, full, sems = rest[nd:]
    for copy in load_blocks(me_ref[0], rest[:nd], full, sems, 0):
        copy.wait()

    @pl.loop(0, WIN // BLOCK)
    def _(t):
        rows = pl.ds(pl.multiple_of(t * BLOCK, BLOCK), BLOCK)
        total = dot(full[:, :GR], grads[0][:, rows])
        for i in range(1, 3 * GROUPS):
            total += dot(full[:, i * GR : (i + 1) * GR], grads[i][:, rows])
        h, rstd = norm_parts(x_ref[rows, :].astype(f32))
        gt_ref[rows, :] = gm_ref[rows, :] + norm_back(total.T, vec_ref[0:1, :], h, rstd)


def project_back(me, tokens, grad_middle, vec, grads, w):
    nd = len(w)
    return pl.pallas_call(
        functools.partial(project_back_kernel, nd),
        grid=(1,),
        in_specs=[SMEM, whole((WIN, D)), whole((WIN, D)), whole((16, D))]
        + [whole((GR, WIN))] * (3 * GROUPS)
        + [ANY] * nd,
        out_specs=whole((WIN, D)),
        out_shape=jax.ShapeDtypeStruct((WIN, D), f32),
        scratch_shapes=[pltpu.VMEM((D, w[0].shape[1]), bf16), pltpu.SemaphoreType.DMA((nd,))],
        compiler_params=room(58),
        cost_estimate=pl.CostEstimate(flops=2 * WIN * D * 3 * D, bytes_accessed=20 << 20, transcendentals=0),
        name="project_back",
    )(me, tokens, grad_middle, vec, *grads, *w)


def body(nd, nf, tokens, segment_ids, cotangent, projector, combiner, attend_bias, expander,
         expand_bias, reducer, reduce_bias, first_gain, first_shift, second_gain, second_shift):
    r, q = projector.shape[0], reducer.shape[0] // 2
    count = nd * nf
    me = lax.axis_index("dp").astype(jnp.int32).reshape(1)
    picks = half_columns(q)
    turns = half_columns(r)
    vectors = (first_gain, first_shift, attend_bias, second_gain, second_shift, reduce_bias, expand_bias)
    tie = lax.optimization_barrier

    shard_w, shard_1, shard_2 = pack(projector, expander, reducer, combiner, picks, vectors)
    parts_w, parts_1 = shifts(shard_w, nf), shifts(shard_1, nf)
    scaled_t, cotangent_t = prepare(after(tokens, shard_w), cotangent)
    parts_w, scaled_t, cotangent_t = tie((parts_w, scaled_t, cotangent_t))
    (zw,) = line_up(nf, [(0, r, 0, 0, 0)], [(nf * r, 3 * D + VEC)], parts_w)
    w = spread_plane(zw, nd)
    moves = [(0, r, 0, 0, 0), (r, r, 0, nf * r, 0), (2 * r, q, 0, 2 * nf * r, 0)]
    extra = [(2 * r + q, r, 0, nf * (2 * r + q), 0)]
    (z1,) = line_up(nf, moves + extra, [(nf * (3 * r + q), D)], after(parts_1, zw))
    w, z1 = tie((w, z1))
    w = spread_cores(w, nd)
    scaled_t, z1 = tie((scaled_t, z1))
    f1 = spread_plane(z1, nd)
    project_t, normed_t, vecs, bias = project(me, scaled_t, turns, w)
    parts_2 = shifts(after(shard_2, project_t), nf)
    attended, sums = [], []
    for g in range(GROUPS):
        if g == GROUPS - 1:
            f1, parts_2, project_t, _ = tie((f1, parts_2, project_t, attended))
            (z2,) = line_up(nf, moves, [(nf * (2 * r + q), D)], parts_2)
            z2, project_t = tie((z2, project_t))
            f2 = spread_plane(z2, nd)
            f1 = spread_cores(f1, nd)
        a, l = attend(g, project_t, segment_ids)
        attended.append(a)
        sums.append(l)
    *state, s1, k1, gbe1 = ffn_first(me, tokens, attended, cotangent, cotangent_t, vecs, bias, f1, nd)
    s1, k1, f2 = tie((s1, k1, f2))
    got, f2 = tie((flip(s1, 1, nd), f2))
    f2 = spread_cores(f2, nd)
    t1 = [add(k1[m], got[m]) for m in range(nd // 2)]
    t1, cotangent = tie((t1, cotangent))
    m1 = meet_plane(t1, nd)
    out, grad_middle, grad_t, s2, k2, gbe2, gvec = ffn_last(
        me, attended, cotangent, cotangent_t, vecs, bias, f2, f1, state, nd
    )

    cuts = [(0, r, 0), (nf * r, r, r), (2 * nf * r, q, 2 * r)]
    more = [(nf * (2 * r + q), r, 2 * r + q)]
    m1, s2, k2, grad_t = tie((m1, s2, k2, grad_t))
    p1 = pieces(nf, cuts, m1)
    p1, grad_t = tie((p1, grad_t))
    got = flip(s2, 1, nd)
    p1 = [shift(p, k, nf) if k else p for k, p in enumerate(p1)]
    grads = [attend_back(0, project_t, attended[0], grad_t, sums[0], segment_ids)]
    got, k2, grads, grad_t, p1 = tie((got, k2, grads, grad_t, p1))
    t2 = [add(k2[m], got[m]) for m in range(nd // 2)]
    t2, grad_t = tie((t2, grad_t))
    m2 = meet_plane(t2, nd)
    for g in range(1, GROUPS):
        grads.append(attend_back(g, project_t, attended[g], grad_t, sums[g], segment_ids))
    m2, p1, grads = tie((m2, p1, grads))
    p2 = pieces(nf, cuts + more, m2)
    p2, grads = tie((p2, grads))
    p2 = [shift(p, k, nf) if k else p for k, p in enumerate(p2)]
    grads = [grads[g][j] for j in range(3) for g in range(GROUPS)]
    send, keep = weight_grad(me, nd, normed_t, vecs, gvec, (gbe1, gbe2), turns, grads, w)
    totals = sum_cores(send, keep, nd)
    grads, totals = tie((grads, totals))
    met = meet_plane(totals, nd)
    grad_tokens = project_back(me, tokens, grad_middle, vecs, grads, w)
    grad_tokens, met, p2 = tie((grad_tokens, met, p2))
    gw = sum(v.astype(f32) for v in met).astype(bf16)
    grad_expander, grad_reducer, grad_combiner = finish(r, q, picks, p1, p2)
    last = scatter_z(gw, [r], nf)
    grad_projector, small = last[:, : 3 * D], last[:, 3 * D :]
    return (
        out,
        grad_tokens,
        grad_projector,
        grad_combiner,
        small[:, 2],
        grad_expander,
        small[:, 6:10].T.reshape(-1),
        grad_reducer,
        small[:, 5],
        small[:, 0],
        small[:, 1],
        small[:, 3],
        small[:, 4],
    )


def solution(mesh):
    rows, flat = P(("dp", "fsdp"), None), P(("dp", "fsdp"))
    return jax.shard_map(
        functools.partial(body, mesh.shape["dp"], mesh.shape["fsdp"]),
        mesh=mesh,
        in_specs=(rows, rows, rows, rows, rows, flat, rows, flat, rows, flat, flat, flat, flat, flat),
        out_specs=(rows, rows, rows, rows, flat, rows, flat, rows, flat, flat, flat, flat, flat),
        check_vma=False,
    )
```

```python
import functools
import math

import jax
import jax.numpy as jnp
import numpy as np
from jax import lax
from jax.experimental import pallas as pl
from jax.experimental.pallas import tpu as pltpu
from jax.sharding import PartitionSpec as P

D = 768
HD = 32
HEADS = 24
WIN = 1024
BLOCK = 256
EPS = 1e-05
LOG2E = math.log2(math.e)
BIG = float(2**30)
VEC = 128
f32 = jnp.float32
bf16 = jnp.bfloat16
NN = (((1,), (0,)), ((), ()))
NT = (((1,), (1,)), ((), ()))
ANY = pl.BlockSpec(memory_space=pl.ANY)
SMEM = pl.BlockSpec(memory_space=pltpu.SMEM)


def room(mib):
    return pltpu.CompilerParams(vmem_limit_bytes=mib << 20)


def dot(a, b, dims=NN):
    return lax.dot_general(a, b, dims, preferred_element_type=f32)


def whole(shape):
    return pl.BlockSpec(shape, lambda *_: (0,) * len(shape), pipeline_mode=pl.Buffered(1))


def flip(value, bit, count):
    return lax.ppermute(value, "dp", [(i, i ^ bit) for i in range(count)])


def shift(value, step, count):
    return lax.ppermute(value, "fsdp", [(i, (i + step) % count) for i in range(count)])


def after(value, *others):
    return lax.optimization_barrier((value, others))[0]


def shifts(shard, nf):
    return [shard] + [shift(shard, k, nf) for k in range(1, nf)]


def line_up_kernel(nf, moves, me_ref, *refs):
    me = me_ref[0]
    parts, outs = refs[:nf], refs[nf:]
    for k in range(nf):
        for j in range(nf):
            @pl.when(lax.rem(me - k + nf, nf) == j)
            def _():
                for source, rows, out, row, col in moves:
                    value = parts[k][source : source + rows, :]
                    at = row + j * rows
                    outs[out][at : at + rows, col : col + value.shape[1]] = value


def line_up(nf, moves, shapes, parts):
    return pl.pallas_call(
        functools.partial(line_up_kernel, nf, moves),
        in_specs=[SMEM] + [whole(p.shape) for p in parts],
        out_specs=[whole(x) for x in shapes],
        out_shape=[jax.ShapeDtypeStruct(x, bf16) for x in shapes],
        grid=(1,),
        compiler_params=room(10),
        cost_estimate=pl.CostEstimate(flops=0, bytes_accessed=4 << 20, transcendentals=0),
        name="line_up",
    )(lax.axis_index("fsdp").astype(jnp.int32).reshape(1), *parts)


def add(a, b):
    return (a.astype(f32) + b.astype(f32)).astype(bf16)


def spread_plane(block, nd):
    return {m: flip(block, m, nd) if m else block for m in range(0, nd, 2)}


def spread_cores(blocks, nd):
    both = {**blocks, **{m ^ 1: flip(v, 1, nd) for m, v in blocks.items()}}
    return [both[m] for m in range(nd)]


def sum_cores(send, keep, nd):
    got = flip(send, 1, nd)
    return [add(keep[m], got[m]) for m in range(nd // 2)]


def meet_plane(totals, nd):
    return [flip(v, 2 * m, nd) if m else v for m, v in enumerate(totals)]


def scatter_z(block, rows, nf):
    me = lax.axis_index("fsdp")

    def piece(z):
        got, at = [], 0
        for r in rows:
            got.append(lax.dynamic_slice_in_dim(block, at + z * r, r, 0))
            at += nf * r
        return got[0] if len(got) == 1 else jnp.concatenate(got, axis=0)

    total = piece(me).astype(f32)
    for k in range(1, nf):
        total = total + shift(piece(lax.rem(me + k, nf)), k, nf).astype(f32)
    return total


def half_columns(q):
    o = np.arange(D // 2)
    source = (o // q) * (2 * q) + o % q
    picks = np.arange(D)[None, :, None] == (source[None, None, :] + q * np.arange(2)[:, None, None])
    return jnp.asarray(picks, bf16)


def pack_kernel(proj_ref, exp_ref, red_ref, comb_ref, pick_ref, *refs):
    vec_refs, (w_ref, f1_ref, f2_ref) = refs[:-3], refs[-3:]
    r, q = proj_ref.shape[0], red_ref.shape[0] // 2
    w_ref[:, : 3 * D] = proj_ref[...]
    row = [ref[...].astype(f32).reshape(1, -1) for ref in vec_refs]
    rows = row[:6] + [row[6][:, j * r : (j + 1) * r] for j in range(4)]
    rows.append(jnp.zeros((VEC - 10, r), f32))
    w_ref[:, 3 * D :] = jnp.concatenate(rows, axis=0).T.astype(bf16)
    for h, ref in enumerate((f1_ref, f2_ref)):
        for c in range(4):
            at, col = (c // 2) * r, (c % 2) * (D // 2)
            ref[at : at + r, col : col + D // 2] = dot(
                exp_ref[:, c * D : (c + 1) * D], pick_ref[h]
            ).astype(bf16)
        ref[2 * r : 2 * r + q, :] = red_ref[h * q : (h + 1) * q, :]
    f1_ref[2 * r + q :, :] = comb_ref[...]


def pack(projector, expander, reducer, combiner, picks, vectors):
    r, q = projector.shape[0], reducer.shape[0] // 2
    shapes = [(r, 3 * D + VEC), (3 * r + q, D), (2 * r + q, D)]
    arrays = (projector, expander, reducer, combiner, picks, *vectors)
    return pl.pallas_call(
        pack_kernel,
        grid=(1,),
        in_specs=[whole(a.shape) for a in arrays],
        out_specs=[whole(x) for x in shapes],
        out_shape=[jax.ShapeDtypeStruct(x, bf16) for x in shapes],
        compiler_params=room(58),
        cost_estimate=pl.CostEstimate(flops=0, bytes_accessed=3 << 20, transcendentals=0),
        name="pack",
    )(*arrays)


def pieces_kernel(nf, moves, me_ref, *refs):
    terms, outs = refs[:-nf], refs[-nf:]
    me = me_ref[0]
    for row, rows, at in moves:
        for j in range(nf):
            here = slice(row + j * rows, row + (j + 1) * rows)
            value = sum(t[here, :].astype(f32) for t in terms).astype(bf16)
            for k in range(nf):
                @pl.when(lax.rem(me + k, nf) == j)
                def _():
                    outs[k][at : at + rows, :] = value


def pieces(nf, moves, terms):
    rows = sum(m[1] for m in moves)
    return pl.pallas_call(
        functools.partial(pieces_kernel, nf, moves),
        in_specs=[SMEM] + [whole(x.shape) for x in terms],
        out_specs=[whole((rows, D))] * nf,
        out_shape=[jax.ShapeDtypeStruct((rows, D), bf16)] * nf,
        grid=(1,),
        compiler_params=room(12),
        cost_estimate=pl.CostEstimate(flops=0, bytes_accessed=6 << 20, transcendentals=0),
        name="pieces",
    )(lax.axis_index("fsdp").astype(jnp.int32).reshape(1), *terms)


def finish_kernel(r, q, nf, pick_ref, *refs):
    halves, (ge_ref, gr_ref, gc_ref) = (refs[:nf], refs[nf : 2 * nf]), refs[2 * nf :]
    for c in range(4):
        total = jnp.zeros((r, D), f32)
        for h in range(2):
            at, col = (c // 2) * r, (c % 2) * (D // 2)
            for p in halves[h]:
                total += dot(p[at : at + r, col : col + D // 2], pick_ref[h], NT)
        ge_ref[:, c * D : (c + 1) * D] = total
    for h in range(2):
        gr_ref[h * q : (h + 1) * q, :] = sum(p[2 * r : 2 * r + q, :].astype(f32) for p in halves[h])
    gc_ref[...] = sum(p[2 * r + q :, :].astype(f32) for p in halves[1])


def finish(r, q, picks, first, second):
    shapes = [(r, 4 * D), (2 * q, D), (r, D)]
    arrays = (picks, *first, *second)
    return pl.pallas_call(
        functools.partial(finish_kernel, r, q, len(first)),
        grid=(1,),
        in_specs=[whole(x.shape) for x in arrays],
        out_specs=[whole(x) for x in shapes],
        out_shape=[jax.ShapeDtypeStruct(x, f32) for x in shapes],
        compiler_params=room(12),
        cost_estimate=pl.CostEstimate(flops=0, bytes_accessed=3 << 20, transcendentals=0),
        name="finish",
    )(*arrays)


def load_blocks(me, refs, target, sems, base, row=0, rows=None, col=0):
    rows = rows or refs[0].shape[0]
    width = refs[0].shape[1]
    copies = []
    for m, ref in enumerate(refs):
        at = pl.multiple_of((me ^ m) * rows, 16)
        copy = pltpu.make_async_copy(
            ref.at[pl.ds(row, rows), :], target.at[pl.ds(at, rows), pl.ds(col, width)], sems.at[base + m]
        )
        copy.start()
        copies.append(copy)
    return copies


def norm_parts(v):
    c = v - jnp.mean(v, axis=-1, keepdims=True)
    rstd = lax.rsqrt(jnp.mean(c * c, axis=-1, keepdims=True) + EPS)
    return c * rstd, rstd


def norm_back(grad, gain, h, rstd):
    e = grad * gain
    return (e - jnp.mean(e, -1, keepdims=True) - h * jnp.mean(e * h, -1, keepdims=True)) * rstd


def prepare_kernel(x_ref, cot_ref, ht_ref, ct_ref):
    @pl.loop(0, WIN // BLOCK)
    def _(t):
        rows = pl.ds(pl.multiple_of(t * BLOCK, BLOCK), BLOCK)
        h, _ = norm_parts(x_ref[rows, :].astype(f32))
        ht_ref[:, rows] = h.T
        ct_ref[:, rows] = cot_ref[rows, :].T


def prepare(tokens, cotangent):
    return pl.pallas_call(
        prepare_kernel,
        grid=(1,),
        in_specs=[whole((WIN, D))] * 2,
        out_specs=[whole((D, WIN))] * 2,
        out_shape=[jax.ShapeDtypeStruct((D, WIN), f32), jax.ShapeDtypeStruct((D, WIN), bf16)],
        compiler_params=room(20),
        cost_estimate=pl.CostEstimate(flops=5_000_000_000, bytes_accessed=8 << 20, transcendentals=0),
        name="prepare",
    )(tokens, cotangent)


def project_kernel(nd, me_ref, ht_ref, turn_ref, *rest):
    w = rest[:nd]
    pt_ref, nt_ref, vec_ref, bias_ref, full, sems = rest[nd:]
    for copy in load_blocks(me_ref[0], w, full, sems, 0):
        copy.wait()
    columns = full[:, 3 * D :].astype(f32)
    vec = columns.T
    vec_ref[...] = vec[:16]
    low = vec[:16].astype(bf16)
    for i in range(4):
        c, row = i % 2, 6 + 2 * (i // 2)
        parts = [dot(low[:, c * (D // 2) : (c + 1) * (D // 2)], turn_ref[k], NT) for k in range(2)]
        bias_ref[:, i * D : (i + 1) * D] = parts[0][row : row + 1] + parts[1][row + 1 : row + 2]
    nt_ref[...] = (ht_ref[...] * columns[:, 0:1] + columns[:, 1:2]).astype(bf16)

    for c in range(0, 3 * D, BLOCK):
        cols = slice(c, c + BLOCK)
        pt_ref[cols, :] = dot(full[:, cols].T, nt_ref[...]).astype(bf16)


def project(me, normed_t, turns, w):
    nd = len(w)
    return pl.pallas_call(
        functools.partial(project_kernel, nd),
        in_specs=[SMEM, whole((D, WIN)), whole(turns.shape)] + [ANY] * nd,
        out_specs=[whole((3 * D, WIN)), whole((D, WIN)), whole((16, D)), whole((1, 4 * D))],
        out_shape=[
            jax.ShapeDtypeStruct((3 * D, WIN), bf16),
            jax.ShapeDtypeStruct((D, WIN), bf16),
            jax.ShapeDtypeStruct((16, D), f32),
            jax.ShapeDtypeStruct((1, 4 * D), f32),
        ],
        scratch_shapes=[pltpu.VMEM((D, w[0].shape[1]), bf16), pltpu.SemaphoreType.DMA((nd,))],
        grid=(1,),
        compiler_params=room(26),
        cost_estimate=pl.CostEstimate(flops=2 * WIN * D * 3 * D, bytes_accessed=12 << 20, transcendentals=0),
        name="project",
    )(me, normed_t, turns, *w)


GH = 8
SH = 8
GR = GH * HD


def causal_penalty():
    ik = lax.broadcasted_iota(jnp.int32, (BLOCK, BLOCK), 0)
    iq = lax.broadcasted_iota(jnp.int32, (BLOCK, BLOCK), 1)
    return jnp.where(iq >= ik, 0.0, -BIG)


def split_scaled(q):
    scaled = q.astype(f32) * (HD**-0.5 * LOG2E)
    high = scaled.astype(bf16)
    return high, (scaled - high.astype(f32)).astype(bf16)


def episode_rows(seg):
    hot = lax.broadcasted_iota(jnp.int32, (8, WIN), 0) == seg
    return hot.astype(f32), jnp.where(hot, 0.0, -BIG)


def attend_kernel(q_ref, k_ref, v_ref, seg_ref, out_ref, lse_ref, qa, ka, va, cm):
    @pl.when(pl.program_id(0) == 0)
    def _():
        cm[...] = causal_penalty()

    hot, pen = episode_rows(seg_ref[...])
    pad = jnp.zeros((56, WIN), f32)
    tail_q = jnp.concatenate([hot, pad], axis=0).astype(bf16)
    tail_k = jnp.concatenate([pen, pad], axis=0).astype(bf16)
    ones = jnp.ones((16, WIN), bf16)
    for h in range(GH):
        rows = slice(h * HD, (h + 1) * HD)
        high, low = split_scaled(q_ref[rows, :])
        k = k_ref[rows, :]
        qa[h] = jnp.concatenate([high, low, tail_q], axis=0)
        ka[h] = jnp.concatenate([k, k, tail_k], axis=0).T
        va[h] = jnp.concatenate([v_ref[rows, :], ones], axis=0)
    c = cm[...]
    for qb in range(WIN // BLOCK):
        k0, k1 = max(0, qb - 2) * BLOCK, (qb + 1) * BLOCK
        qs = slice(qb * BLOCK, k1)
        for hb in range(0, GH, SH):
            heads = range(hb, hb + SH)
            s = [dot(ka[h, k0:k1, :], qa[h, :, qs]) for h in heads]
            w = k1 - k0 - BLOCK
            s = [jnp.concatenate([x[:w], x[w:] + c], axis=0) if w else x + c for x in s]
            top = [jnp.max(x, axis=0, keepdims=True) for x in s]
            p = [jnp.exp2(x - y) for x, y in zip(s, top)]
            o = [dot(va[h, :, k0:k1], y.astype(bf16)) for h, y in zip(heads, p)]
            for i, h in enumerate(heads):
                total = o[i][HD : HD + 1]
                out_ref[h * HD : (h + 1) * HD, qs] = (o[i][:HD] * (1.0 / total)).astype(bf16)
                lse_ref[h, :, qs] = top[i] + jnp.log2(total)


GROUPS = HEADS // GH


def head_rows(index):
    return pl.BlockSpec((GR, WIN), lambda i: (index, 0))


def head_sums(index):
    return pl.BlockSpec((GH, 1, WIN), lambda i: (index, 0, 0))


def attend(group, project_t, seg):
    return pl.pallas_call(
        attend_kernel,
        grid=(1,),
        in_specs=[head_rows(group + j * GROUPS) for j in range(3)] + [whole((1, WIN))],
        out_specs=[head_rows(0), head_sums(0)],
        out_shape=[
            jax.ShapeDtypeStruct((GR, WIN), bf16),
            jax.ShapeDtypeStruct((GH, 1, WIN), f32),
        ],
        scratch_shapes=[
            pltpu.VMEM((GH, 128, WIN), bf16),
            pltpu.VMEM((GH, WIN, 128), bf16),
            pltpu.VMEM((GH, HD + 16, WIN), bf16),
            pltpu.VMEM((BLOCK, BLOCK), f32),
        ],
        compiler_params=room(24),
        cost_estimate=pl.CostEstimate(flops=7_000_000_000, bytes_accessed=3 << 20, transcendentals=0),
        name="attend",
    )(project_t, project_t, project_t, seg)


def attend_back_kernel(
    q_ref, k_ref, v_ref, o_ref, do_ref, lse_ref, seg_ref, dq_ref, dk_ref, dv_ref, qa, ka, va, da, aq, cm
):
    hot, pen = episode_rows(seg_ref[...])
    ids = lax.broadcasted_iota(jnp.int32, (8, WIN), 0)
    ones3 = jnp.where(ids < 3, 1.0, 0.0)
    z48 = jnp.zeros((48, WIN), f32)
    z88 = jnp.zeros((88, WIN), f32)

    def rows3(v):
        a = v.astype(bf16).astype(f32)
        b = (v - a).astype(bf16).astype(f32)
        return jnp.where(ids == 0, a, jnp.where(ids == 1, b, jnp.where(ids == 2, v - a - b, 0.0)))

    tail_k = jnp.concatenate([pen, ones3, z48], axis=0).astype(bf16)
    tail_v = jnp.concatenate([ones3, z88], axis=0).astype(bf16)
    for h in range(GH):
        rows = slice(h * HD, (h + 1) * HD)
        high, low = split_scaled(q_ref[rows, :])
        k, v, g = k_ref[rows, :], v_ref[rows, :], do_ref[rows, :]
        delta = jnp.sum(g.astype(f32) * o_ref[rows, :].astype(f32), axis=0, keepdims=True)
        tail_q = jnp.concatenate([hot, rows3(-lse_ref[h]), z48], axis=0).astype(bf16)
        tail_g = jnp.concatenate([rows3(-delta), z88], axis=0).astype(bf16)
        qa[h] = jnp.concatenate([high, low, tail_q], axis=0).T
        ka[h] = jnp.concatenate([k, k, tail_k], axis=0)
        va[h] = jnp.concatenate([v, tail_v], axis=0)
        da[h] = jnp.concatenate([g, tail_g], axis=0).T
    ik = lax.broadcasted_iota(jnp.int32, (BLOCK, BLOCK), 1)
    iq = lax.broadcasted_iota(jnp.int32, (BLOCK, BLOCK), 0)
    cm[...] = jnp.where(iq >= ik, 0.0, -BIG)
    c = cm[...]
    scale = HD**-0.5
    step = 4
    nb = WIN // BLOCK
    for kb in range(nb):
        q0, q1 = kb * BLOCK, min(nb, kb + 3) * BLOCK
        ks = slice(q0, q0 + BLOCK)
        for hb in range(0, GH, step):
            heads = range(hb, hb + step)
            rows = [slice(h * HD, (h + 1) * HD) for h in heads]
            s = [dot(qa[h, q0:q1, :], ka[h, :, ks]) for h in heads]
            dp = [dot(da[h, q0:q1, :], va[h, :, ks]) for h in heads]
            s = [
                jnp.concatenate([x[:BLOCK] + c, x[BLOCK:]], axis=0) if q1 - q0 > BLOCK else x + c
                for x in s
            ]
            p = [jnp.exp2(x) for x in s]
            ds = [(x * y).astype(bf16) for x, y in zip(p, dp)]
            pb = [x.astype(bf16) for x in p]
            dv = [dot(do_ref[x, q0:q1], y) for x, y in zip(rows, pb)]
            dk = [dot(q_ref[x, q0:q1], y) for x, y in zip(rows, ds)]
            dq = [dot(k_ref[x, ks], y, NT) for x, y in zip(rows, ds)]
            for i in range(step):
                dv_ref[rows[i], ks] = dv[i].astype(bf16)
                dk_ref[rows[i], ks] = (dk[i] * scale).astype(bf16)
                done = min(nb, kb + 2) * BLOCK if kb else 0
                if done > q0:
                    aq[rows[i], q0:done] += dq[i][:, : done - q0]
                if q1 > max(done, q0):
                    at = max(done, q0)
                    aq[rows[i], at:q1] = dq[i][:, at - q0 :]
    dq_ref[...] = (aq[...] * scale).astype(bf16)


def attend_back(group, project_t, attended_t, grad_t, lse, seg):
    return pl.pallas_call(
        attend_back_kernel,
        grid=(1,),
        in_specs=[head_rows(group + j * GROUPS) for j in range(3)]
        + [head_rows(0), head_rows(group), head_sums(0), whole((1, WIN))],
        out_specs=[head_rows(0)] * 3,
        out_shape=[jax.ShapeDtypeStruct((GR, WIN), bf16)] * 3,
        scratch_shapes=[
            pltpu.VMEM((GH, WIN, 128), bf16),
            pltpu.VMEM((GH, 128, WIN), bf16),
            pltpu.VMEM((GH, 128, WIN), bf16),
            pltpu.VMEM((GH, WIN, 128), bf16),
            pltpu.VMEM((GR, WIN), f32),
            pltpu.VMEM((BLOCK, BLOCK), f32),
        ],
        compiler_params=room(32),
        cost_estimate=pl.CostEstimate(flops=14_000_000_000, bytes_accessed=5 << 20, transcendentals=0),
        name="attend_back",
    )(project_t, project_t, project_t, attended_t, grad_t, lse, seg)


def gelu_both(u):
    a, b = math.sqrt(2 / math.pi), 0.044715
    sq = u * u
    t = jnp.tanh(u * (a + (a * b) * sq))
    half = 0.5 + 0.5 * t
    slope = half + (0.5 * u) * (1.0 - t * t) * (a + (3 * a * b) * sq)
    return u * half, slope


TB = 512


def token_loop(step):
    @pl.loop(0, WIN // TB)
    def _(t):
        step(pl.ds(pl.multiple_of(t * TB, TB), TB))


def load_weights(me, nd, blocks, exp, red, sems):
    rb, rr = D // nd, red.shape[0] // nd
    copies = load_blocks(me, blocks, exp, sems, nd, 0, rb, 0)
    copies += load_blocks(me, blocks, exp, sems, 2 * nd, rb, rb, D)
    return copies + load_blocks(me, blocks, red, sems, 3 * nd, 2 * rb, rr, 0)


def ffn_chunk(i, me, nd, cot_ref, be_ref, exp, red, n2, n2t, cott, oacc, nacc, ascr, gscr, tmp, gbe_ref, send, keep):
    rb, rr, chunk = D // nd, red.shape[0] // nd, tmp.shape[1]
    cols = pl.ds(pl.multiple_of(i * chunk, 128), chunk)
    gbe_ref[...] = jnp.zeros((1, chunk), f32)

    def step(rows):
        u = dot(n2[rows, :], exp[:, cols]) + be_ref[...]
        ga = dot(cot_ref[rows, :], red[cols, :], NT)
        act, slope = gelu_both(u)
        act = act.astype(bf16)
        gu = (ga * slope).astype(bf16)
        ascr[rows, :] = act
        gscr[rows, :] = gu
        gbe_ref[...] += jnp.sum(gu.astype(f32), axis=0, keepdims=True)
        oacc[rows, :] += dot(act, red[cols, :])
        nacc[rows, :] += dot(gu, exp[:, cols], NT)

    token_loop(step)
    tmp[...] = dot(n2t[...], gscr[...]).astype(bf16)
    emit(me, tmp, send, keep, pl.ds(pl.multiple_of(i * rb, 16), rb))
    tmp[...] = dot(cott[...], ascr[...]).astype(bf16).T
    per = chunk // rr
    for b in range(per):
        mask = me ^ (i * per + b)
        for odd, ref in ((1, send), (0, keep)):
            @pl.when((mask & 1) == odd)
            def _():
                ref[mask >> 1, 2 * rb : 2 * rb + rr, :] = tmp[b * rr : (b + 1) * rr, :]


def ffn_first_kernel(nd, me_ref, x_ref, cot_ref, cott, vec_ref, be_ref, *rest):
    att, blocks, rest = rest[:GROUPS], rest[GROUPS : GROUPS + nd], rest[GROUPS + nd :]
    mid_ref, n2_ref, part_ref, nacc_ref, send, keep, gbe_ref = rest[:7]
    comb, exp, red, mid, n2, n2t, oacc, nacc, ascr, gscr, tmp, sems = rest[7:]
    i = pl.program_id(0)
    me = me_ref[0]
    rb, rr = D // nd, red.shape[0] // nd
    outs = [
        pltpu.make_async_copy(a, b, sems.at[4 * nd + j])
        for j, (a, b) in enumerate(((mid, mid_ref), (n2, n2_ref), (oacc, part_ref), (nacc, nacc_ref)))
    ]

    @pl.when(i == 0)
    def _():
        got = load_blocks(me, blocks, comb, sems, 0, 2 * rb + rr, rb, 0)
        late = load_weights(me, nd, blocks, exp, red, sems)
        for copy in got:
            copy.wait()

        def step(rows):
            m = x_ref[rows, :].astype(f32) + vec_ref[2:3, :]
            for g in range(GROUPS):
                m += dot(att[g][:, rows].T, comb[g * GR : (g + 1) * GR, :])
            mid[rows, :] = m
            oacc[rows, :] = m + vec_ref[5:6, :]
            h, _ = norm_parts(m)
            n = (h * vec_ref[3:4, :] + vec_ref[4:5, :]).astype(bf16)
            n2[rows, :] = n
            n2t[:, rows] = n.T

        token_loop(step)
        nacc[...] = jnp.zeros_like(nacc)
        outs[0].start()
        outs[1].start()
        for copy in late:
            copy.wait()

    ffn_chunk(i, me, nd, cot_ref, be_ref, exp, red, n2, n2t, cott, oacc, nacc, ascr, gscr, tmp, gbe_ref, send, keep)

    @pl.when(i == pl.num_programs(0) - 1)
    def _():
        outs[2].start()
        outs[3].start()
        for copy in outs:
            copy.wait()


def ffn_last_kernel(nd, me_ref, cot_ref, cott, vec_ref, be_ref, *rest):
    att, blocks, rest = rest[:GROUPS], rest[GROUPS : GROUPS + nd], rest[GROUPS + nd :]
    others, rest = rest[:nd], rest[nd:]
    mid_ref, n2_ref, part_ref, naccin_ref = rest[:4]
    out_any, gm_any, dt_any, send_any, keep_any, gbe_ref, gv_ref = rest[4:11]
    comb, exp, red, mid, part, nin, n2, n2t, oacc, nacc, ascr, gscr, tmp, sems = rest[11:25]
    out_ref, gm_ref, dt_ref, send, keep = rest[25:]
    i = pl.program_id(0)
    me = me_ref[0]
    rb, rr = D // nd, red.shape[0] // nd
    ins = [
        pltpu.make_async_copy(a, b, sems.at[4 * nd + j])
        for j, (a, b) in enumerate(((n2_ref, n2), (mid_ref, mid), (part_ref, part), (naccin_ref, nin)))
    ]
    early, last = pl.ds(0, 2 * rb + rr), pl.ds(2 * rb + rr, rb)
    leaving = (
        (send.at[:, early, :], send_any.at[:, early, :]),
        (keep.at[:, early, :], keep_any.at[:, early, :]),
        (out_ref, out_any),
        (gm_ref, gm_any),
        (dt_ref, dt_any),
        (send.at[:, last, :], send_any.at[:, last, :]),
        (keep.at[:, last, :], keep_any.at[:, last, :]),
    )
    outs = [pltpu.make_async_copy(a, b, sems.at[4 * nd + 4 + j]) for j, (a, b) in enumerate(leaving)]

    @pl.when(i == 0)
    def _():
        ins[0].start()
        got = load_weights(me, nd, blocks, exp, red, sems)
        got += load_blocks(me, others, comb, sems, 0, 2 * rb + rr, rb, 0)
        for copy in ins[1:]:
            copy.start()
        oacc[...] = jnp.zeros_like(oacc)
        nacc[...] = jnp.zeros_like(nacc)
        ins[0].wait()
        n2t[...] = n2[...].T
        for copy in got:
            copy.wait()

    ffn_chunk(i, me, nd, cot_ref, be_ref, exp, red, n2, n2t, cott, oacc, nacc, ascr, gscr, tmp, gbe_ref, send, keep)

    @pl.when(i == pl.num_programs(0) - 1)
    def _():
        for copy in outs[:2]:
            copy.start()
        for copy in ins[1:]:
            copy.wait()
        gv_ref[...] = jnp.zeros((8, D), f32)

        def step(rows):
            out_ref[rows, :] = (part[rows, :] + oacc[rows, :]).astype(bf16)
            h, rstd = norm_parts(mid[rows, :])
            g = nacc[rows, :] + nin[rows, :]
            cot = cot_ref[rows, :].astype(f32)
            gm = cot + norm_back(g, vec_ref[3:4, :], h, rstd)
            gm_ref[rows, :] = gm
            low = gm.astype(bf16)
            n2[rows, :] = low
            n2t[:, rows] = low.T
            sums = (low.astype(f32), g * h, g, cot)
            gv_ref[2:6, :] += jnp.concatenate([jnp.sum(v, axis=0, keepdims=True) for v in sums], axis=0)

        token_loop(step)
        outs[2].start()
        outs[3].start()
        dt_ref[...] = dot(comb[...], n2t[...]).astype(bf16)
        outs[4].start()
        for g in range(GROUPS):
            tmp[g * GR : (g + 1) * GR, :] = dot(att[g][...], n2[...]).astype(bf16)
        emit(me, tmp, send, keep, slice(2 * rb + rr, 3 * rb + rr))
        outs[5].start()
        outs[6].start()
        for copy in outs:
            copy.wait()


def ffn_call(kernel, specs, arrays, nd, rows, out_shapes, last):
    ff = 2 * D
    shape = jax.ShapeDtypeStruct
    half = (nd // 2, rows, D)
    wide = pltpu.VMEM((WIN, D), f32)
    low, turned = pltpu.VMEM((WIN, D), bf16), pltpu.VMEM((D, WIN), bf16)
    return pl.pallas_call(
        functools.partial(kernel, nd),
        grid=(ff // D,),
        in_specs=specs,
        out_specs=[ANY for x in out_shapes]
        + [ANY if last else whole(half)] * 2
        + [pl.BlockSpec((1, D), lambda i: (0, i))]
        + ([whole((8, D))] if last else []),
        out_shape=list(out_shapes)
        + [shape(half, bf16), shape(half, bf16), shape((1, ff), f32)]
        + ([shape((8, D), f32)] if last else []),
        scratch_shapes=[pltpu.VMEM((D, D), bf16), pltpu.VMEM((D, ff), bf16), pltpu.VMEM((ff, D), bf16)]
        + [wide] * (3 if last else 1)
        + [low, turned, wide, wide, low, low, pltpu.VMEM((D, D), bf16)]
        + [pltpu.SemaphoreType.DMA((4 * nd + 11,))]
        + ([low, wide, turned, pltpu.VMEM(half, bf16), pltpu.VMEM(half, bf16)] if last else []),
        compiler_params=room(52 if last else 36),
        cost_estimate=pl.CostEstimate(flops=12 * WIN * D * ff, bytes_accessed=20 << 20, transcendentals=0),
        name="ffn_last" if last else "ffn_first",
    )(*arrays)


def ffn_first(me, tokens, attended, cotangent, cotangent_t, vec, bias, blocks, nd):
    shape = jax.ShapeDtypeStruct
    outs = [shape((WIN, D), f32), shape((WIN, D), bf16), shape((WIN, D), f32), shape((WIN, D), f32)]
    specs = [SMEM, whole((WIN, D)), whole((WIN, D)), whole((D, WIN)), whole((16, D))]
    specs += [pl.BlockSpec((1, D), lambda i: (0, i))]
    specs += [whole((GR, WIN))] * GROUPS + [ANY] * nd
    arrays = (me, tokens, cotangent, cotangent_t, vec, bias, *attended, *blocks)
    return ffn_call(ffn_first_kernel, specs, arrays, nd, (4 * D) // nd, outs, False)


def ffn_last(me, attended, cotangent, cotangent_t, vec, bias, blocks, others, state, nd):
    shape = jax.ShapeDtypeStruct
    outs = [shape((WIN, D), bf16), shape((WIN, D), f32), shape((D, WIN), bf16)]
    specs = [SMEM, whole((WIN, D)), whole((D, WIN)), whole((16, D)), pl.BlockSpec((1, D), lambda i: (0, i + 2))]
    specs += [whole((GR, WIN))] * GROUPS + [ANY] * (2 * nd + 4)
    arrays = (me, cotangent, cotangent_t, vec, bias, *attended, *blocks, *others, *state)
    return ffn_call(ffn_last_kernel, specs, arrays, nd, (5 * D) // nd, outs, True)


def emit(me, source, send, keep, rows=slice(None), cols=slice(None)):
    steps = send.shape[0]
    rb = source.shape[0] // (2 * steps)
    for s in range(steps):
        far = pl.multiple_of((me ^ (2 * s + 1)) * rb, 16)
        near = pl.multiple_of((me ^ (2 * s)) * rb, 16)
        send[s, rows, cols] = source[pl.ds(far, rb), :]
        keep[s, rows, cols] = source[pl.ds(near, rb), :]


def weight_grad_kernel(nd, me_ref, nt_ref, vec_ref, gv_ref, b1_ref, b2_ref, turn_ref, *rest):
    grads, rest = rest[: 3 * GROUPS], rest[3 * GROUPS :]
    send, keep, full, tmp, gvt, acc, sems = rest[nd:]
    me = me_ref[0]
    copies = load_blocks(me, rest[:nd], full, sems, 0)
    acc[...] = jnp.zeros_like(acc)
    for i, ref in enumerate(grads):
        g = ref[...].T
        gw = dot(nt_ref[...], g)
        tmp[...] = gw.astype(bf16)
        emit(me, tmp, send, keep, cols=slice(i * GR, (i + 1) * GR))
        if i == 0:
            for copy in copies:
                copy.wait()
        w = full[:, i * GR : (i + 1) * GR].astype(f32)
        total = jnp.sum(g.astype(f32), axis=0, keepdims=True)
        for j, value in enumerate((w * gw, w * total)):
            acc[j] += value[:, :128] + value[:, 128:]
    rows = [gv_ref[:6, :]]
    for ref in (b1_ref, b2_ref):
        low = ref[...].astype(bf16)
        for k in range(2):
            rows.append(
                jnp.concatenate([dot(low[:, c * D : (c + 1) * D], turn_ref[k]) for c in range(2)], axis=1)
            )
    rows += [jnp.zeros((6, D), f32), vec_ref[:2, :], jnp.zeros((VEC - 18, D), f32)]
    base = jnp.concatenate(rows, axis=0).T
    gshift = jnp.sum(acc[1], axis=1, keepdims=True)
    ggain = (jnp.sum(acc[0], axis=1, keepdims=True) - base[:, 17:18] * gshift) / base[:, 16:17]
    lane = lax.broadcasted_iota(jnp.int32, (D, VEC), 1)
    gvt[...] = jnp.where(lane == 0, ggain, jnp.where(lane == 1, gshift, base)).astype(bf16)
    emit(me, gvt, send, keep, cols=slice(3 * D, 3 * D + VEC))


def weight_grad(me, nd, normed_t, vec, gvec, sums, turns, grads, w):
    half = (nd // 2, D // nd, 3 * D + VEC)
    return pl.pallas_call(
        functools.partial(weight_grad_kernel, nd),
        grid=(1,),
        in_specs=[SMEM, whole((D, WIN)), whole((16, D)), whole((8, D))]
        + [whole((1, 2 * D))] * 2
        + [whole(turns.shape)]
        + [whole((GR, WIN))] * (3 * GROUPS)
        + [ANY] * nd,
        out_specs=[whole(half)] * 2,
        out_shape=[jax.ShapeDtypeStruct(half, bf16)] * 2,
        scratch_shapes=[
            pltpu.VMEM((D, 3 * D + VEC), bf16),
            pltpu.VMEM((D, GR), bf16),
            pltpu.VMEM((D, VEC), bf16),
            pltpu.VMEM((2, D, 128), f32),
            pltpu.SemaphoreType.DMA((nd,)),
        ],
        compiler_params=room(30),
        cost_estimate=pl.CostEstimate(flops=2 * WIN * D * 3 * D, bytes_accessed=10 << 20, transcendentals=0),
        name="weight_grad",
    )(me, normed_t, vec, gvec, *sums, turns, *grads, *w)


def project_back_kernel(nd, me_ref, x_ref, gm_ref, vec_ref, *rest):
    grads, rest = rest[: 3 * GROUPS], rest[3 * GROUPS :]
    gt_ref, full, sems = rest[nd:]
    for copy in load_blocks(me_ref[0], rest[:nd], full, sems, 0):
        copy.wait()

    @pl.loop(0, WIN // BLOCK)
    def _(t):
        rows = pl.ds(pl.multiple_of(t * BLOCK, BLOCK), BLOCK)
        total = dot(full[:, :GR], grads[0][:, rows])
        for i in range(1, 3 * GROUPS):
            total += dot(full[:, i * GR : (i + 1) * GR], grads[i][:, rows])
        h, rstd = norm_parts(x_ref[rows, :].astype(f32))
        gt_ref[rows, :] = gm_ref[rows, :] + norm_back(total.T, vec_ref[0:1, :], h, rstd)


def project_back(me, tokens, grad_middle, vec, grads, w):
    nd = len(w)
    return pl.pallas_call(
        functools.partial(project_back_kernel, nd),
        grid=(1,),
        in_specs=[SMEM, whole((WIN, D)), whole((WIN, D)), whole((16, D))]
        + [whole((GR, WIN))] * (3 * GROUPS)
        + [ANY] * nd,
        out_specs=whole((WIN, D)),
        out_shape=jax.ShapeDtypeStruct((WIN, D), f32),
        scratch_shapes=[pltpu.VMEM((D, w[0].shape[1]), bf16), pltpu.SemaphoreType.DMA((nd,))],
        compiler_params=room(58),
        cost_estimate=pl.CostEstimate(flops=2 * WIN * D * 3 * D, bytes_accessed=20 << 20, transcendentals=0),
        name="project_back",
    )(me, tokens, grad_middle, vec, *grads, *w)


def body(nd, nf, tokens, segment_ids, cotangent, projector, combiner, attend_bias, expander,
         expand_bias, reducer, reduce_bias, first_gain, first_shift, second_gain, second_shift):
    r, q = projector.shape[0], reducer.shape[0] // 2
    count = nd * nf
    me = lax.axis_index("dp").astype(jnp.int32).reshape(1)
    picks = half_columns(q)
    turns = half_columns(r)
    vectors = (first_gain, first_shift, attend_bias, second_gain, second_shift, reduce_bias, expand_bias)
    tie = lax.optimization_barrier

    shard_w, shard_1, shard_2 = pack(projector, expander, reducer, combiner, picks, vectors)
    parts_w, parts_1 = shifts(shard_w, nf), shifts(shard_1, nf)
    scaled_t, cotangent_t = prepare(after(tokens, shard_w), cotangent)
    parts_w, scaled_t, cotangent_t = tie((parts_w, scaled_t, cotangent_t))
    (zw,) = line_up(nf, [(0, r, 0, 0, 0)], [(nf * r, 3 * D + VEC)], parts_w)
    w = spread_plane(zw, nd)
    moves = [(0, r, 0, 0, 0), (r, r, 0, nf * r, 0), (2 * r, q, 0, 2 * nf * r, 0)]
    extra = [(2 * r + q, r, 0, nf * (2 * r + q), 0)]
    (z1,) = line_up(nf, moves + extra, [(nf * (3 * r + q), D)], after(parts_1, zw))
    w, z1 = tie((w, z1))
    w = spread_cores(w, nd)
    scaled_t, z1 = tie((scaled_t, z1))
    f1 = spread_plane(z1, nd)
    project_t, normed_t, vecs, bias = project(me, scaled_t, turns, w)
    parts_2 = shifts(after(shard_2, project_t), nf)
    attended, sums = [], []
    for g in range(GROUPS):
        if g == GROUPS - 1:
            f1, parts_2, project_t, _ = tie((f1, parts_2, project_t, attended))
            (z2,) = line_up(nf, moves, [(nf * (2 * r + q), D)], parts_2)
            z2, project_t = tie((z2, project_t))
            f2 = spread_plane(z2, nd)
            f1 = spread_cores(f1, nd)
        a, l = attend(g, project_t, segment_ids)
        attended.append(a)
        sums.append(l)
    *state, s1, k1, gbe1 = ffn_first(me, tokens, attended, cotangent, cotangent_t, vecs, bias, f1, nd)
    s1, k1, f2 = tie((s1, k1, f2))
    got, f2 = tie((flip(s1, 1, nd), f2))
    f2 = spread_cores(f2, nd)
    t1 = [add(k1[m], got[m]) for m in range(nd // 2)]
    t1, cotangent = tie((t1, cotangent))
    m1 = meet_plane(t1, nd)
    out, grad_middle, grad_t, s2, k2, gbe2, gvec = ffn_last(
        me, attended, cotangent, cotangent_t, vecs, bias, f2, f1, state, nd
    )

    cuts = [(0, r, 0), (nf * r, r, r), (2 * nf * r, q, 2 * r)]
    more = [(nf * (2 * r + q), r, 2 * r + q)]
    m1, s2, k2, grad_t = tie((m1, s2, k2, grad_t))
    got = flip(s2, 1, nd)
    p1 = pieces(nf, cuts, m1)
    got, k2, p1, grad_t = tie((got, k2, p1, grad_t))
    t2 = [add(k2[m], got[m]) for m in range(nd // 2)]
    t2, grad_t = tie((t2, grad_t))
    m2 = meet_plane(t2, nd)
    p1 = [shift(p, k, nf) if k else p for k, p in enumerate(p1)]
    grads = [attend_back(0, project_t, attended[0], grad_t, sums[0], segment_ids)]
    grads, grad_t, p1 = tie((grads, grad_t, p1))
    for g in range(1, GROUPS):
        grads.append(attend_back(g, project_t, attended[g], grad_t, sums[g], segment_ids))
    grads = [grads[g][j] for j in range(3) for g in range(GROUPS)]
    m2, grads = tie((m2, grads))
    send, keep = weight_grad(me, nd, normed_t, vecs, gvec, (gbe1, gbe2), turns, grads, w)
    p2 = pieces(nf, cuts + more, after(m2, send))
    p2 = [shift(p, k, nf) if k else p for k, p in enumerate(p2)]
    totals = sum_cores(send, keep, nd)
    grads, totals = tie((grads, totals))
    met = meet_plane(totals, nd)
    grad_tokens = project_back(me, tokens, grad_middle, vecs, grads, w)
    grad_tokens, met, p2 = tie((grad_tokens, met, p2))
    gw = sum(v.astype(f32) for v in met).astype(bf16)
    grad_expander, grad_reducer, grad_combiner = finish(r, q, picks, p1, p2)
    last = scatter_z(gw, [r], nf)
    grad_projector, small = last[:, : 3 * D], last[:, 3 * D :]
    return (
        out,
        grad_tokens,
        grad_projector,
        grad_combiner,
        small[:, 2],
        grad_expander,
        small[:, 6:10].T.reshape(-1),
        grad_reducer,
        small[:, 5],
        small[:, 0],
        small[:, 1],
        small[:, 3],
        small[:, 4],
    )


def solution(mesh):
    rows, flat = P(("dp", "fsdp"), None), P(("dp", "fsdp"))
    return jax.shard_map(
        functools.partial(body, mesh.shape["dp"], mesh.shape["fsdp"]),
        mesh=mesh,
        in_specs=(rows, rows, rows, rows, rows, flat, rows, flat, rows, flat, flat, flat, flat, flat),
        out_specs=(rows, rows, rows, rows, flat, rows, flat, rows, flat, flat, flat, flat, flat),
        check_vma=False,
    )
```

```python
import functools
import math

import jax
import jax.numpy as jnp
import numpy as np
from jax import lax
from jax.experimental import pallas as pl
from jax.experimental.pallas import tpu as pltpu
from jax.sharding import PartitionSpec as P

D = 768
HD = 32
HEADS = 24
WIN = 1024
BLOCK = 256
EPS = 1e-05
LOG2E = math.log2(math.e)
BIG = float(2**30)
VEC = 128
f32 = jnp.float32
bf16 = jnp.bfloat16
NN = (((1,), (0,)), ((), ()))
NT = (((1,), (1,)), ((), ()))
ANY = pl.BlockSpec(memory_space=pl.ANY)
SMEM = pl.BlockSpec(memory_space=pltpu.SMEM)


def room(mib):
    return pltpu.CompilerParams(vmem_limit_bytes=mib << 20)


def dot(a, b, dims=NN):
    return lax.dot_general(a, b, dims, preferred_element_type=f32)


def whole(shape):
    return pl.BlockSpec(shape, lambda *_: (0,) * len(shape), pipeline_mode=pl.Buffered(1))


def flip(value, bit, count):
    return lax.ppermute(value, "dp", [(i, i ^ bit) for i in range(count)])


def shift(value, step, count):
    return lax.ppermute(value, "fsdp", [(i, (i + step) % count) for i in range(count)])


def after(value, *others):
    return lax.optimization_barrier((value, others))[0]


def shifts(shard, nf):
    return [shard] + [shift(shard, k, nf) for k in range(1, nf)]


def line_up_kernel(nf, moves, me_ref, *refs):
    me = me_ref[0]
    parts, outs = refs[:nf], refs[nf:]
    for k in range(nf):
        for j in range(nf):
            @pl.when(lax.rem(me - k + nf, nf) == j)
            def _():
                for source, rows, out, row, col in moves:
                    value = parts[k][source : source + rows, :]
                    at = row + j * rows
                    outs[out][at : at + rows, col : col + value.shape[1]] = value


def line_up(nf, moves, shapes, parts):
    return pl.pallas_call(
        functools.partial(line_up_kernel, nf, moves),
        in_specs=[SMEM] + [whole(p.shape) for p in parts],
        out_specs=[whole(x) for x in shapes],
        out_shape=[jax.ShapeDtypeStruct(x, bf16) for x in shapes],
        grid=(1,),
        compiler_params=room(10),
        cost_estimate=pl.CostEstimate(flops=0, bytes_accessed=4 << 20, transcendentals=0),
        name="line_up",
    )(lax.axis_index("fsdp").astype(jnp.int32).reshape(1), *parts)


def add(a, b):
    return (a.astype(f32) + b.astype(f32)).astype(bf16)


def spread_plane(block, nd):
    return {m: flip(block, m, nd) if m else block for m in range(0, nd, 2)}


def spread_cores(blocks, nd):
    both = {**blocks, **{m ^ 1: flip(v, 1, nd) for m, v in blocks.items()}}
    return [both[m] for m in range(nd)]


def sum_cores(send, keep, nd):
    got = flip(send, 1, nd)
    return [add(keep[m], got[m]) for m in range(nd // 2)]


def meet_plane(totals, nd):
    return [flip(v, 2 * m, nd) if m else v for m, v in enumerate(totals)]


def scatter_z(block, rows, nf):
    me = lax.axis_index("fsdp")

    def piece(z):
        got, at = [], 0
        for r in rows:
            got.append(lax.dynamic_slice_in_dim(block, at + z * r, r, 0))
            at += nf * r
        return got[0] if len(got) == 1 else jnp.concatenate(got, axis=0)

    total = piece(me).astype(f32)
    for k in range(1, nf):
        total = total + shift(piece(lax.rem(me + k, nf)), k, nf).astype(f32)
    return total


def half_columns(q):
    o = np.arange(D // 2)
    source = (o // q) * (2 * q) + o % q
    picks = np.arange(D)[None, :, None] == (source[None, None, :] + q * np.arange(2)[:, None, None])
    return jnp.asarray(picks, bf16)


def pack_kernel(proj_ref, exp_ref, red_ref, comb_ref, pick_ref, *refs):
    vec_refs, (w_ref, f1_ref, f2_ref) = refs[:-3], refs[-3:]
    r, q = proj_ref.shape[0], red_ref.shape[0] // 2
    w_ref[:, : 3 * D] = proj_ref[...]
    row = [ref[...].astype(f32).reshape(1, -1) for ref in vec_refs]
    rows = row[:6] + [row[6][:, j * r : (j + 1) * r] for j in range(4)]
    rows.append(jnp.zeros((VEC - 10, r), f32))
    w_ref[:, 3 * D :] = jnp.concatenate(rows, axis=0).T.astype(bf16)
    for h, ref in enumerate((f1_ref, f2_ref)):
        for c in range(4):
            at, col = (c // 2) * r, (c % 2) * (D // 2)
            ref[at : at + r, col : col + D // 2] = dot(
                exp_ref[:, c * D : (c + 1) * D], pick_ref[h]
            ).astype(bf16)
        ref[2 * r : 2 * r + q, :] = red_ref[h * q : (h + 1) * q, :]
    f1_ref[2 * r + q :, :] = comb_ref[...]


def pack(projector, expander, reducer, combiner, picks, vectors):
    r, q = projector.shape[0], reducer.shape[0] // 2
    shapes = [(r, 3 * D + VEC), (3 * r + q, D), (2 * r + q, D)]
    arrays = (projector, expander, reducer, combiner, picks, *vectors)
    return pl.pallas_call(
        pack_kernel,
        grid=(1,),
        in_specs=[whole(a.shape) for a in arrays],
        out_specs=[whole(x) for x in shapes],
        out_shape=[jax.ShapeDtypeStruct(x, bf16) for x in shapes],
        compiler_params=room(58),
        cost_estimate=pl.CostEstimate(flops=0, bytes_accessed=3 << 20, transcendentals=0),
        name="pack",
    )(*arrays)


def pieces_kernel(nf, moves, me_ref, *refs):
    terms, outs = refs[:-nf], refs[-nf:]
    me = me_ref[0]
    for row, rows, at in moves:
        for j in range(nf):
            here = slice(row + j * rows, row + (j + 1) * rows)
            value = sum(t[here, :].astype(f32) for t in terms).astype(bf16)
            for k in range(nf):
                @pl.when(lax.rem(me + k, nf) == j)
                def _():
                    outs[k][at : at + rows, :] = value


def pieces(nf, moves, terms):
    rows = sum(m[1] for m in moves)
    return pl.pallas_call(
        functools.partial(pieces_kernel, nf, moves),
        in_specs=[SMEM] + [whole(x.shape) for x in terms],
        out_specs=[whole((rows, D))] * nf,
        out_shape=[jax.ShapeDtypeStruct((rows, D), bf16)] * nf,
        grid=(1,),
        compiler_params=room(12),
        cost_estimate=pl.CostEstimate(flops=0, bytes_accessed=6 << 20, transcendentals=0),
        name="pieces",
    )(lax.axis_index("fsdp").astype(jnp.int32).reshape(1), *terms)


def finish_kernel(r, q, nf, pick_ref, *refs):
    halves, (ge_ref, gr_ref, gc_ref) = (refs[:nf], refs[nf : 2 * nf]), refs[2 * nf :]
    for c in range(4):
        total = jnp.zeros((r, D), f32)
        for h in range(2):
            at, col = (c // 2) * r, (c % 2) * (D // 2)
            for p in halves[h]:
                total += dot(p[at : at + r, col : col + D // 2], pick_ref[h], NT)
        ge_ref[:, c * D : (c + 1) * D] = total
    for h in range(2):
        gr_ref[h * q : (h + 1) * q, :] = sum(p[2 * r : 2 * r + q, :].astype(f32) for p in halves[h])
    gc_ref[...] = sum(p[2 * r + q :, :].astype(f32) for p in halves[1])


def finish(r, q, picks, first, second):
    shapes = [(r, 4 * D), (2 * q, D), (r, D)]
    arrays = (picks, *first, *second)
    return pl.pallas_call(
        functools.partial(finish_kernel, r, q, len(first)),
        grid=(1,),
        in_specs=[whole(x.shape) for x in arrays],
        out_specs=[whole(x) for x in shapes],
        out_shape=[jax.ShapeDtypeStruct(x, f32) for x in shapes],
        compiler_params=room(12),
        cost_estimate=pl.CostEstimate(flops=0, bytes_accessed=3 << 20, transcendentals=0),
        name="finish",
    )(*arrays)


def load_blocks(me, refs, target, sems, base, row=0, rows=None, col=0):
    rows = rows or refs[0].shape[0]
    width = refs[0].shape[1]
    copies = []
    for m, ref in enumerate(refs):
        at = pl.multiple_of((me ^ m) * rows, 16)
        copy = pltpu.make_async_copy(
            ref.at[pl.ds(row, rows), :], target.at[pl.ds(at, rows), pl.ds(col, width)], sems.at[base + m]
        )
        copy.start()
        copies.append(copy)
    return copies


def norm_parts(v):
    c = v - jnp.mean(v, axis=-1, keepdims=True)
    rstd = lax.rsqrt(jnp.mean(c * c, axis=-1, keepdims=True) + EPS)
    return c * rstd, rstd


def norm_back(grad, gain, h, rstd):
    e = grad * gain
    return (e - jnp.mean(e, -1, keepdims=True) - h * jnp.mean(e * h, -1, keepdims=True)) * rstd


def prepare_kernel(x_ref, cot_ref, ht_ref, ct_ref):
    @pl.loop(0, WIN // BLOCK)
    def _(t):
        rows = pl.ds(pl.multiple_of(t * BLOCK, BLOCK), BLOCK)
        h, _ = norm_parts(x_ref[rows, :].astype(f32))
        ht_ref[:, rows] = h.T
        ct_ref[:, rows] = cot_ref[rows, :].T


def prepare(tokens, cotangent):
    return pl.pallas_call(
        prepare_kernel,
        grid=(1,),
        in_specs=[whole((WIN, D))] * 2,
        out_specs=[whole((D, WIN))] * 2,
        out_shape=[jax.ShapeDtypeStruct((D, WIN), f32), jax.ShapeDtypeStruct((D, WIN), bf16)],
        compiler_params=room(20),
        cost_estimate=pl.CostEstimate(flops=5_000_000_000, bytes_accessed=8 << 20, transcendentals=0),
        name="prepare",
    )(tokens, cotangent)


def project_kernel(nd, me_ref, ht_ref, turn_ref, *rest):
    w = rest[:nd]
    pt_ref, nt_ref, vec_ref, bias_ref, full, sems = rest[nd:]
    for copy in load_blocks(me_ref[0], w, full, sems, 0):
        copy.wait()
    columns = full[:, 3 * D :].astype(f32)
    vec = columns.T
    vec_ref[...] = vec[:16]
    low = vec[:16].astype(bf16)
    for i in range(4):
        c, row = i % 2, 6 + 2 * (i // 2)
        parts = [dot(low[:, c * (D // 2) : (c + 1) * (D // 2)], turn_ref[k], NT) for k in range(2)]
        bias_ref[:, i * D : (i + 1) * D] = parts[0][row : row + 1] + parts[1][row + 1 : row + 2]
    nt_ref[...] = (ht_ref[...] * columns[:, 0:1] + columns[:, 1:2]).astype(bf16)

    for c in range(0, 3 * D, BLOCK):
        cols = slice(c, c + BLOCK)
        pt_ref[cols, :] = dot(full[:, cols].T, nt_ref[...]).astype(bf16)


def project(me, normed_t, turns, w):
    nd = len(w)
    return pl.pallas_call(
        functools.partial(project_kernel, nd),
        in_specs=[SMEM, whole((D, WIN)), whole(turns.shape)] + [ANY] * nd,
        out_specs=[whole((3 * D, WIN)), whole((D, WIN)), whole((16, D)), whole((1, 4 * D))],
        out_shape=[
            jax.ShapeDtypeStruct((3 * D, WIN), bf16),
            jax.ShapeDtypeStruct((D, WIN), bf16),
            jax.ShapeDtypeStruct((16, D), f32),
            jax.ShapeDtypeStruct((1, 4 * D), f32),
        ],
        scratch_shapes=[pltpu.VMEM((D, w[0].shape[1]), bf16), pltpu.SemaphoreType.DMA((nd,))],
        grid=(1,),
        compiler_params=room(26),
        cost_estimate=pl.CostEstimate(flops=2 * WIN * D * 3 * D, bytes_accessed=12 << 20, transcendentals=0),
        name="project",
    )(me, normed_t, turns, *w)


GH = 8
SH = 8
GR = GH * HD


def causal_penalty():
    ik = lax.broadcasted_iota(jnp.int32, (BLOCK, BLOCK), 0)
    iq = lax.broadcasted_iota(jnp.int32, (BLOCK, BLOCK), 1)
    return jnp.where(iq >= ik, 0.0, -BIG)


def split_scaled(q):
    scaled = q.astype(f32) * (HD**-0.5 * LOG2E)
    high = scaled.astype(bf16)
    return high, (scaled - high.astype(f32)).astype(bf16)


def episode_rows(seg):
    hot = lax.broadcasted_iota(jnp.int32, (8, WIN), 0) == seg
    return hot.astype(f32), jnp.where(hot, 0.0, -BIG)


def attend_kernel(q_ref, k_ref, v_ref, seg_ref, out_ref, lse_ref, qa, ka, va, cm):
    @pl.when(pl.program_id(0) == 0)
    def _():
        cm[...] = causal_penalty()

    hot, pen = episode_rows(seg_ref[...])
    pad = jnp.zeros((56, WIN), f32)
    tail_q = jnp.concatenate([hot, pad], axis=0).astype(bf16)
    tail_k = jnp.concatenate([pen, pad], axis=0).astype(bf16)
    ones = jnp.ones((16, WIN), bf16)
    for h in range(GH):
        rows = slice(h * HD, (h + 1) * HD)
        high, low = split_scaled(q_ref[rows, :])
        k = k_ref[rows, :]
        qa[h] = jnp.concatenate([high, low, tail_q], axis=0)
        ka[h] = jnp.concatenate([k, k, tail_k], axis=0).T
        va[h] = jnp.concatenate([v_ref[rows, :], ones], axis=0)
    c = cm[...]
    for qb in range(WIN // BLOCK):
        k0, k1 = max(0, qb - 2) * BLOCK, (qb + 1) * BLOCK
        qs = slice(qb * BLOCK, k1)
        for hb in range(0, GH, SH):
            heads = range(hb, hb + SH)
            s = [dot(ka[h, k0:k1, :], qa[h, :, qs]) for h in heads]
            w = k1 - k0 - BLOCK
            s = [jnp.concatenate([x[:w], x[w:] + c], axis=0) if w else x + c for x in s]
            top = [jnp.max(x, axis=0, keepdims=True) for x in s]
            p = [jnp.exp2(x - y) for x, y in zip(s, top)]
            o = [dot(va[h, :, k0:k1], y.astype(bf16)) for h, y in zip(heads, p)]
            for i, h in enumerate(heads):
                total = o[i][HD : HD + 1]
                out_ref[h * HD : (h + 1) * HD, qs] = (o[i][:HD] * (1.0 / total)).astype(bf16)
                lse_ref[h, :, qs] = top[i] + jnp.log2(total)


GROUPS = HEADS // GH


def head_rows(index):
    return pl.BlockSpec((GR, WIN), lambda i: (index, 0))


def head_sums(index):
    return pl.BlockSpec((GH, 1, WIN), lambda i: (index, 0, 0))


def attend(group, project_t, seg):
    return pl.pallas_call(
        attend_kernel,
        grid=(1,),
        in_specs=[head_rows(group + j * GROUPS) for j in range(3)] + [whole((1, WIN))],
        out_specs=[head_rows(0), head_sums(0)],
        out_shape=[
            jax.ShapeDtypeStruct((GR, WIN), bf16),
            jax.ShapeDtypeStruct((GH, 1, WIN), f32),
        ],
        scratch_shapes=[
            pltpu.VMEM((GH, 128, WIN), bf16),
            pltpu.VMEM((GH, WIN, 128), bf16),
            pltpu.VMEM((GH, HD + 16, WIN), bf16),
            pltpu.VMEM((BLOCK, BLOCK), f32),
        ],
        compiler_params=room(24),
        cost_estimate=pl.CostEstimate(flops=7_000_000_000, bytes_accessed=3 << 20, transcendentals=0),
        name="attend",
    )(project_t, project_t, project_t, seg)


def attend_back_kernel(
    q_ref, k_ref, v_ref, o_ref, do_ref, lse_ref, seg_ref, dq_ref, dk_ref, dv_ref, qa, ka, va, da, aq, cm
):
    hot, pen = episode_rows(seg_ref[...])
    ids = lax.broadcasted_iota(jnp.int32, (8, WIN), 0)
    ones3 = jnp.where(ids < 3, 1.0, 0.0)
    z48 = jnp.zeros((48, WIN), f32)
    z88 = jnp.zeros((88, WIN), f32)

    def rows3(v):
        a = v.astype(bf16).astype(f32)
        b = (v - a).astype(bf16).astype(f32)
        return jnp.where(ids == 0, a, jnp.where(ids == 1, b, jnp.where(ids == 2, v - a - b, 0.0)))

    tail_k = jnp.concatenate([pen, ones3, z48], axis=0).astype(bf16)
    tail_v = jnp.concatenate([ones3, z88], axis=0).astype(bf16)
    for h in range(GH):
        rows = slice(h * HD, (h + 1) * HD)
        high, low = split_scaled(q_ref[rows, :])
        k, v, g = k_ref[rows, :], v_ref[rows, :], do_ref[rows, :]
        delta = jnp.sum(g.astype(f32) * o_ref[rows, :].astype(f32), axis=0, keepdims=True)
        tail_q = jnp.concatenate([hot, rows3(-lse_ref[h]), z48], axis=0).astype(bf16)
        tail_g = jnp.concatenate([rows3(-delta), z88], axis=0).astype(bf16)
        qa[h] = jnp.concatenate([high, low, tail_q], axis=0).T
        ka[h] = jnp.concatenate([k, k, tail_k], axis=0)
        va[h] = jnp.concatenate([v, tail_v], axis=0)
        da[h] = jnp.concatenate([g, tail_g], axis=0).T
    ik = lax.broadcasted_iota(jnp.int32, (BLOCK, BLOCK), 1)
    iq = lax.broadcasted_iota(jnp.int32, (BLOCK, BLOCK), 0)
    cm[...] = jnp.where(iq >= ik, 0.0, -BIG)
    c = cm[...]
    scale = HD**-0.5
    step = 4
    nb = WIN // BLOCK
    for kb in range(nb):
        q0, q1 = kb * BLOCK, min(nb, kb + 3) * BLOCK
        ks = slice(q0, q0 + BLOCK)
        for hb in range(0, GH, step):
            heads = range(hb, hb + step)
            rows = [slice(h * HD, (h + 1) * HD) for h in heads]
            s = [dot(qa[h, q0:q1, :], ka[h, :, ks]) for h in heads]
            dp = [dot(da[h, q0:q1, :], va[h, :, ks]) for h in heads]
            s = [
                jnp.concatenate([x[:BLOCK] + c, x[BLOCK:]], axis=0) if q1 - q0 > BLOCK else x + c
                for x in s
            ]
            p = [jnp.exp2(x) for x in s]
            ds = [(x * y).astype(bf16) for x, y in zip(p, dp)]
            pb = [x.astype(bf16) for x in p]
            dv = [dot(do_ref[x, q0:q1], y) for x, y in zip(rows, pb)]
            dk = [dot(q_ref[x, q0:q1], y) for x, y in zip(rows, ds)]
            dq = [dot(k_ref[x, ks], y, NT) for x, y in zip(rows, ds)]
            for i in range(step):
                dv_ref[rows[i], ks] = dv[i].astype(bf16)
                dk_ref[rows[i], ks] = (dk[i] * scale).astype(bf16)
                done = min(nb, kb + 2) * BLOCK if kb else 0
                if done > q0:
                    aq[rows[i], q0:done] += dq[i][:, : done - q0]
                if q1 > max(done, q0):
                    at = max(done, q0)
                    aq[rows[i], at:q1] = dq[i][:, at - q0 :]
    dq_ref[...] = (aq[...] * scale).astype(bf16)


def attend_back(group, project_t, attended_t, grad_t, lse, seg):
    return pl.pallas_call(
        attend_back_kernel,
        grid=(1,),
        in_specs=[head_rows(group + j * GROUPS) for j in range(3)]
        + [head_rows(0), head_rows(group), head_sums(0), whole((1, WIN))],
        out_specs=[head_rows(0)] * 3,
        out_shape=[jax.ShapeDtypeStruct((GR, WIN), bf16)] * 3,
        scratch_shapes=[
            pltpu.VMEM((GH, WIN, 128), bf16),
            pltpu.VMEM((GH, 128, WIN), bf16),
            pltpu.VMEM((GH, 128, WIN), bf16),
            pltpu.VMEM((GH, WIN, 128), bf16),
            pltpu.VMEM((GR, WIN), f32),
            pltpu.VMEM((BLOCK, BLOCK), f32),
        ],
        compiler_params=room(32),
        cost_estimate=pl.CostEstimate(flops=14_000_000_000, bytes_accessed=5 << 20, transcendentals=0),
        name="attend_back",
    )(project_t, project_t, project_t, attended_t, grad_t, lse, seg)


def gelu_both(u):
    a, b = math.sqrt(2 / math.pi), 0.044715
    sq = u * u
    t = jnp.tanh(u * (a + (a * b) * sq))
    half = 0.5 + 0.5 * t
    slope = half + (0.5 * u) * (1.0 - t * t) * (a + (3 * a * b) * sq)
    return u * half, slope


TB = 512


def token_loop(step):
    @pl.loop(0, WIN // TB)
    def _(t):
        step(pl.ds(pl.multiple_of(t * TB, TB), TB))


def load_weights(me, nd, blocks, exp, red, sems):
    rb, rr = D // nd, red.shape[0] // nd
    copies = load_blocks(me, blocks, exp, sems, nd, 0, rb, 0)
    copies += load_blocks(me, blocks, exp, sems, 2 * nd, rb, rb, D)
    return copies + load_blocks(me, blocks, red, sems, 3 * nd, 2 * rb, rr, 0)


def ffn_chunk(i, me, nd, cot_ref, be_ref, exp, red, n2, n2t, cott, oacc, nacc, ascr, gscr, tmp, gbe_ref, send, keep):
    rb, rr, chunk = D // nd, red.shape[0] // nd, tmp.shape[1]
    cols = pl.ds(pl.multiple_of(i * chunk, 128), chunk)
    gbe_ref[...] = jnp.zeros((1, chunk), f32)

    def step(rows):
        u = dot(n2[rows, :], exp[:, cols]) + be_ref[...]
        ga = dot(cot_ref[rows, :], red[cols, :], NT)
        act, slope = gelu_both(u)
        act = act.astype(bf16)
        gu = (ga * slope).astype(bf16)
        ascr[rows, :] = act
        gscr[rows, :] = gu
        gbe_ref[...] += jnp.sum(gu.astype(f32), axis=0, keepdims=True)
        oacc[rows, :] += dot(act, red[cols, :])
        nacc[rows, :] += dot(gu, exp[:, cols], NT)

    token_loop(step)
    tmp[...] = dot(n2t[...], gscr[...]).astype(bf16)
    emit(me, tmp, send, keep, pl.ds(pl.multiple_of(i * rb, 16), rb))
    tmp[...] = dot(cott[...], ascr[...]).astype(bf16).T
    per = chunk // rr
    for b in range(per):
        mask = me ^ (i * per + b)
        for odd, ref in ((1, send), (0, keep)):
            @pl.when((mask & 1) == odd)
            def _():
                ref[mask >> 1, 2 * rb : 2 * rb + rr, :] = tmp[b * rr : (b + 1) * rr, :]


def ffn_first_kernel(nd, me_ref, x_ref, cot_ref, cott, vec_ref, be_ref, *rest):
    att, blocks, rest = rest[:GROUPS], rest[GROUPS : GROUPS + nd], rest[GROUPS + nd :]
    mid_ref, n2_ref, part_ref, nacc_ref, send, keep, gbe_ref = rest[:7]
    comb, exp, red, mid, n2, n2t, oacc, nacc, ascr, gscr, tmp, sems = rest[7:]
    i = pl.program_id(0)
    me = me_ref[0]
    rb, rr = D // nd, red.shape[0] // nd
    outs = [
        pltpu.make_async_copy(a, b, sems.at[4 * nd + j])
        for j, (a, b) in enumerate(((mid, mid_ref), (n2, n2_ref), (oacc, part_ref), (nacc, nacc_ref)))
    ]

    @pl.when(i == 0)
    def _():
        got = load_blocks(me, blocks, comb, sems, 0, 2 * rb + rr, rb, 0)
        late = load_weights(me, nd, blocks, exp, red, sems)
        for copy in got:
            copy.wait()

        def step(rows):
            m = x_ref[rows, :].astype(f32) + vec_ref[2:3, :]
            for g in range(GROUPS):
                m += dot(att[g][:, rows].T, comb[g * GR : (g + 1) * GR, :])
            mid[rows, :] = m
            oacc[rows, :] = m + vec_ref[5:6, :]
            h, _ = norm_parts(m)
            n = (h * vec_ref[3:4, :] + vec_ref[4:5, :]).astype(bf16)
            n2[rows, :] = n
            n2t[:, rows] = n.T

        token_loop(step)
        nacc[...] = jnp.zeros_like(nacc)
        outs[0].start()
        outs[1].start()
        for copy in late:
            copy.wait()

    ffn_chunk(i, me, nd, cot_ref, be_ref, exp, red, n2, n2t, cott, oacc, nacc, ascr, gscr, tmp, gbe_ref, send, keep)

    @pl.when(i == pl.num_programs(0) - 1)
    def _():
        outs[2].start()
        outs[3].start()
        for copy in outs:
            copy.wait()


def ffn_last_kernel(nd, me_ref, cot_ref, cott, vec_ref, be_ref, *rest):
    att, blocks, rest = rest[:GROUPS], rest[GROUPS : GROUPS + nd], rest[GROUPS + nd :]
    others, rest = rest[:nd], rest[nd:]
    mid_ref, n2_ref, part_ref, naccin_ref = rest[:4]
    out_any, gm_any, dt_any, send_any, keep_any, gbe_ref, gv_ref = rest[4:11]
    comb, exp, red, mid, part, nin, n2, n2t, oacc, nacc, ascr, gscr, tmp, sems = rest[11:25]
    out_ref, gm_ref, dt_ref, send, keep = rest[25:]
    i = pl.program_id(0)
    me = me_ref[0]
    rb, rr = D // nd, red.shape[0] // nd
    ins = [
        pltpu.make_async_copy(a, b, sems.at[4 * nd + j])
        for j, (a, b) in enumerate(((n2_ref, n2), (mid_ref, mid), (part_ref, part), (naccin_ref, nin)))
    ]
    early, last = pl.ds(0, 2 * rb + rr), pl.ds(2 * rb + rr, rb)
    leaving = (
        (send.at[:, early, :], send_any.at[:, early, :]),
        (keep.at[:, early, :], keep_any.at[:, early, :]),
        (out_ref, out_any),
        (gm_ref, gm_any),
        (dt_ref, dt_any),
        (send.at[:, last, :], send_any.at[:, last, :]),
        (keep.at[:, last, :], keep_any.at[:, last, :]),
    )
    outs = [pltpu.make_async_copy(a, b, sems.at[4 * nd + 4 + j]) for j, (a, b) in enumerate(leaving)]

    @pl.when(i == 0)
    def _():
        ins[0].start()
        got = load_weights(me, nd, blocks, exp, red, sems)
        got += load_blocks(me, others, comb, sems, 0, 2 * rb + rr, rb, 0)
        for copy in ins[1:]:
            copy.start()
        oacc[...] = jnp.zeros_like(oacc)
        nacc[...] = jnp.zeros_like(nacc)
        ins[0].wait()
        n2t[...] = n2[...].T
        for copy in got:
            copy.wait()

    ffn_chunk(i, me, nd, cot_ref, be_ref, exp, red, n2, n2t, cott, oacc, nacc, ascr, gscr, tmp, gbe_ref, send, keep)

    @pl.when(i == pl.num_programs(0) - 1)
    def _():
        for copy in outs[:2]:
            copy.start()
        for copy in ins[1:]:
            copy.wait()
        gv_ref[...] = jnp.zeros((8, D), f32)

        def step(rows):
            out_ref[rows, :] = (part[rows, :] + oacc[rows, :]).astype(bf16)
            h, rstd = norm_parts(mid[rows, :])
            g = nacc[rows, :] + nin[rows, :]
            cot = cot_ref[rows, :].astype(f32)
            gm = cot + norm_back(g, vec_ref[3:4, :], h, rstd)
            gm_ref[rows, :] = gm
            low = gm.astype(bf16)
            n2[rows, :] = low
            n2t[:, rows] = low.T
            sums = (low.astype(f32), g * h, g, cot)
            gv_ref[2:6, :] += jnp.concatenate([jnp.sum(v, axis=0, keepdims=True) for v in sums], axis=0)

        token_loop(step)
        outs[2].start()
        outs[3].start()
        dt_ref[...] = dot(comb[...], n2t[...]).astype(bf16)
        outs[4].start()
        for g in range(GROUPS):
            tmp[g * GR : (g + 1) * GR, :] = dot(att[g][...], n2[...]).astype(bf16)
        emit(me, tmp, send, keep, slice(2 * rb + rr, 3 * rb + rr))
        outs[5].start()
        outs[6].start()
        for copy in outs:
            copy.wait()


def ffn_call(kernel, specs, arrays, nd, rows, out_shapes, last):
    ff = 2 * D
    shape = jax.ShapeDtypeStruct
    half = (nd // 2, rows, D)
    wide = pltpu.VMEM((WIN, D), f32)
    low, turned = pltpu.VMEM((WIN, D), bf16), pltpu.VMEM((D, WIN), bf16)
    return pl.pallas_call(
        functools.partial(kernel, nd),
        grid=(ff // D,),
        in_specs=specs,
        out_specs=[ANY for x in out_shapes]
        + [ANY if last else whole(half)] * 2
        + [pl.BlockSpec((1, D), lambda i: (0, i))]
        + ([whole((8, D))] if last else []),
        out_shape=list(out_shapes)
        + [shape(half, bf16), shape(half, bf16), shape((1, ff), f32)]
        + ([shape((8, D), f32)] if last else []),
        scratch_shapes=[pltpu.VMEM((D, D), bf16), pltpu.VMEM((D, ff), bf16), pltpu.VMEM((ff, D), bf16)]
        + [wide] * (3 if last else 1)
        + [low, turned, wide, wide, low, low, pltpu.VMEM((D, D), bf16)]
        + [pltpu.SemaphoreType.DMA((4 * nd + 11,))]
        + ([low, wide, turned, pltpu.VMEM(half, bf16), pltpu.VMEM(half, bf16)] if last else []),
        compiler_params=room(52 if last else 36),
        cost_estimate=pl.CostEstimate(flops=12 * WIN * D * ff, bytes_accessed=20 << 20, transcendentals=0),
        name="ffn_last" if last else "ffn_first",
    )(*arrays)


def ffn_first(me, tokens, attended, cotangent, cotangent_t, vec, bias, blocks, nd):
    shape = jax.ShapeDtypeStruct
    outs = [shape((WIN, D), f32), shape((WIN, D), bf16), shape((WIN, D), f32), shape((WIN, D), f32)]
    specs = [SMEM, whole((WIN, D)), whole((WIN, D)), whole((D, WIN)), whole((16, D))]
    specs += [pl.BlockSpec((1, D), lambda i: (0, i))]
    specs += [whole((GR, WIN))] * GROUPS + [ANY] * nd
    arrays = (me, tokens, cotangent, cotangent_t, vec, bias, *attended, *blocks)
    return ffn_call(ffn_first_kernel, specs, arrays, nd, (4 * D) // nd, outs, False)


def ffn_last(me, attended, cotangent, cotangent_t, vec, bias, blocks, others, state, nd):
    shape = jax.ShapeDtypeStruct
    outs = [shape((WIN, D), bf16), shape((WIN, D), f32), shape((D, WIN), bf16)]
    specs = [SMEM, whole((WIN, D)), whole((D, WIN)), whole((16, D)), pl.BlockSpec((1, D), lambda i: (0, i + 2))]
    specs += [whole((GR, WIN))] * GROUPS + [ANY] * (2 * nd + 4)
    arrays = (me, cotangent, cotangent_t, vec, bias, *attended, *blocks, *others, *state)
    return ffn_call(ffn_last_kernel, specs, arrays, nd, (5 * D) // nd, outs, True)


def emit(me, source, send, keep, rows=slice(None), cols=slice(None)):
    steps = send.shape[0]
    rb = source.shape[0] // (2 * steps)
    for s in range(steps):
        far = pl.multiple_of((me ^ (2 * s + 1)) * rb, 16)
        near = pl.multiple_of((me ^ (2 * s)) * rb, 16)
        send[s, rows, cols] = source[pl.ds(far, rb), :]
        keep[s, rows, cols] = source[pl.ds(near, rb), :]


def weight_grad_kernel(nd, me_ref, nt_ref, vec_ref, gv_ref, b1_ref, b2_ref, turn_ref, *rest):
    grads, rest = rest[: 3 * GROUPS], rest[3 * GROUPS :]
    send, keep, full, tmp, gvt, acc, sems = rest[nd:]
    me = me_ref[0]
    copies = load_blocks(me, rest[:nd], full, sems, 0)
    acc[...] = jnp.zeros_like(acc)
    for i, ref in enumerate(grads):
        g = ref[...].T
        gw = dot(nt_ref[...], g)
        tmp[...] = gw.astype(bf16)
        emit(me, tmp, send, keep, cols=slice(i * GR, (i + 1) * GR))
        if i == 0:
            for copy in copies:
                copy.wait()
        w = full[:, i * GR : (i + 1) * GR].astype(f32)
        total = jnp.sum(g.astype(f32), axis=0, keepdims=True)
        for j, value in enumerate((w * gw, w * total)):
            acc[j] += value[:, :128] + value[:, 128:]
    rows = [gv_ref[:6, :]]
    for ref in (b1_ref, b2_ref):
        low = ref[...].astype(bf16)
        for k in range(2):
            rows.append(
                jnp.concatenate([dot(low[:, c * D : (c + 1) * D], turn_ref[k]) for c in range(2)], axis=1)
            )
    rows += [jnp.zeros((6, D), f32), vec_ref[:2, :], jnp.zeros((VEC - 18, D), f32)]
    base = jnp.concatenate(rows, axis=0).T
    gshift = jnp.sum(acc[1], axis=1, keepdims=True)
    ggain = (jnp.sum(acc[0], axis=1, keepdims=True) - base[:, 17:18] * gshift) / base[:, 16:17]
    lane = lax.broadcasted_iota(jnp.int32, (D, VEC), 1)
    gvt[...] = jnp.where(lane == 0, ggain, jnp.where(lane == 1, gshift, base)).astype(bf16)
    emit(me, gvt, send, keep, cols=slice(3 * D, 3 * D + VEC))


def weight_grad(me, nd, normed_t, vec, gvec, sums, turns, grads, w):
    half = (nd // 2, D // nd, 3 * D + VEC)
    return pl.pallas_call(
        functools.partial(weight_grad_kernel, nd),
        grid=(1,),
        in_specs=[SMEM, whole((D, WIN)), whole((16, D)), whole((8, D))]
        + [whole((1, 2 * D))] * 2
        + [whole(turns.shape)]
        + [whole((GR, WIN))] * (3 * GROUPS)
        + [ANY] * nd,
        out_specs=[whole(half)] * 2,
        out_shape=[jax.ShapeDtypeStruct(half, bf16)] * 2,
        scratch_shapes=[
            pltpu.VMEM((D, 3 * D + VEC), bf16),
            pltpu.VMEM((D, GR), bf16),
            pltpu.VMEM((D, VEC), bf16),
            pltpu.VMEM((2, D, 128), f32),
            pltpu.SemaphoreType.DMA((nd,)),
        ],
        compiler_params=room(30),
        cost_estimate=pl.CostEstimate(flops=2 * WIN * D * 3 * D, bytes_accessed=10 << 20, transcendentals=0),
        name="weight_grad",
    )(me, normed_t, vec, gvec, *sums, turns, *grads, *w)


def project_back_kernel(nd, me_ref, x_ref, gm_ref, vec_ref, *rest):
    grads, rest = rest[: 3 * GROUPS], rest[3 * GROUPS :]
    gt_ref, full, sems = rest[nd:]
    for copy in load_blocks(me_ref[0], rest[:nd], full, sems, 0):
        copy.wait()

    @pl.loop(0, WIN // BLOCK)
    def _(t):
        rows = pl.ds(pl.multiple_of(t * BLOCK, BLOCK), BLOCK)
        total = dot(full[:, :GR], grads[0][:, rows])
        for i in range(1, 3 * GROUPS):
            total += dot(full[:, i * GR : (i + 1) * GR], grads[i][:, rows])
        h, rstd = norm_parts(x_ref[rows, :].astype(f32))
        gt_ref[rows, :] = gm_ref[rows, :] + norm_back(total.T, vec_ref[0:1, :], h, rstd)


def project_back(me, tokens, grad_middle, vec, grads, w):
    nd = len(w)
    return pl.pallas_call(
        functools.partial(project_back_kernel, nd),
        grid=(1,),
        in_specs=[SMEM, whole((WIN, D)), whole((WIN, D)), whole((16, D))]
        + [whole((GR, WIN))] * (3 * GROUPS)
        + [ANY] * nd,
        out_specs=whole((WIN, D)),
        out_shape=jax.ShapeDtypeStruct((WIN, D), f32),
        scratch_shapes=[pltpu.VMEM((D, w[0].shape[1]), bf16), pltpu.SemaphoreType.DMA((nd,))],
        compiler_params=room(58),
        cost_estimate=pl.CostEstimate(flops=2 * WIN * D * 3 * D, bytes_accessed=20 << 20, transcendentals=0),
        name="project_back",
    )(me, tokens, grad_middle, vec, *grads, *w)


def body(nd, nf, tokens, segment_ids, cotangent, projector, combiner, attend_bias, expander,
         expand_bias, reducer, reduce_bias, first_gain, first_shift, second_gain, second_shift):
    r, q = projector.shape[0], reducer.shape[0] // 2
    count = nd * nf
    me = lax.axis_index("dp").astype(jnp.int32).reshape(1)
    picks = half_columns(q)
    turns = half_columns(r)
    vectors = (first_gain, first_shift, attend_bias, second_gain, second_shift, reduce_bias, expand_bias)
    tie = lax.optimization_barrier

    shard_w, shard_1, shard_2 = pack(projector, expander, reducer, combiner, picks, vectors)
    parts_w, parts_1 = shifts(shard_w, nf), shifts(shard_1, nf)
    scaled_t, cotangent_t = prepare(after(tokens, shard_w), cotangent)
    parts_w, scaled_t, cotangent_t = tie((parts_w, scaled_t, cotangent_t))
    (zw,) = line_up(nf, [(0, r, 0, 0, 0)], [(nf * r, 3 * D + VEC)], parts_w)
    w = spread_plane(zw, nd)
    moves = [(0, r, 0, 0, 0), (r, r, 0, nf * r, 0), (2 * r, q, 0, 2 * nf * r, 0)]
    extra = [(2 * r + q, r, 0, nf * (2 * r + q), 0)]
    (z1,) = line_up(nf, moves + extra, [(nf * (3 * r + q), D)], after(parts_1, zw))
    w, z1 = tie((w, z1))
    w = spread_cores(w, nd)
    scaled_t, z1 = tie((scaled_t, z1))
    f1 = spread_plane(z1, nd)
    project_t, normed_t, vecs, bias = project(me, scaled_t, turns, w)
    parts_2 = shifts(after(shard_2, project_t), nf)
    attended, sums = [], []
    for g in range(GROUPS):
        if g == GROUPS - 1:
            f1, parts_2, project_t, _ = tie((f1, parts_2, project_t, attended))
            (z2,) = line_up(nf, moves, [(nf * (2 * r + q), D)], parts_2)
            z2, project_t = tie((z2, project_t))
            f2 = spread_plane(z2, nd)
            f1 = spread_cores(f1, nd)
        a, l = attend(g, project_t, segment_ids)
        attended.append(a)
        sums.append(l)
    *state, s1, k1, gbe1 = ffn_first(me, tokens, attended, cotangent, cotangent_t, vecs, bias, f1, nd)
    s1, k1, f2 = tie((s1, k1, f2))
    got, f2 = tie((flip(s1, 1, nd), f2))
    f2 = spread_cores(f2, nd)
    t1 = [add(k1[m], got[m]) for m in range(nd // 2)]
    t1, cotangent = tie((t1, cotangent))
    m1 = meet_plane(t1, nd)
    out, grad_middle, grad_t, s2, k2, gbe2, gvec = ffn_last(
        me, attended, cotangent, cotangent_t, vecs, bias, f2, f1, state, nd
    )

    cuts = [(0, r, 0), (nf * r, r, r), (2 * nf * r, q, 2 * r)]
    more = [(nf * (2 * r + q), r, 2 * r + q)]
    m1, s2, k2, grad_t = tie((m1, s2, k2, grad_t))
    got = flip(s2, 1, nd)
    p1 = pieces(nf, cuts, m1)
    p1, grad_t = tie((p1, grad_t))
    p1 = [shift(p, k, nf) if k else p for k, p in enumerate(p1)]
    grads = [attend_back(0, project_t, attended[0], grad_t, sums[0], segment_ids)]
    got, k2, grads, grad_t, p1 = tie((got, k2, grads, grad_t, p1))
    t2 = [add(k2[m], got[m]) for m in range(nd // 2)]
    t2, grad_t = tie((t2, grad_t))
    m2 = meet_plane(t2, nd)
    for g in range(1, GROUPS):
        grads.append(attend_back(g, project_t, attended[g], grad_t, sums[g], segment_ids))
    grads = [grads[g][j] for j in range(3) for g in range(GROUPS)]
    send, keep = weight_grad(me, nd, normed_t, vecs, gvec, (gbe1, gbe2), turns, grads, w)
    send, m2 = tie((send, m2))
    p2 = pieces(nf, cuts + more, m2)
    p2 = [shift(p, k, nf) if k else p for k, p in enumerate(p2)]
    totals = sum_cores(send, keep, nd)
    grads, totals = tie((grads, totals))
    met = meet_plane(totals, nd)
    grad_tokens = project_back(me, tokens, grad_middle, vecs, grads, w)
    grad_tokens, met, p2 = tie((grad_tokens, met, p2))
    gw = sum(v.astype(f32) for v in met).astype(bf16)
    grad_expander, grad_reducer, grad_combiner = finish(r, q, picks, p1, p2)
    last = scatter_z(gw, [r], nf)
    grad_projector, small = last[:, : 3 * D], last[:, 3 * D :]
    return (
        out,
        grad_tokens,
        grad_projector,
        grad_combiner,
        small[:, 2],
        grad_expander,
        small[:, 6:10].T.reshape(-1),
        grad_reducer,
        small[:, 5],
        small[:, 0],
        small[:, 1],
        small[:, 3],
        small[:, 4],
    )


def solution(mesh):
    rows, flat = P(("dp", "fsdp"), None), P(("dp", "fsdp"))
    return jax.shard_map(
        functools.partial(body, mesh.shape["dp"], mesh.shape["fsdp"]),
        mesh=mesh,
        in_specs=(rows, rows, rows, rows, rows, flat, rows, flat, rows, flat, flat, flat, flat, flat),
        out_specs=(rows, rows, rows, rows, flat, rows, flat, rows, flat, flat, flat, flat, flat),
        check_vma=False,
    )
```

```python
import functools
import math

import jax
import jax.numpy as jnp
import numpy as np
from jax import lax
from jax.experimental import pallas as pl
from jax.experimental.pallas import tpu as pltpu
from jax.sharding import PartitionSpec as P

D = 768
HD = 32
HEADS = 24
WIN = 1024
BLOCK = 256
EPS = 1e-05
LOG2E = math.log2(math.e)
BIG = float(2**30)
VEC = 128
f32 = jnp.float32
bf16 = jnp.bfloat16
NN = (((1,), (0,)), ((), ()))
NT = (((1,), (1,)), ((), ()))
ANY = pl.BlockSpec(memory_space=pl.ANY)
SMEM = pl.BlockSpec(memory_space=pltpu.SMEM)


def room(mib):
    return pltpu.CompilerParams(vmem_limit_bytes=mib << 20)


def dot(a, b, dims=NN):
    return lax.dot_general(a, b, dims, preferred_element_type=f32)


def whole(shape):
    return pl.BlockSpec(shape, lambda *_: (0,) * len(shape), pipeline_mode=pl.Buffered(1))


def flip(value, bit, count):
    return lax.ppermute(value, "dp", [(i, i ^ bit) for i in range(count)])


def shift(value, step, count):
    return lax.ppermute(value, "fsdp", [(i, (i + step) % count) for i in range(count)])


def after(value, *others):
    return lax.optimization_barrier((value, others))[0]


def shifts(shard, nf):
    return [shard] + [shift(shard, k, nf) for k in range(1, nf)]


def line_up_kernel(nf, moves, me_ref, *refs):
    me = me_ref[0]
    parts, outs = refs[:nf], refs[nf:]
    for k in range(nf):
        for j in range(nf):
            @pl.when(lax.rem(me - k + nf, nf) == j)
            def _():
                for source, rows, out, row, col in moves:
                    value = parts[k][source : source + rows, :]
                    at = row + j * rows
                    outs[out][at : at + rows, col : col + value.shape[1]] = value


def line_up(nf, moves, shapes, parts):
    return pl.pallas_call(
        functools.partial(line_up_kernel, nf, moves),
        in_specs=[SMEM] + [whole(p.shape) for p in parts],
        out_specs=[whole(x) for x in shapes],
        out_shape=[jax.ShapeDtypeStruct(x, bf16) for x in shapes],
        grid=(1,),
        compiler_params=room(10),
        cost_estimate=pl.CostEstimate(flops=0, bytes_accessed=4 << 20, transcendentals=0),
        name="line_up",
    )(lax.axis_index("fsdp").astype(jnp.int32).reshape(1), *parts)


def add(a, b):
    return (a.astype(f32) + b.astype(f32)).astype(bf16)


def spread_plane(block, nd):
    return {m: flip(block, m, nd) if m else block for m in range(0, nd, 2)}


def spread_cores(blocks, nd):
    both = {**blocks, **{m ^ 1: flip(v, 1, nd) for m, v in blocks.items()}}
    return [both[m] for m in range(nd)]


def sum_cores(send, keep, nd):
    got = flip(send, 1, nd)
    return [add(keep[m], got[m]) for m in range(nd // 2)]


def meet_plane(totals, nd):
    return [flip(v, 2 * m, nd) if m else v for m, v in enumerate(totals)]


def scatter_z(block, rows, nf):
    me = lax.axis_index("fsdp")

    def piece(z):
        got, at = [], 0
        for r in rows:
            got.append(lax.dynamic_slice_in_dim(block, at + z * r, r, 0))
            at += nf * r
        return got[0] if len(got) == 1 else jnp.concatenate(got, axis=0)

    total = piece(me).astype(f32)
    for k in range(1, nf):
        total = total + shift(piece(lax.rem(me + k, nf)), k, nf).astype(f32)
    return total


def half_columns(q):
    o = np.arange(D // 2)
    source = (o // q) * (2 * q) + o % q
    picks = np.arange(D)[None, :, None] == (source[None, None, :] + q * np.arange(2)[:, None, None])
    return jnp.asarray(picks, bf16)


def pack_kernel(proj_ref, exp_ref, red_ref, comb_ref, pick_ref, *refs):
    vec_refs, (w_ref, f1_ref, f2_ref) = refs[:-3], refs[-3:]
    r, q = proj_ref.shape[0], red_ref.shape[0] // 2
    w_ref[:, : 3 * D] = proj_ref[...]
    row = [ref[...].astype(f32).reshape(1, -1) for ref in vec_refs]
    rows = row[:6] + [row[6][:, j * r : (j + 1) * r] for j in range(4)]
    rows.append(jnp.zeros((VEC - 10, r), f32))
    w_ref[:, 3 * D :] = jnp.concatenate(rows, axis=0).T.astype(bf16)
    for h, ref in enumerate((f1_ref, f2_ref)):
        for c in range(4):
            at, col = (c // 2) * r, (c % 2) * (D // 2)
            ref[at : at + r, col : col + D // 2] = dot(
                exp_ref[:, c * D : (c + 1) * D], pick_ref[h]
            ).astype(bf16)
        ref[2 * r : 2 * r + q, :] = red_ref[h * q : (h + 1) * q, :]
    f1_ref[2 * r + q :, :] = comb_ref[...]


def pack(projector, expander, reducer, combiner, picks, vectors):
    r, q = projector.shape[0], reducer.shape[0] // 2
    shapes = [(r, 3 * D + VEC), (3 * r + q, D), (2 * r + q, D)]
    arrays = (projector, expander, reducer, combiner, picks, *vectors)
    return pl.pallas_call(
        pack_kernel,
        grid=(1,),
        in_specs=[whole(a.shape) for a in arrays],
        out_specs=[whole(x) for x in shapes],
        out_shape=[jax.ShapeDtypeStruct(x, bf16) for x in shapes],
        compiler_params=room(58),
        cost_estimate=pl.CostEstimate(flops=0, bytes_accessed=3 << 20, transcendentals=0),
        name="pack",
    )(*arrays)


def pieces_kernel(nf, groups, me_ref, *refs):
    terms, outs = refs[:-nf], refs[-nf:]
    me = me_ref[0]
    at = 0
    for first, last, moves in groups:
        for row, rows in moves:
            for j in range(nf):
                here = slice(row + j * rows, row + (j + 1) * rows)
                value = sum(t[here, :].astype(f32) for t in terms[first:last]).astype(bf16)
                for k in range(nf):
                    @pl.when(lax.rem(me + k, nf) == j)
                    def _():
                        outs[k][at : at + rows, :] = value
            at += rows


def pieces(nf, groups):
    terms, spans, rows = [], [], 0
    for moves, arrays in groups:
        spans.append((len(terms), len(terms) + len(arrays), moves))
        terms += arrays
        rows += sum(m[1] for m in moves)
    return pl.pallas_call(
        functools.partial(pieces_kernel, nf, spans),
        in_specs=[SMEM] + [whole(x.shape) for x in terms],
        out_specs=[whole((rows, D))] * nf,
        out_shape=[jax.ShapeDtypeStruct((rows, D), bf16)] * nf,
        grid=(1,),
        compiler_params=room(16),
        cost_estimate=pl.CostEstimate(flops=0, bytes_accessed=10 << 20, transcendentals=0),
        name="pieces",
    )(lax.axis_index("fsdp").astype(jnp.int32).reshape(1), *terms)


def finish_kernel(r, q, pick_ref, *refs):
    parts, (ge_ref, gr_ref, gc_ref) = refs[:-3], refs[-3:]
    for c in range(4):
        total = jnp.zeros((r, D), f32)
        for h in range(2):
            at, col = h * (2 * r + q) + (c // 2) * r, (c % 2) * (D // 2)
            for p in parts:
                total += dot(p[at : at + r, col : col + D // 2], pick_ref[h], NT)
        ge_ref[:, c * D : (c + 1) * D] = total
    for h in range(2):
        at = h * (2 * r + q) + 2 * r
        gr_ref[h * q : (h + 1) * q, :] = sum(p[at : at + q, :].astype(f32) for p in parts)
    gc_ref[...] = sum(p[2 * (2 * r + q) :, :].astype(f32) for p in parts)


def finish(r, q, picks, parts):
    shapes = [(r, 4 * D), (2 * q, D), (r, D)]
    arrays = (picks, *parts)
    return pl.pallas_call(
        functools.partial(finish_kernel, r, q),
        grid=(1,),
        in_specs=[whole(x.shape) for x in arrays],
        out_specs=[whole(x) for x in shapes],
        out_shape=[jax.ShapeDtypeStruct(x, f32) for x in shapes],
        compiler_params=room(12),
        cost_estimate=pl.CostEstimate(flops=0, bytes_accessed=3 << 20, transcendentals=0),
        name="finish",
    )(*arrays)


def load_blocks(me, refs, target, sems, base, row=0, rows=None, col=0):
    rows = rows or refs[0].shape[0]
    width = refs[0].shape[1]
    copies = []
    for m, ref in enumerate(refs):
        at = pl.multiple_of((me ^ m) * rows, 16)
        copy = pltpu.make_async_copy(
            ref.at[pl.ds(row, rows), :], target.at[pl.ds(at, rows), pl.ds(col, width)], sems.at[base + m]
        )
        copy.start()
        copies.append(copy)
    return copies


def norm_parts(v):
    c = v - jnp.mean(v, axis=-1, keepdims=True)
    rstd = lax.rsqrt(jnp.mean(c * c, axis=-1, keepdims=True) + EPS)
    return c * rstd, rstd


def norm_back(grad, gain, h, rstd):
    e = grad * gain
    return (e - jnp.mean(e, -1, keepdims=True) - h * jnp.mean(e * h, -1, keepdims=True)) * rstd


def prepare_kernel(x_ref, cot_ref, ht_ref, ct_ref):
    @pl.loop(0, WIN // BLOCK)
    def _(t):
        rows = pl.ds(pl.multiple_of(t * BLOCK, BLOCK), BLOCK)
        h, _ = norm_parts(x_ref[rows, :].astype(f32))
        ht_ref[:, rows] = h.T
        ct_ref[:, rows] = cot_ref[rows, :].T


def prepare(tokens, cotangent):
    return pl.pallas_call(
        prepare_kernel,
        grid=(1,),
        in_specs=[whole((WIN, D))] * 2,
        out_specs=[whole((D, WIN))] * 2,
        out_shape=[jax.ShapeDtypeStruct((D, WIN), f32), jax.ShapeDtypeStruct((D, WIN), bf16)],
        compiler_params=room(20),
        cost_estimate=pl.CostEstimate(flops=5_000_000_000, bytes_accessed=8 << 20, transcendentals=0),
        name="prepare",
    )(tokens, cotangent)


def project_kernel(nd, me_ref, ht_ref, turn_ref, *rest):
    w = rest[:nd]
    pt_ref, nt_ref, vec_ref, bias_ref, full, sems = rest[nd:]
    for copy in load_blocks(me_ref[0], w, full, sems, 0):
        copy.wait()
    columns = full[:, 3 * D :].astype(f32)
    vec = columns.T
    vec_ref[...] = vec[:16]
    low = vec[:16].astype(bf16)
    for c in range(2):
        parts = [dot(low[:, c * (D // 2) : (c + 1) * (D // 2)], turn_ref[k], NT) for k in range(2)]
        for h in range(2):
            row, at = 6 + 2 * h, (2 * h + c) * D
            bias_ref[:, at : at + D] = parts[0][row : row + 1] + parts[1][row + 1 : row + 2]
    nt_ref[...] = (ht_ref[...] * columns[:, 0:1] + columns[:, 1:2]).astype(bf16)

    for c in range(0, 3 * D, BLOCK):
        cols = slice(c, c + BLOCK)
        pt_ref[cols, :] = dot(full[:, cols].T, nt_ref[...]).astype(bf16)


def project(me, normed_t, turns, w):
    nd = len(w)
    return pl.pallas_call(
        functools.partial(project_kernel, nd),
        in_specs=[SMEM, whole((D, WIN)), whole(turns.shape)] + [ANY] * nd,
        out_specs=[whole((3 * D, WIN)), whole((D, WIN)), whole((16, D)), whole((1, 4 * D))],
        out_shape=[
            jax.ShapeDtypeStruct((3 * D, WIN), bf16),
            jax.ShapeDtypeStruct((D, WIN), bf16),
            jax.ShapeDtypeStruct((16, D), f32),
            jax.ShapeDtypeStruct((1, 4 * D), f32),
        ],
        scratch_shapes=[pltpu.VMEM((D, w[0].shape[1]), bf16), pltpu.SemaphoreType.DMA((nd,))],
        grid=(1,),
        compiler_params=room(26),
        cost_estimate=pl.CostEstimate(flops=2 * WIN * D * 3 * D, bytes_accessed=12 << 20, transcendentals=0),
        name="project",
    )(me, normed_t, turns, *w)


GH = 8
SH = 8
GR = GH * HD


def causal_penalty():
    ik = lax.broadcasted_iota(jnp.int32, (BLOCK, BLOCK), 0)
    iq = lax.broadcasted_iota(jnp.int32, (BLOCK, BLOCK), 1)
    return jnp.where(iq >= ik, 0.0, -BIG)


def split_scaled(q):
    scaled = q.astype(f32) * (HD**-0.5 * LOG2E)
    high = scaled.astype(bf16)
    return high, (scaled - high.astype(f32)).astype(bf16)


def episode_rows(seg):
    hot = lax.broadcasted_iota(jnp.int32, (8, WIN), 0) == seg
    return hot.astype(f32), jnp.where(hot, 0.0, -BIG)


def attend_kernel(q_ref, k_ref, v_ref, seg_ref, out_ref, lse_ref, qa, ka, va, cm):
    @pl.when(pl.program_id(0) == 0)
    def _():
        cm[...] = causal_penalty()

    hot, pen = episode_rows(seg_ref[...])
    pad = jnp.zeros((56, WIN), f32)
    tail_q = jnp.concatenate([hot, pad], axis=0).astype(bf16)
    tail_k = jnp.concatenate([pen, pad], axis=0).astype(bf16)
    ones = jnp.ones((16, WIN), bf16)
    for h in range(GH):
        rows = slice(h * HD, (h + 1) * HD)
        high, low = split_scaled(q_ref[rows, :])
        k = k_ref[rows, :]
        qa[h] = jnp.concatenate([high, low, tail_q], axis=0)
        ka[h] = jnp.concatenate([k, k, tail_k], axis=0).T
        va[h] = jnp.concatenate([v_ref[rows, :], ones], axis=0)
    c = cm[...]
    for qb in range(WIN // BLOCK):
        k0, k1 = max(0, qb - 2) * BLOCK, (qb + 1) * BLOCK
        qs = slice(qb * BLOCK, k1)
        for hb in range(0, GH, SH):
            heads = range(hb, hb + SH)
            s = [dot(ka[h, k0:k1, :], qa[h, :, qs]) for h in heads]
            w = k1 - k0 - BLOCK
            s = [jnp.concatenate([x[:w], x[w:] + c], axis=0) if w else x + c for x in s]
            top = [jnp.max(x, axis=0, keepdims=True) for x in s]
            p = [jnp.exp2(x - y) for x, y in zip(s, top)]
            o = [dot(va[h, :, k0:k1], y.astype(bf16)) for h, y in zip(heads, p)]
            for i, h in enumerate(heads):
                total = o[i][HD : HD + 1]
                out_ref[h * HD : (h + 1) * HD, qs] = (o[i][:HD] * (1.0 / total)).astype(bf16)
                lse_ref[h, :, qs] = top[i] + jnp.log2(total)


GROUPS = HEADS // GH


def head_rows(index):
    return pl.BlockSpec((GR, WIN), lambda i: (index, 0))


def head_sums(index):
    return pl.BlockSpec((GH, 1, WIN), lambda i: (index, 0, 0))


def attend(group, project_t, seg):
    return pl.pallas_call(
        attend_kernel,
        grid=(1,),
        in_specs=[head_rows(group + j * GROUPS) for j in range(3)] + [whole((1, WIN))],
        out_specs=[head_rows(0), head_sums(0)],
        out_shape=[
            jax.ShapeDtypeStruct((GR, WIN), bf16),
            jax.ShapeDtypeStruct((GH, 1, WIN), f32),
        ],
        scratch_shapes=[
            pltpu.VMEM((GH, 128, WIN), bf16),
            pltpu.VMEM((GH, WIN, 128), bf16),
            pltpu.VMEM((GH, HD + 16, WIN), bf16),
            pltpu.VMEM((BLOCK, BLOCK), f32),
        ],
        compiler_params=room(24),
        cost_estimate=pl.CostEstimate(flops=7_000_000_000, bytes_accessed=3 << 20, transcendentals=0),
        name="attend",
    )(project_t, project_t, project_t, seg)


def attend_back_kernel(
    q_ref, k_ref, v_ref, o_ref, do_ref, lse_ref, seg_ref, dq_ref, dk_ref, dv_ref, qa, ka, va, da, aq, cm
):
    hot, pen = episode_rows(seg_ref[...])
    ids = lax.broadcasted_iota(jnp.int32, (8, WIN), 0)
    ones3 = jnp.where(ids < 3, 1.0, 0.0)
    z48 = jnp.zeros((48, WIN), f32)
    z88 = jnp.zeros((88, WIN), f32)

    def rows3(v):
        a = v.astype(bf16).astype(f32)
        b = (v - a).astype(bf16).astype(f32)
        return jnp.where(ids == 0, a, jnp.where(ids == 1, b, jnp.where(ids == 2, v - a - b, 0.0)))

    tail_k = jnp.concatenate([pen, ones3, z48], axis=0).astype(bf16)
    tail_v = jnp.concatenate([ones3, z88], axis=0).astype(bf16)
    for h in range(GH):
        rows = slice(h * HD, (h + 1) * HD)
        high, low = split_scaled(q_ref[rows, :])
        k, v, g = k_ref[rows, :], v_ref[rows, :], do_ref[rows, :]
        delta = jnp.sum(g.astype(f32) * o_ref[rows, :].astype(f32), axis=0, keepdims=True)
        tail_q = jnp.concatenate([hot, rows3(-lse_ref[h]), z48], axis=0).astype(bf16)
        tail_g = jnp.concatenate([rows3(-delta), z88], axis=0).astype(bf16)
        qa[h] = jnp.concatenate([high, low, tail_q], axis=0).T
        ka[h] = jnp.concatenate([k, k, tail_k], axis=0)
        va[h] = jnp.concatenate([v, tail_v], axis=0)
        da[h] = jnp.concatenate([g, tail_g], axis=0).T
    ik = lax.broadcasted_iota(jnp.int32, (BLOCK, BLOCK), 1)
    iq = lax.broadcasted_iota(jnp.int32, (BLOCK, BLOCK), 0)
    cm[...] = jnp.where(iq >= ik, 0.0, -BIG)
    c = cm[...]
    scale = HD**-0.5
    step = 4
    nb = WIN // BLOCK
    for kb in range(nb):
        q0, q1 = kb * BLOCK, min(nb, kb + 3) * BLOCK
        ks = slice(q0, q0 + BLOCK)
        for hb in range(0, GH, step):
            heads = range(hb, hb + step)
            rows = [slice(h * HD, (h + 1) * HD) for h in heads]
            s = [dot(qa[h, q0:q1, :], ka[h, :, ks]) for h in heads]
            dp = [dot(da[h, q0:q1, :], va[h, :, ks]) for h in heads]
            s = [
                jnp.concatenate([x[:BLOCK] + c, x[BLOCK:]], axis=0) if q1 - q0 > BLOCK else x + c
                for x in s
            ]
            p = [jnp.exp2(x) for x in s]
            ds = [(x * y).astype(bf16) for x, y in zip(p, dp)]
            pb = [x.astype(bf16) for x in p]
            dv = [dot(do_ref[x, q0:q1], y) for x, y in zip(rows, pb)]
            dk = [dot(q_ref[x, q0:q1], y) for x, y in zip(rows, ds)]
            dq = [dot(k_ref[x, ks], y, NT) for x, y in zip(rows, ds)]
            for i in range(step):
                dv_ref[rows[i], ks] = dv[i].astype(bf16)
                dk_ref[rows[i], ks] = (dk[i] * scale).astype(bf16)
                done = min(nb, kb + 2) * BLOCK if kb else 0
                if done > q0:
                    aq[rows[i], q0:done] += dq[i][:, : done - q0]
                if q1 > max(done, q0):
                    at = max(done, q0)
                    aq[rows[i], at:q1] = dq[i][:, at - q0 :]
    dq_ref[...] = (aq[...] * scale).astype(bf16)


def attend_back(group, project_t, attended_t, grad_t, lse, seg):
    return pl.pallas_call(
        attend_back_kernel,
        grid=(1,),
        in_specs=[head_rows(group + j * GROUPS) for j in range(3)]
        + [head_rows(0), head_rows(group), head_sums(0), whole((1, WIN))],
        out_specs=[head_rows(0)] * 3,
        out_shape=[jax.ShapeDtypeStruct((GR, WIN), bf16)] * 3,
        scratch_shapes=[
            pltpu.VMEM((GH, WIN, 128), bf16),
            pltpu.VMEM((GH, 128, WIN), bf16),
            pltpu.VMEM((GH, 128, WIN), bf16),
            pltpu.VMEM((GH, WIN, 128), bf16),
            pltpu.VMEM((GR, WIN), f32),
            pltpu.VMEM((BLOCK, BLOCK), f32),
        ],
        compiler_params=room(32),
        cost_estimate=pl.CostEstimate(flops=14_000_000_000, bytes_accessed=5 << 20, transcendentals=0),
        name="attend_back",
    )(project_t, project_t, project_t, attended_t, grad_t, lse, seg)


def gelu_both(u):
    a, b = math.sqrt(2 / math.pi), 0.044715
    sq = u * u
    t = jnp.tanh(u * (a + (a * b) * sq))
    half = 0.5 + 0.5 * t
    slope = half + (0.5 * u) * (1.0 - t * t) * (a + (3 * a * b) * sq)
    return u * half, slope


TB = 512


def token_loop(step):
    @pl.loop(0, WIN // TB)
    def _(t):
        step(pl.ds(pl.multiple_of(t * TB, TB), TB))


def load_weights(me, nd, blocks, exp, red, sems):
    rb, rr = D // nd, red.shape[0] // nd
    copies = load_blocks(me, blocks, exp, sems, nd, 0, rb, 0)
    copies += load_blocks(me, blocks, exp, sems, 2 * nd, rb, rb, D)
    return copies + load_blocks(me, blocks, red, sems, 3 * nd, 2 * rb, rr, 0)


def ffn_chunk(i, me, nd, cot_ref, be_ref, exp, red, n2, n2t, cott, oacc, nacc, ascr, gscr, tmp, gbe_ref, send, keep):
    rb, rr, chunk = D // nd, red.shape[0] // nd, tmp.shape[1]
    cols = pl.ds(pl.multiple_of(i * chunk, 128), chunk)
    gbe_ref[...] = jnp.zeros((1, chunk), f32)

    def step(rows):
        u = dot(n2[rows, :], exp[:, cols]) + be_ref[...]
        ga = dot(cot_ref[rows, :], red[cols, :], NT)
        act, slope = gelu_both(u)
        act = act.astype(bf16)
        gu = (ga * slope).astype(bf16)
        ascr[rows, :] = act
        gscr[rows, :] = gu
        gbe_ref[...] += jnp.sum(gu.astype(f32), axis=0, keepdims=True)
        oacc[rows, :] += dot(act, red[cols, :])
        nacc[rows, :] += dot(gu, exp[:, cols], NT)

    token_loop(step)
    tmp[...] = dot(n2t[...], gscr[...]).astype(bf16)
    emit(me, tmp, send, keep, pl.ds(pl.multiple_of(i * rb, 16), rb))
    tmp[...] = dot(cott[...], ascr[...]).astype(bf16).T
    per = chunk // rr
    for b in range(per):
        mask = me ^ (i * per + b)
        for odd, ref in ((1, send), (0, keep)):
            @pl.when((mask & 1) == odd)
            def _():
                ref[mask >> 1, 2 * rb : 2 * rb + rr, :] = tmp[b * rr : (b + 1) * rr, :]


def ffn_first_kernel(nd, me_ref, x_ref, cot_ref, cott, vec_ref, be_ref, *rest):
    att, blocks, rest = rest[:GROUPS], rest[GROUPS : GROUPS + nd], rest[GROUPS + nd :]
    mid_ref, n2_ref, part_ref, nacc_ref, send, keep, gbe_ref = rest[:7]
    comb, exp, red, mid, n2, n2t, oacc, nacc, ascr, gscr, tmp, sems = rest[7:]
    i = pl.program_id(0)
    me = me_ref[0]
    rb, rr = D // nd, red.shape[0] // nd
    outs = [
        pltpu.make_async_copy(a, b, sems.at[4 * nd + j])
        for j, (a, b) in enumerate(((mid, mid_ref), (n2, n2_ref), (oacc, part_ref), (nacc, nacc_ref)))
    ]

    @pl.when(i == 0)
    def _():
        got = load_blocks(me, blocks, comb, sems, 0, 2 * rb + rr, rb, 0)
        late = load_weights(me, nd, blocks, exp, red, sems)
        for copy in got:
            copy.wait()

        def step(rows):
            m = x_ref[rows, :].astype(f32) + vec_ref[2:3, :]
            for g in range(GROUPS):
                m += dot(att[g][:, rows].T, comb[g * GR : (g + 1) * GR, :])
            mid[rows, :] = m
            oacc[rows, :] = m + vec_ref[5:6, :]
            h, _ = norm_parts(m)
            n = (h * vec_ref[3:4, :] + vec_ref[4:5, :]).astype(bf16)
            n2[rows, :] = n
            n2t[:, rows] = n.T

        token_loop(step)
        nacc[...] = jnp.zeros_like(nacc)
        outs[0].start()
        outs[1].start()
        for copy in late:
            copy.wait()

    ffn_chunk(i, me, nd, cot_ref, be_ref, exp, red, n2, n2t, cott, oacc, nacc, ascr, gscr, tmp, gbe_ref, send, keep)

    @pl.when(i == pl.num_programs(0) - 1)
    def _():
        outs[2].start()
        outs[3].start()
        for copy in outs:
            copy.wait()


def ffn_last_kernel(nd, me_ref, cot_ref, cott, vec_ref, be_ref, *rest):
    att, blocks, rest = rest[:GROUPS], rest[GROUPS : GROUPS + nd], rest[GROUPS + nd :]
    others, rest = rest[:nd], rest[nd:]
    mid_ref, n2_ref, part_ref, naccin_ref = rest[:4]
    out_any, gm_any, dt_any, send_any, keep_any, gbe_ref, gv_ref = rest[4:11]
    comb, exp, red, mid, part, nin, n2, n2t, oacc, nacc, ascr, gscr, tmp, sems = rest[11:25]
    out_ref, gm_ref, dt_ref, send, keep = rest[25:]
    i = pl.program_id(0)
    me = me_ref[0]
    rb, rr = D // nd, red.shape[0] // nd
    ins = [
        pltpu.make_async_copy(a, b, sems.at[4 * nd + j])
        for j, (a, b) in enumerate(((n2_ref, n2), (mid_ref, mid), (part_ref, part), (naccin_ref, nin)))
    ]
    early, last = pl.ds(0, 2 * rb + rr), pl.ds(2 * rb + rr, rb)
    leaving = (
        (send.at[:, early, :], send_any.at[:, early, :]),
        (keep.at[:, early, :], keep_any.at[:, early, :]),
        (out_ref, out_any),
        (gm_ref, gm_any),
        (dt_ref, dt_any),
        (send.at[:, last, :], send_any.at[:, last, :]),
        (keep.at[:, last, :], keep_any.at[:, last, :]),
    )
    outs = [pltpu.make_async_copy(a, b, sems.at[4 * nd + 4 + j]) for j, (a, b) in enumerate(leaving)]

    @pl.when(i == 0)
    def _():
        ins[0].start()
        got = load_weights(me, nd, blocks, exp, red, sems)
        got += load_blocks(me, others, comb, sems, 0, 2 * rb + rr, rb, 0)
        for copy in ins[1:]:
            copy.start()
        oacc[...] = jnp.zeros_like(oacc)
        nacc[...] = jnp.zeros_like(nacc)
        ins[0].wait()
        n2t[...] = n2[...].T
        for copy in got:
            copy.wait()

    ffn_chunk(i, me, nd, cot_ref, be_ref, exp, red, n2, n2t, cott, oacc, nacc, ascr, gscr, tmp, gbe_ref, send, keep)

    @pl.when(i == pl.num_programs(0) - 1)
    def _():
        for copy in outs[:2]:
            copy.start()
        for copy in ins[1:]:
            copy.wait()
        gv_ref[...] = jnp.zeros((8, D), f32)

        def step(rows):
            out_ref[rows, :] = (part[rows, :] + oacc[rows, :]).astype(bf16)
            h, rstd = norm_parts(mid[rows, :])
            g = nacc[rows, :] + nin[rows, :]
            cot = cot_ref[rows, :].astype(f32)
            gm = cot + norm_back(g, vec_ref[3:4, :], h, rstd)
            gm_ref[rows, :] = gm
            low = gm.astype(bf16)
            n2[rows, :] = low
            n2t[:, rows] = low.T
            sums = (low.astype(f32), g * h, g, cot)
            gv_ref[2:6, :] += jnp.concatenate([jnp.sum(v, axis=0, keepdims=True) for v in sums], axis=0)

        token_loop(step)
        outs[2].start()
        outs[3].start()
        dt_ref[...] = dot(comb[...], n2t[...]).astype(bf16)
        outs[4].start()
        for g in range(GROUPS):
            tmp[g * GR : (g + 1) * GR, :] = dot(att[g][...], n2[...]).astype(bf16)
        emit(me, tmp, send, keep, slice(2 * rb + rr, 3 * rb + rr))
        outs[5].start()
        outs[6].start()
        for copy in outs:
            copy.wait()


def ffn_call(kernel, specs, arrays, nd, rows, out_shapes, last):
    ff = 2 * D
    shape = jax.ShapeDtypeStruct
    half = (nd // 2, rows, D)
    wide = pltpu.VMEM((WIN, D), f32)
    low, turned = pltpu.VMEM((WIN, D), bf16), pltpu.VMEM((D, WIN), bf16)
    return pl.pallas_call(
        functools.partial(kernel, nd),
        grid=(ff // D,),
        in_specs=specs,
        out_specs=[ANY for x in out_shapes]
        + [ANY if last else whole(half)] * 2
        + [pl.BlockSpec((1, D), lambda i: (0, i))]
        + ([whole((8, D))] if last else []),
        out_shape=list(out_shapes)
        + [shape(half, bf16), shape(half, bf16), shape((1, ff), f32)]
        + ([shape((8, D), f32)] if last else []),
        scratch_shapes=[pltpu.VMEM((D, D), bf16), pltpu.VMEM((D, ff), bf16), pltpu.VMEM((ff, D), bf16)]
        + [wide] * (3 if last else 1)
        + [low, turned, wide, wide, low, low, pltpu.VMEM((D, D), bf16)]
        + [pltpu.SemaphoreType.DMA((4 * nd + 11,))]
        + ([low, wide, turned, pltpu.VMEM(half, bf16), pltpu.VMEM(half, bf16)] if last else []),
        compiler_params=room(52 if last else 36),
        cost_estimate=pl.CostEstimate(flops=12 * WIN * D * ff, bytes_accessed=20 << 20, transcendentals=0),
        name="ffn_last" if last else "ffn_first",
    )(*arrays)


def ffn_first(me, tokens, attended, cotangent, cotangent_t, vec, bias, blocks, nd):
    shape = jax.ShapeDtypeStruct
    outs = [shape((WIN, D), f32), shape((WIN, D), bf16), shape((WIN, D), f32), shape((WIN, D), f32)]
    specs = [SMEM, whole((WIN, D)), whole((WIN, D)), whole((D, WIN)), whole((16, D))]
    specs += [pl.BlockSpec((1, D), lambda i: (0, i))]
    specs += [whole((GR, WIN))] * GROUPS + [ANY] * nd
    arrays = (me, tokens, cotangent, cotangent_t, vec, bias, *attended, *blocks)
    return ffn_call(ffn_first_kernel, specs, arrays, nd, (4 * D) // nd, outs, False)


def ffn_last(me, attended, cotangent, cotangent_t, vec, bias, blocks, others, state, nd):
    shape = jax.ShapeDtypeStruct
    outs = [shape((WIN, D), bf16), shape((WIN, D), f32), shape((D, WIN), bf16)]
    specs = [SMEM, whole((WIN, D)), whole((D, WIN)), whole((16, D)), pl.BlockSpec((1, D), lambda i: (0, i + 2))]
    specs += [whole((GR, WIN))] * GROUPS + [ANY] * (2 * nd + 4)
    arrays = (me, cotangent, cotangent_t, vec, bias, *attended, *blocks, *others, *state)
    return ffn_call(ffn_last_kernel, specs, arrays, nd, (5 * D) // nd, outs, True)


def emit(me, source, send, keep, rows=slice(None), cols=slice(None)):
    steps = send.shape[0]
    rb = source.shape[0] // (2 * steps)
    for s in range(steps):
        far = pl.multiple_of((me ^ (2 * s + 1)) * rb, 16)
        near = pl.multiple_of((me ^ (2 * s)) * rb, 16)
        send[s, rows, cols] = source[pl.ds(far, rb), :]
        keep[s, rows, cols] = source[pl.ds(near, rb), :]


def weight_grad_kernel(nd, me_ref, nt_ref, vec_ref, gv_ref, b1_ref, b2_ref, turn_ref, *rest):
    grads, rest = rest[: 3 * GROUPS], rest[3 * GROUPS :]
    send, keep, full, tmp, gvt, acc, sems = rest[nd:]
    me = me_ref[0]
    copies = load_blocks(me, rest[:nd], full, sems, 0)
    acc[...] = jnp.zeros_like(acc)
    for i, ref in enumerate(grads):
        g = ref[...].T
        gw = dot(nt_ref[...], g)
        tmp[...] = gw.astype(bf16)
        emit(me, tmp, send, keep, cols=slice(i * GR, (i + 1) * GR))
        if i == 0:
            for copy in copies:
                copy.wait()
        w = full[:, i * GR : (i + 1) * GR].astype(f32)
        total = jnp.sum(g.astype(f32), axis=0, keepdims=True)
        for j, value in enumerate((w * gw, w * total)):
            acc[j] += value[:, :128] + value[:, 128:]
    rows = [gv_ref[:6, :]]
    for ref in (b1_ref, b2_ref):
        low = ref[...].astype(bf16)
        for k in range(2):
            rows.append(
                jnp.concatenate([dot(low[:, c * D : (c + 1) * D], turn_ref[k]) for c in range(2)], axis=1)
            )
    rows += [jnp.zeros((6, D), f32), vec_ref[:2, :], jnp.zeros((VEC - 18, D), f32)]
    base = jnp.concatenate(rows, axis=0).T
    gshift = jnp.sum(acc[1], axis=1, keepdims=True)
    ggain = (jnp.sum(acc[0], axis=1, keepdims=True) - base[:, 17:18] * gshift) / base[:, 16:17]
    lane = lax.broadcasted_iota(jnp.int32, (D, VEC), 1)
    gvt[...] = jnp.where(lane == 0, ggain, jnp.where(lane == 1, gshift, base)).astype(bf16)
    emit(me, gvt, send, keep, cols=slice(3 * D, 3 * D + VEC))


def weight_grad(me, nd, normed_t, vec, gvec, sums, turns, grads, w):
    half = (nd // 2, D // nd, 3 * D + VEC)
    return pl.pallas_call(
        functools.partial(weight_grad_kernel, nd),
        grid=(1,),
        in_specs=[SMEM, whole((D, WIN)), whole((16, D)), whole((8, D))]
        + [whole((1, 2 * D))] * 2
        + [whole(turns.shape)]
        + [whole((GR, WIN))] * (3 * GROUPS)
        + [ANY] * nd,
        out_specs=[whole(half)] * 2,
        out_shape=[jax.ShapeDtypeStruct(half, bf16)] * 2,
        scratch_shapes=[
            pltpu.VMEM((D, 3 * D + VEC), bf16),
            pltpu.VMEM((D, GR), bf16),
            pltpu.VMEM((D, VEC), bf16),
            pltpu.VMEM((2, D, 128), f32),
            pltpu.SemaphoreType.DMA((nd,)),
        ],
        compiler_params=room(30),
        cost_estimate=pl.CostEstimate(flops=2 * WIN * D * 3 * D, bytes_accessed=10 << 20, transcendentals=0),
        name="weight_grad",
    )(me, normed_t, vec, gvec, *sums, turns, *grads, *w)


def project_back_kernel(nd, me_ref, x_ref, gm_ref, vec_ref, *rest):
    grads, rest = rest[: 3 * GROUPS], rest[3 * GROUPS :]
    gt_ref, full, sems = rest[nd:]
    for copy in load_blocks(me_ref[0], rest[:nd], full, sems, 0):
        copy.wait()

    @pl.loop(0, WIN // BLOCK)
    def _(t):
        rows = pl.ds(pl.multiple_of(t * BLOCK, BLOCK), BLOCK)
        total = dot(full[:, :GR], grads[0][:, rows])
        for i in range(1, 3 * GROUPS):
            total += dot(full[:, i * GR : (i + 1) * GR], grads[i][:, rows])
        h, rstd = norm_parts(x_ref[rows, :].astype(f32))
        gt_ref[rows, :] = gm_ref[rows, :] + norm_back(total.T, vec_ref[0:1, :], h, rstd)


def project_back(me, tokens, grad_middle, vec, grads, w):
    nd = len(w)
    return pl.pallas_call(
        functools.partial(project_back_kernel, nd),
        grid=(1,),
        in_specs=[SMEM, whole((WIN, D)), whole((WIN, D)), whole((16, D))]
        + [whole((GR, WIN))] * (3 * GROUPS)
        + [ANY] * nd,
        out_specs=whole((WIN, D)),
        out_shape=jax.ShapeDtypeStruct((WIN, D), f32),
        scratch_shapes=[pltpu.VMEM((D, w[0].shape[1]), bf16), pltpu.SemaphoreType.DMA((nd,))],
        compiler_params=room(58),
        cost_estimate=pl.CostEstimate(flops=2 * WIN * D * 3 * D, bytes_accessed=20 << 20, transcendentals=0),
        name="project_back",
    )(me, tokens, grad_middle, vec, *grads, *w)


def body(nd, nf, tokens, segment_ids, cotangent, projector, combiner, attend_bias, expander,
         expand_bias, reducer, reduce_bias, first_gain, first_shift, second_gain, second_shift):
    r, q = projector.shape[0], reducer.shape[0] // 2
    count = nd * nf
    me = lax.axis_index("dp").astype(jnp.int32).reshape(1)
    picks = half_columns(q)
    turns = half_columns(r)
    vectors = (first_gain, first_shift, attend_bias, second_gain, second_shift, reduce_bias, expand_bias)
    tie = lax.optimization_barrier

    shard_w, shard_1, shard_2 = pack(projector, expander, reducer, combiner, picks, vectors)
    parts_w, parts_1 = shifts(shard_w, nf), shifts(shard_1, nf)
    scaled_t, cotangent_t = prepare(after(tokens, shard_w), cotangent)
    parts_w, scaled_t, cotangent_t = tie((parts_w, scaled_t, cotangent_t))
    (zw,) = line_up(nf, [(0, r, 0, 0, 0)], [(nf * r, 3 * D + VEC)], parts_w)
    w = spread_plane(zw, nd)
    moves = [(0, r, 0, 0, 0), (r, r, 0, nf * r, 0), (2 * r, q, 0, 2 * nf * r, 0)]
    extra = [(2 * r + q, r, 0, nf * (2 * r + q), 0)]
    (z1,) = line_up(nf, moves + extra, [(nf * (3 * r + q), D)], after(parts_1, zw))
    w, z1 = tie((w, z1))
    w = spread_cores(w, nd)
    scaled_t, z1 = tie((scaled_t, z1))
    f1 = spread_plane(z1, nd)
    project_t, normed_t, vecs, bias = project(me, scaled_t, turns, w)
    parts_2 = shifts(after(shard_2, project_t), nf)
    attended, sums = [], []
    for g in range(GROUPS):
        if g == GROUPS - 1:
            f1, parts_2, project_t, _ = tie((f1, parts_2, project_t, attended))
            (z2,) = line_up(nf, moves, [(nf * (2 * r + q), D)], parts_2)
            z2, project_t = tie((z2, project_t))
            f2 = spread_plane(z2, nd)
            f1 = spread_cores(f1, nd)
        a, l = attend(g, project_t, segment_ids)
        attended.append(a)
        sums.append(l)
    *state, s1, k1, gbe1 = ffn_first(me, tokens, attended, cotangent, cotangent_t, vecs, bias, f1, nd)
    s1, k1, f2 = tie((s1, k1, f2))
    got, f2 = tie((flip(s1, 1, nd), f2))
    f2 = spread_cores(f2, nd)
    t1 = [add(k1[m], got[m]) for m in range(nd // 2)]
    t1, cotangent = tie((t1, cotangent))
    m1 = meet_plane(t1, nd)
    out, grad_middle, grad_t, s2, k2, gbe2, gvec = ffn_last(
        me, attended, cotangent, cotangent_t, vecs, bias, f2, f1, state, nd
    )

    cuts = [(0, r), (nf * r, r), (2 * nf * r, q)]
    more = [(nf * (2 * r + q), r)]
    m1, s2, k2, grad_t = tie((m1, s2, k2, grad_t))
    got = flip(s2, 1, nd)
    grads = [attend_back(0, project_t, attended[0], grad_t, sums[0], segment_ids)]
    got, k2, grads, grad_t = tie((got, k2, grads, grad_t))
    t2 = [add(k2[m], got[m]) for m in range(nd // 2)]
    t2, grad_t = tie((t2, grad_t))
    m2 = meet_plane(t2, nd)
    for g in range(1, GROUPS):
        grads.append(attend_back(g, project_t, attended[g], grad_t, sums[g], segment_ids))
    grads = [grads[g][j] for j in range(3) for g in range(GROUPS)]
    send, keep = weight_grad(me, nd, normed_t, vecs, gvec, (gbe1, gbe2), turns, grads, w)
    send, m2 = tie((send, m2))
    p2 = pieces(nf, [(cuts, m1), (cuts + more, m2)])
    p2 = [shift(p, k, nf) if k else p for k, p in enumerate(p2)]
    totals = sum_cores(send, keep, nd)
    grads, totals = tie((grads, totals))
    met = meet_plane(totals, nd)
    grad_tokens = project_back(me, tokens, grad_middle, vecs, grads, w)
    grad_tokens, met, p2 = tie((grad_tokens, met, p2))
    gw = sum(v.astype(f32) for v in met).astype(bf16)
    grad_expander, grad_reducer, grad_combiner = finish(r, q, picks, p2)
    last = scatter_z(gw, [r], nf)
    grad_projector, small = last[:, : 3 * D], last[:, 3 * D :]
    return (
        out,
        grad_tokens,
        grad_projector,
        grad_combiner,
        small[:, 2],
        grad_expander,
        small[:, 6:10].T.reshape(-1),
        grad_reducer,
        small[:, 5],
        small[:, 0],
        small[:, 1],
        small[:, 3],
        small[:, 4],
    )


def solution(mesh):
    rows, flat = P(("dp", "fsdp"), None), P(("dp", "fsdp"))
    return jax.shard_map(
        functools.partial(body, mesh.shape["dp"], mesh.shape["fsdp"]),
        mesh=mesh,
        in_specs=(rows, rows, rows, rows, rows, flat, rows, flat, rows, flat, flat, flat, flat, flat),
        out_specs=(rows, rows, rows, rows, flat, rows, flat, rows, flat, flat, flat, flat, flat),
        check_vma=False,
    )
```
